256 devices in a mesh: gossip: 8 (over x_hi, y), shard: 32 (over x_lo, z, core).
Axes of the slice: x: 4 (x_hi: 2, x_lo: 2; x = x_hi * 2 + x_lo), y: 4, z: 8, core: 2. Of those that a mesh axis runs over, the one named last changes fastest.
Arguments:
- activ: bfloat16 [8, 16384, 2048], P('gossip', 'shard'), may hold values from -48 to 48
- grad_out: bfloat16 [8, 16384, 2048], P('gossip', 'shard'), may hold values from -6 to 6
- weight: bfloat16 [8, 2048, 2048], P('gossip', 'shard'), may hold values from -0.125 to 0.125
- q_seed: int32 [8, 2048, 2], replicated, may hold values from -4 to 4
Outputs:
- grad_in: bfloat16 [8, 16384, 2048], P('gossip', 'shard')
- new_weight: float32 [8, 2048, 2048], P('gossip', 'shard')
- next_q: float32 [8, 2048, 2], P('gossip')
The draws below stay inside these ranges and needn't reach their ends.
All inputs are finite; a program needn't handle non-finite values.
Results may differ from the reference program's by a relative error of at most 0.00045.
Values may be sent and summed in bfloat16 or wider, within the bound.
No kernel may reach another device: no remote copies, remote signals or barrier semaphores. Data moves between devices by JAX's collectives and lax.ppermute only.
A program may use at most 128 MiB of HBM per device.

```python
import jax
import jax.numpy as jnp
from jax import lax

D = 2048
TOK_DEV = 512
RANK = 2
REP = 8
TOKENS = 16384


def draw_activ(key, part):
    key = jax.random.fold_in(key, 11)
    key_values, key_pairs = jax.random.split(key, 2)
    blocks = TOKENS // TOK_DEV
    values = jax.random.truncated_normal(key_values, -4.0, 4.0, (REP, TOKENS, D), jnp.float32)
    lowest = 0.3
    spread = 10.0
    columns = jnp.arange(D, dtype=jnp.float32) / (D - 1)
    scales = lowest * jnp.power(spread, columns)
    pairing = jax.random.permutation(key_pairs, blocks)
    token_block = jnp.arange(TOKENS) // TOK_DEV
    column_block = jnp.arange(D) // (D // blocks)
    matched = pairing[token_block][:, None] == column_block[None, :]
    boost = jnp.where(matched, 4.0, 1.0)
    return (values * scales[None, None, :] * boost[None, :, :]).astype(jnp.bfloat16)


def plant(entries, own_key, low, largest):
    index_at = [jax.random.randint(jax.random.fold_in(own_key, axis), (), 0, length) for axis, length in enumerate(entries.shape)]
    widest = entries.shape.index(max(entries.shape))
    neighbour = index_at[:widest] + [(index_at[widest] + 1) % entries.shape[widest]] + index_at[widest + 1:]
    return entries.at[tuple(index_at)].set(low).at[tuple(neighbour)].set(largest)


def block_levels(key, dims, shards, smallest, high):
    gain, own = 1.0, jax.random.fold_in(key, 6)
    for position, blocks in shards:
        draws = jnp.exp(jax.random.uniform(jax.random.fold_in(own, position), (blocks,), jnp.float32, smallest / len(shards), high / len(shards)))
        gain = gain * jnp.repeat(draws, dims[position] // blocks).reshape([-1 if axis == position else 1 for axis in range(len(dims))])
    return gain


def centred(rng, dims, scale, reach, shards=(), kind=jnp.bfloat16):
    factor_of = block_levels(rng, dims, shards, -0.22, 0.18) if shards else 1.0
    result = jax.random.normal(rng, dims, jnp.float32) * scale * factor_of
    return jnp.minimum(jnp.maximum(result, -reach), reach).astype(kind)


def setup_inputs(seed: int = 0) -> dict:
    keys = jax.random.split(jax.random.key(seed), 5)
    activ = draw_activ(jax.random.fold_in(keys[4], 71), 0)
    grad_out = centred(keys[1], (REP, TOKENS, D), 1.0, 6.0, ((0, 8), (1, 32)))
    weight = centred(keys[2], (REP, D, D), D ** -0.5, 0.125, ((0, 8), (1, 32)))
    q_seed = plant(jax.random.randint(keys[3], (REP, D, RANK), -4, 5), jax.random.fold_in(keys[3], 1), -4, 4).astype(jnp.int32)
    return dict(activ=activ, grad_out=grad_out, weight=weight, q_seed=q_seed)


LEARN = 0.002
GOSSIP = 0.5
EPS = 1e-06

def orthonormal(proj):
    first = proj[..., 0]
    second = proj[..., 1]
    unit_first = first / jnp.sqrt(lax.optimization_barrier(jnp.sum(first * first, -1, keepdims=True)) + EPS)
    correlation = lax.optimization_barrier(jnp.sum(unit_first * second, -1, keepdims=True))
    remain = second - correlation * unit_first
    unit_second = remain / jnp.sqrt(lax.optimization_barrier(jnp.sum(remain * remain, -1, keepdims=True)) + EPS)
    return jnp.stack([unit_first, unit_second], -1)

def replica_pass(operands):
    acts, cotan, weight_bf = operands
    grad_in = jnp.dot(cotan, weight_bf.T, preferred_element_type=jnp.float32).astype(jnp.bfloat16)
    grads = jnp.dot(acts.T, cotan, preferred_element_type=jnp.float32)
    return (grad_in, grads)

def reference(activ, grad_out, weight, q_seed):
    grad_in, grads = lax.map(replica_pass, (activ, grad_out, weight))
    stepped = weight.astype(jnp.float32) - LEARN * grads
    seeds = q_seed.astype(jnp.float32)
    diff = stepped - jnp.roll(stepped, -1, axis=0)
    proj = jnp.einsum('eij,ejk->eik', diff, seeds, precision=lax.Precision.HIGHEST)
    basis = orthonormal(proj)
    next_q = jnp.einsum('eij,eik->ejk', diff, basis, precision=lax.Precision.HIGHEST)
    moves = jnp.einsum('eik,ejk->eij', basis, next_q, precision=lax.Precision.HIGHEST)
    new_weight = stepped - GOSSIP * moves + GOSSIP * jnp.roll(moves, 1, axis=0)
    return (grad_in, new_weight, next_q)
```

```python
import jax
import jax.numpy as jnp
from jax import lax
from jax.sharding import Mesh
from jax.sharding import PartitionSpec as P

LEARN = 0.002
GOSSIP = 0.5
EPS = 1e-06

CYCLE = ("xh", "y")
SHARD = ("xl", "z", "core")
NT = (((1,), (1,)), ((), ()))
NN = (((1,), (0,)), ((), ()))
TN = (((0,), (0,)), ((), ()))


def dot(left, right, dims):
    return lax.dot_general(left, right, dims, preferred_element_type=jnp.float32)


def thin(left, right, dims):
    count = left.shape[0]
    high = lax.reduce_precision(left, 8, 7)
    rest = left - high
    middle = lax.reduce_precision(rest, 8, 7)
    low = lax.reduce_precision(rest - middle, 8, 7)
    terms = jnp.concatenate([high, middle, low], 0).astype(jnp.bfloat16)
    out = dot(terms, right, dims)
    return out[:count] + (out[count : 2 * count] + out[2 * count :])


def partner(value, axis, step):
    count = lax.axis_size(axis)
    return lax.ppermute(value, axis, [(i, i ^ step) for i in range(count)])


def shard_sum(value):
    for axis, step in (("core", 1), ("xl", 1), ("z", 1), ("z", 2), ("z", 4)):
        value = value + partner(value, axis, step)
    return value


def passed_along(value, steps):
    count = lax.axis_size(CYCLE)
    return lax.ppermute(value, CYCLE, [(i, (i + steps) % count) for i in range(count)])


def edges(value):
    from_right = passed_along(value[2:], -1)
    from_left = passed_along(value[:2], 1)
    return value[:2] - from_right, from_left - value[2:]


def orthonormal(proj):
    first, second = proj[0], proj[1]
    unit_first = first * lax.rsqrt(jnp.sum(first * first) + EPS)
    remain = second - jnp.sum(unit_first * second) * unit_first
    unit_second = remain * lax.rsqrt(jnp.sum(remain * remain) + EPS)
    return [unit_first, unit_second]


def on_device(activ, grad_out, weight, q_seed):
    acts = activ[0]
    cotan = grad_out[0]
    weight_bf = weight[0]
    rows, width = weight_bf.shape
    own = lax.axis_index(SHARD)
    replica = lax.axis_index(CYCLE)
    cycle_size = lax.axis_size(CYCLE)

    grads = lax.psum_scatter(dot(acts, cotan, TN), SHARD, scatter_dimension=0, tiled=True)
    weights = lax.all_gather(weight_bf, SHARD, axis=0, tiled=True)
    grad_in = dot(cotan, weights, NT).astype(jnp.bfloat16)

    q_right = lax.dynamic_index_in_dim(q_seed, replica, 0, keepdims=False)
    q_left = lax.dynamic_index_in_dim(
        q_seed, (replica + cycle_size - 1) % cycle_size, 0, keepdims=False
    )
    probes = jnp.concatenate([q_right.T, q_left.T], 0).astype(jnp.bfloat16)
    from_grads = thin(dot(probes, cotan, NT), acts, NN)
    from_weight = dot(probes, weight_bf, NT)
    at_own = lax.broadcasted_iota(jnp.int32, (1, width), 1) // rows == own
    from_weight = jnp.where(at_own, jnp.tile(from_weight, (1, width // rows)), 0.0)
    proj_right, proj_left = edges(shard_sum(from_weight - LEARN * from_grads))

    basis = jnp.stack(orthonormal(proj_right) + orthonormal(proj_left), 0)
    basis_own = lax.dynamic_slice_in_dim(basis, own * rows, rows, 1)
    back = thin(basis_own, weight_bf, NN) - LEARN * thin(thin(basis, acts, NT), cotan, NN)
    next_right, next_left = edges(shard_sum(back))

    basis_rows = basis_own.T
    moves = (
        basis_rows[:, 0:1] * next_right[0:1]
        + basis_rows[:, 1:2] * next_right[1:2]
        - basis_rows[:, 2:3] * next_left[0:1]
        - basis_rows[:, 3:4] * next_left[1:2]
    )
    new_weight = weight_bf.astype(jnp.float32) - LEARN * grads - GOSSIP * moves
    return (grad_in[None], new_weight[None], next_right.T[None])


def solution(mesh):
    fine = Mesh(mesh.devices.reshape(2, 4, 2, 8, 2), CYCLE + SHARD)
    tokens = P(CYCLE, SHARD, None)
    return jax.shard_map(
        on_device,
        mesh=fine,
        in_specs=(tokens, tokens, tokens, P()),
        out_specs=(tokens, tokens, P(CYCLE, None, None)),
        check_vma=False,
    )
```

```python
import functools

import jax
import jax.numpy as jnp
from jax import lax
from jax.experimental import pallas as pl
from jax.experimental.pallas import tpu as pltpu
from jax.sharding import Mesh
from jax.sharding import PartitionSpec as P

LEARN = 0.002
GOSSIP = 0.5
EPS = 1e-06
LANES = 128
LEVELS = 64.0
STEPS = 32767.0
VMEM = 32 * 2**20

CYCLE = ("xh", "y")
SHARD = ("xl", "z", "core")
NT = (((1,), (1,)), ((), ()))
NN = (((1,), (0,)), ((), ()))
TN = (((0,), (0,)), ((), ()))


def dot(left, right, dims):
    return lax.dot_general(left, right, dims, preferred_element_type=jnp.float32)


def thin(left, right, dims):
    count = left.shape[0]
    high = lax.reduce_precision(left, 8, 7)
    rest = left - high
    middle = lax.reduce_precision(rest, 8, 7)
    low = lax.reduce_precision(rest - middle, 8, 7)
    terms = jnp.concatenate([high, middle, low], 0).astype(jnp.bfloat16)
    out = dot(terms, right, dims)
    return out[:count] + (out[count : 2 * count] + out[2 * count :])


def partner(value, axis, step):
    count = lax.axis_size(axis)
    return lax.ppermute(value, axis, [(i, i ^ step) for i in range(count)])


def shard_sum(value):
    for axis, step in (("core", 1), ("xl", 1), ("z", 1), ("z", 2), ("z", 4)):
        value = value + partner(value, axis, step)
    return value


def passed_along(value, steps):
    count = lax.axis_size(CYCLE)
    return lax.ppermute(value, CYCLE, [(i, (i + steps) % count) for i in range(count)])


def edges(value):
    from_right = passed_along(value[2:], -1)
    from_left = passed_along(value[:2], 1)
    return value[:2] - from_right, from_left - value[2:]


def coded(value):
    largest = jnp.maximum(jnp.max(jnp.abs(value), 1, keepdims=True), 1e-30)
    level = jnp.ceil(jnp.log2(largest) * LEVELS + 0.01)
    steps = jnp.floor(value * (STEPS * jnp.exp2(level * (-1.0 / LEVELS))) + 0.5)
    steps = jnp.clip(steps, -STEPS, STEPS).astype(jnp.int32)
    level = jnp.broadcast_to(level, (value.shape[0], LANES)).astype(jnp.int32)
    return jnp.concatenate([steps, level], 1).astype(jnp.int16)


def decoded(code):
    code = code.astype(jnp.int32).astype(jnp.float32)
    size = jnp.exp2(code[:, -1:] * (1.0 / LEVELS)) * (1.0 / STEPS)
    return code[:, :-LANES] * size


def product(acts, other_acts, cotan, other_cotan):
    return dot(acts[...], cotan[...], TN) + dot(other_acts[...], other_cotan[...], TN)


def product_kernel(place, acts, other_acts, cotan, other_cotan, out):
    out[0] = product(acts, other_acts, cotan, other_cotan)


def coded_product_kernel(place, acts, other_acts, cotan, other_cotan, out):
    out[0] = coded(product(acts, other_acts, cotan, other_cotan))


def gradient_chunks(kernel, place, column, acts, other_acts, cotan, other_cotan, out_width, dtype):
    tokens, width = acts.shape
    rows, columns = width // 16, width // 2
    count = place.shape[0]
    return pl.pallas_call(
        kernel,
        grid_spec=pltpu.PrefetchScalarGridSpec(
            num_scalar_prefetch=1,
            grid=(count,),
            in_specs=[
                pl.BlockSpec((tokens, rows), lambda i, at: (0, at[i])),
                pl.BlockSpec((tokens, rows), lambda i, at: (0, at[i])),
                pl.BlockSpec((tokens, columns), lambda i, at: (0, at[count])),
                pl.BlockSpec((tokens, columns), lambda i, at: (0, 0)),
            ],
            out_specs=pl.BlockSpec((1, rows, out_width), lambda i, at: (i, 0, 0)),
        ),
        out_shape=jax.ShapeDtypeStruct((count, rows, out_width), dtype),
        cost_estimate=pl.CostEstimate(
            flops=4 * tokens * rows * columns * count,
            bytes_accessed=4 * tokens * (columns + rows * count),
            transcendentals=0,
        ),
        compiler_params=pltpu.CompilerParams(vmem_limit_bytes=VMEM),
    )(jnp.concatenate([place, column[None]]), acts, other_acts, cotan, other_cotan)


def hop_kernel(step, *refs):
    mine, from_x = refs[:2]
    down = mine[0] + decoded(from_x[0])
    up = mine[1] + decoded(from_x[1])
    if step > 0:
        down = down + decoded(refs[2][...])
        up = up + decoded(refs[3][...])
    refs[-2][...] = coded(down)
    refs[-1][...] = up if step == 3 else coded(up)


def hop(step, mine, from_x, received):
    _, rows, columns = mine.shape
    wide = columns + LANES
    whole = pl.BlockSpec((rows, wide), lambda i: (0, 0))
    sent = jax.ShapeDtypeStruct((rows, wide), jnp.int16)
    last = jax.ShapeDtypeStruct((rows, columns), jnp.float32) if step == 3 else sent
    return pl.pallas_call(
        functools.partial(hop_kernel, step),
        grid=(1,),
        in_specs=[
            pl.BlockSpec((2, rows, columns), lambda i: (step, 0, 0)),
            pl.BlockSpec((2, rows, wide), lambda i: (0, 0, 0)),
        ]
        + [whole] * len(received),
        out_specs=[whole, pl.BlockSpec(last.shape, lambda i: (0, 0))],
        out_shape=[sent, last],
        cost_estimate=pl.CostEstimate(
            flops=20 * rows * columns, bytes_accessed=16 * rows * columns, transcendentals=0
        ),
        compiler_params=pltpu.CompilerParams(vmem_limit_bytes=VMEM),
    )(mine, from_x, *received)


def shifted(value, axis, steps):
    count = lax.axis_size(axis)
    return lax.ppermute(value, axis, [(i, (i + steps) % count) for i in range(count)])


def gradient_rows(acts, cotan):
    width = acts.shape[1]
    columns, rows = width // 2, width // 32
    core, x, z = lax.axis_index("core"), lax.axis_index("xl"), lax.axis_index("z")
    other_acts = partner(acts, "core", 1)
    other_cotan = partner(
        lax.dynamic_slice_in_dim(cotan, (1 - core) * columns, columns, 1), "core", 1
    )
    order = [offset for step in range(4) for offset in (4 + step, 3 - step)]
    place = jnp.stack([(z + offset) % 8 for offset in order])
    operands = (acts, other_acts, cotan, other_cotan)
    from_x = []
    for step in range(4):
        piece = gradient_chunks(
            coded_product_kernel,
            place[2 * step : 2 * step + 2] + 8 * (1 - x),
            core,
            *operands,
            columns + LANES,
            jnp.int16,
        )
        from_x.append(partner(piece, "xl", 1))
    mine = gradient_chunks(
        product_kernel, place + 8 * x, core, *operands, columns, jnp.float32
    )
    received = ()
    for step in range(4):
        down, up = hop(step, mine, from_x[step], received)
        received = (shifted(down, "z", -1), shifted(up, "z", 1) if step < 3 else up)
    total = received[1] + decoded(received[0])
    kept = lax.dynamic_slice_in_dim(total, core * rows, rows, 0)
    given = lax.dynamic_slice_in_dim(total, (1 - core) * rows, rows, 0)
    taken = partner(given, "core", 1)
    return jnp.where(
        core == 0, jnp.concatenate([kept, taken], 1), jnp.concatenate([taken, kept], 1)
    )


def orthonormal(proj):
    first, second = proj[0], proj[1]
    unit_first = first * lax.rsqrt(jnp.sum(first * first) + EPS)
    remain = second - jnp.sum(unit_first * second) * unit_first
    unit_second = remain * lax.rsqrt(jnp.sum(remain * remain) + EPS)
    return [unit_first, unit_second]


def on_device(activ, grad_out, weight, q_seed):
    acts = activ[0]
    cotan = grad_out[0]
    weight_bf = weight[0]
    rows, width = weight_bf.shape
    own = lax.axis_index(SHARD)
    replica = lax.axis_index(CYCLE)
    cycle_size = lax.axis_size(CYCLE)

    grads = gradient_rows(acts, cotan)
    weights = lax.all_gather(weight_bf, SHARD, axis=0, tiled=True)
    grad_in = dot(cotan, weights, NT).astype(jnp.bfloat16)

    q_right = lax.dynamic_index_in_dim(q_seed, replica, 0, keepdims=False)
    q_left = lax.dynamic_index_in_dim(
        q_seed, (replica + cycle_size - 1) % cycle_size, 0, keepdims=False
    )
    probes = jnp.concatenate([q_right.T, q_left.T], 0).astype(jnp.bfloat16)
    from_grads = thin(dot(probes, cotan, NT), acts, NN)
    from_weight = dot(probes, weight_bf, NT)
    at_own = lax.broadcasted_iota(jnp.int32, (1, width), 1) // rows == own
    from_weight = jnp.where(at_own, jnp.tile(from_weight, (1, width // rows)), 0.0)
    proj_right, proj_left = edges(shard_sum(from_weight - LEARN * from_grads))

    basis = jnp.stack(orthonormal(proj_right) + orthonormal(proj_left), 0)
    basis_own = lax.dynamic_slice_in_dim(basis, own * rows, rows, 1)
    back = thin(basis_own, weight_bf, NN) - LEARN * thin(thin(basis, acts, NT), cotan, NN)
    next_right, next_left = edges(shard_sum(back))

    basis_rows = basis_own.T
    moves = (
        basis_rows[:, 0:1] * next_right[0:1]
        + basis_rows[:, 1:2] * next_right[1:2]
        - basis_rows[:, 2:3] * next_left[0:1]
        - basis_rows[:, 3:4] * next_left[1:2]
    )
    new_weight = weight_bf.astype(jnp.float32) - LEARN * grads - GOSSIP * moves
    return (grad_in[None], new_weight[None], next_right.T[None])


def solution(mesh):
    fine = Mesh(mesh.devices.reshape(2, 4, 2, 8, 2), CYCLE + SHARD)
    tokens = P(CYCLE, SHARD, None)
    return jax.shard_map(
        on_device,
        mesh=fine,
        in_specs=(tokens, tokens, tokens, P()),
        out_specs=(tokens, tokens, P(CYCLE, None, None)),
        check_vma=False,
    )
```

```python
import functools

import jax
import jax.numpy as jnp
from jax import lax
from jax.experimental import pallas as pl
from jax.experimental.pallas import tpu as pltpu
from jax.sharding import Mesh
from jax.sharding import PartitionSpec as P

LEARN = 0.002
GOSSIP = 0.5
EPS = 1e-06
LANES = 128
LEVELS = 64.0
STEPS = 32767.0
VMEM = 32 * 2**20
STEPS_ALONG = (("core", 1), ("xl", 1), ("z", 1), ("z", 2), ("z", 4))

CYCLE = ("xh", "y")
SHARD = ("xl", "z", "core")
NT = (((1,), (1,)), ((), ()))
NN = (((1,), (0,)), ((), ()))
TN = (((0,), (0,)), ((), ()))


def dot(left, right, dims):
    return lax.dot_general(left, right, dims, preferred_element_type=jnp.float32)


def terms(value):
    high = value.astype(jnp.bfloat16)
    rest = value - high.astype(jnp.float32)
    middle = rest.astype(jnp.bfloat16)
    low = (rest - middle.astype(jnp.float32)).astype(jnp.bfloat16)
    parts = [part.astype(jnp.float32) for part in (high, middle, low)]
    return jnp.concatenate(parts, 0).astype(jnp.bfloat16)


def summed(value):
    return value[:8] + (value[8:16] + value[16:])


def thin(left, right, dims):
    return summed(dot(left, right, dims))


def own_columns(own, rows, width):
    row = lax.broadcasted_iota(jnp.int32, (rows, width), 0) + own * rows
    column = lax.broadcasted_iota(jnp.int32, (rows, width), 1)
    return jnp.where(row == column, 1.0, 0.0).astype(jnp.bfloat16)


def kernel_call(kernel, operands, out_shape, scalars=None, after=(), flops=0):
    whole = pl.BlockSpec(memory_space=pltpu.VMEM)
    specs = [whole] * len(operands) + [pl.BlockSpec(memory_space=pl.ANY)] * len(after)
    first = []
    if scalars is not None:
        specs, first = [pl.BlockSpec(memory_space=pltpu.SMEM)] + specs, [scalars]
    lead, unused = len(first) + len(operands), len(after)

    def body(*refs):
        kernel(*refs[:lead], *refs[lead + unused :])

    moved = sum(a.size * a.dtype.itemsize for a in operands)
    return pl.pallas_call(
        body,
        in_specs=specs,
        out_specs=jax.tree.map(lambda _: whole, out_shape),
        out_shape=out_shape,
        cost_estimate=pl.CostEstimate(flops=flops, bytes_accessed=moved, transcendentals=0),
        compiler_params=pltpu.CompilerParams(vmem_limit_bytes=VMEM),
    )(*first, *operands, *after)


def f32(*shape):
    return jax.ShapeDtypeStruct(shape, jnp.float32)


def probe_kernel(own, probes, acts, cotan, weight, out):
    rows, width = weight.shape
    from_grads = thin(terms(dot(probes[...], cotan[...], NT)[:8]), acts[...], NN)
    from_weight = terms(dot(probes[...], weight[...], NT)[:8])
    placed = thin(from_weight, own_columns(own[0], rows, width), NN)
    out[...] = (placed - LEARN * from_grads)[:4]


def unit_vectors(proj):
    first, second = proj[0:1], proj[1:2]
    unit_first = first * lax.rsqrt(jnp.sum(first * first, keepdims=True) + EPS)
    remain = second - jnp.sum(unit_first * second, keepdims=True) * unit_first
    unit_second = remain * lax.rsqrt(jnp.sum(remain * remain, keepdims=True) + EPS)
    return [unit_first, unit_second]


def basis_kernel(
    own, right, left, from_right, from_left, acts, cotan, weight, out, out_basis
):
    rows, width = weight.shape
    units = unit_vectors(right[...] - from_right[...])
    units += unit_vectors(from_left[...] - left[...])
    row = lax.broadcasted_iota(jnp.int32, (8, width), 0)
    basis = jnp.zeros((8, width), jnp.float32)
    for k, unit in enumerate(units):
        basis = jnp.where(row == k, jnp.broadcast_to(unit, (8, width)), basis)
    parts = terms(basis)
    own_parts = dot(parts, own_columns(own[0], rows, width), NT)
    out_basis[...] = summed(own_parts)
    from_weight = thin(own_parts.astype(jnp.bfloat16), weight[...], NN)
    from_grads = thin(terms(thin(parts, acts[...], NT)), cotan[...], NN)
    out[...] = (from_weight - LEARN * from_grads)[:4]


def add_kernel(left, right, out):
    out[...] = left[...] + right[...]


def add_split_kernel(left, right, out_right, out_left):
    total = left[...] + right[...]
    out_right[...] = total[:2]
    out_left[...] = total[2:]


def partner(value, axis, step):
    count = lax.axis_size(axis)
    return lax.ppermute(value, axis, [(i, i ^ step) for i in range(count)])


def shard_sum(value, steps, after):
    for axis, step in steps:
        key = axis + str(step)
        operands = (value, partner(value, axis, step))
        if key == "z4":
            halves = (f32(2, value.shape[1]), f32(2, value.shape[1]))
            value = kernel_call(add_split_kernel, operands, halves, after=after.get(key, ()))
        else:
            value = kernel_call(add_kernel, operands, f32(*value.shape), after=after.get(key, ()))
    return value


def passed_along(value, steps):
    count = lax.axis_size(CYCLE)
    return lax.ppermute(value, CYCLE, [(i, (i + steps) % count) for i in range(count)])


def neighbours(right, left):
    return passed_along(left, -1), passed_along(right, 1)


def coded(value):
    largest = jnp.maximum(jnp.max(jnp.abs(value), 1, keepdims=True), 1e-30)
    level = jnp.ceil(jnp.log2(largest) * LEVELS + 0.01)
    steps = jnp.floor(value * (STEPS * jnp.exp2(level * (-1.0 / LEVELS))) + 0.5)
    steps = jnp.clip(steps, -STEPS, STEPS).astype(jnp.int32)
    level = jnp.broadcast_to(level, (value.shape[0], LANES)).astype(jnp.int32)
    return jnp.concatenate([steps, level], 1).astype(jnp.int16)


def decoded(code):
    code = code.astype(jnp.int32).astype(jnp.float32)
    size = jnp.exp2(code[:, -1:] * (1.0 / LEVELS)) * (1.0 / STEPS)
    return code[:, :-LANES] * size


def product(place, first, count, acts, other_acts, cotan, other_cotan):
    rows = acts.shape[1] // 8

    def columns(ref):
        return jnp.concatenate(
            [ref[:, pl.ds(pl.multiple_of(place[first + k] * rows, rows), rows)] for k in range(count)], 1
        )

    return dot(columns(acts), cotan[...], TN) + dot(columns(other_acts), other_cotan[...], TN)


def chunk_kernel(first, place, acts, other_acts, cotan, other_cotan, *outs):
    rows = acts.shape[1] // 8
    for k, out in enumerate(outs):
        value = product(place, first + 2 * k, 2, acts, other_acts, cotan, other_cotan)
        out[0] = coded(value[:rows])
        out[1] = coded(value[rows:])


def mine_kernel(place, acts, other_acts, cotan, other_cotan, out):
    rows = acts.shape[1] // 8
    for k in range(2):
        value = product(place, 4 * k, 4, acts, other_acts, cotan, other_cotan)
        for j in range(4):
            out[4 * k + j] = value[rows * j : rows * (j + 1)]


def chunks(kernel, out_shape, scalars, acts, other_acts, cotan, other_cotan, after):
    tokens, width = acts.shape
    half = width // 2
    outs = jax.tree.leaves(out_shape)
    unused = len(after)

    def body(place, *refs):
        kernel(place, *refs[:4], *refs[4 + unused :])

    def spec(shape):
        return pl.BlockSpec(shape, lambda i, at: (0,) * len(shape))

    return pl.pallas_call(
        body,
        grid_spec=pltpu.PrefetchScalarGridSpec(
            num_scalar_prefetch=1,
            grid=(1,),
            in_specs=[
                pl.BlockSpec((tokens, half), lambda i, at: (0, at[8])),
                pl.BlockSpec((tokens, half), lambda i, at: (0, at[8])),
                pl.BlockSpec((tokens, half), lambda i, at: (0, at[9])),
                pl.BlockSpec((tokens, half), lambda i, at: (0, 0)),
            ]
            + [pl.BlockSpec(memory_space=pl.ANY)] * unused,
            out_specs=jax.tree.map(lambda a: spec(a.shape), out_shape),
        ),
        out_shape=out_shape,
        cost_estimate=pl.CostEstimate(
            flops=4 * tokens * half * sum(a.shape[0] * a.shape[1] for a in outs),
            bytes_accessed=8 * tokens * half,
            transcendentals=0,
        ),
        compiler_params=pltpu.CompilerParams(vmem_limit_bytes=VMEM),
    )(scalars, acts, other_acts, cotan, other_cotan, *after)


def hop_kernel(step, *refs):
    mine, from_x = refs[:2]
    down = mine[0] + decoded(from_x[0])
    up = mine[1] + decoded(from_x[1])
    if step > 0:
        down = down + decoded(refs[2][...])
        up = up + decoded(refs[3][...])
    refs[-2][...] = coded(down)
    refs[-1][...] = up if step == 3 else coded(up)


def hop(step, mine, from_x, received):
    _, rows, columns = mine.shape
    wide = columns + LANES
    whole = pl.BlockSpec((rows, wide), lambda i: (0, 0))
    sent = jax.ShapeDtypeStruct((rows, wide), jnp.int16)
    last = jax.ShapeDtypeStruct((rows, columns), jnp.float32) if step == 3 else sent
    return pl.pallas_call(
        functools.partial(hop_kernel, step),
        grid=(1,),
        in_specs=[
            pl.BlockSpec((2, rows, columns), lambda i: (step, 0, 0)),
            pl.BlockSpec((2, rows, wide), lambda i: (0, 0, 0)),
        ]
        + [whole] * len(received),
        out_specs=[whole, pl.BlockSpec(last.shape, lambda i: (0, 0))],
        out_shape=[sent, last],
        cost_estimate=pl.CostEstimate(
            flops=20 * rows * columns, bytes_accessed=16 * rows * columns, transcendentals=0
        ),
        compiler_params=pltpu.CompilerParams(vmem_limit_bytes=VMEM),
    )(mine, from_x, *received)


def shifted(value, axis, steps):
    count = lax.axis_size(axis)
    return lax.ppermute(value, axis, [(i, (i + steps) % count) for i in range(count)])


def on_device(activ, grad_out, weight, q_seed):
    acts = activ[0]
    cotan = grad_out[0]
    weight_bf = weight[0]
    rows, width = weight_bf.shape
    columns = width // 2
    core, x, z = lax.axis_index("core"), lax.axis_index("xl"), lax.axis_index("z")
    own = lax.axis_index(SHARD)
    replica = lax.axis_index(CYCLE)
    cycle_size = lax.axis_size(CYCLE)

    weights = lax.all_gather(weight_bf, SHARD, axis=0, tiled=True)
    grad_in = dot(cotan, weights, NT).astype(jnp.bfloat16)

    other_acts = partner(acts, "core", 1)
    other_cotan = partner(
        lax.dynamic_slice_in_dim(cotan, (1 - core) * columns, columns, 1), "core", 1
    )
    tokens = (acts, other_acts, cotan, other_cotan)

    q_right = lax.dynamic_index_in_dim(q_seed, replica, 0, keepdims=False)
    q_left = lax.dynamic_index_in_dim(
        q_seed, (replica + cycle_size - 1) % cycle_size, 0, keepdims=False
    )
    probes = jnp.concatenate([q_right, q_left], 1).astype(jnp.bfloat16).T
    probes = jnp.pad(probes, ((0, 12), (0, 0)))
    at = own[None].astype(jnp.int32)
    part = kernel_call(probe_kernel, (probes, acts, cotan, weight_bf), f32(4, width), at)

    place = [(z + offset) % 8 for step in range(4) for offset in (4 + step, 3 - step)]
    scalars = jnp.stack(place + [1 - x, core]).astype(jnp.int32)
    mine_scalars = jnp.stack(place + [x, core]).astype(jnp.int32)
    piece = jax.ShapeDtypeStruct((2, 2 * rows, columns + LANES), jnp.int16)
    first = chunks(functools.partial(chunk_kernel, 0), (piece,), scalars, *tokens, (part,))
    others = chunks(functools.partial(chunk_kernel, 2), (piece,) * 3, scalars, *tokens, first)
    from_x = [partner(value, "xl", 1) for value in (*first, *others)]
    mine = chunks(mine_kernel, f32(8, 2 * rows, columns), mine_scalars, *tokens, others[2:])

    def hops(step, received):
        down, up = hop(step, mine, from_x[step], received)
        return (shifted(down, "z", -1), shifted(up, "z", 1) if step < 3 else up), (down,)

    received, sent = hops(0, ())
    value = shard_sum(
        part, STEPS_ALONG, {"core1": first, "xl1": others[:1], "z1": (mine,), "z4": sent}
    )
    right, left = value
    back, basis = kernel_call(
        basis_kernel,
        (right, left, *neighbours(right, left), acts, cotan, weight_bf),
        (f32(4, width), f32(8, rows)),
        at,
    )
    received, sent_1 = hops(1, received)
    received, sent_2 = hops(2, received)
    received, sent_3 = hops(3, received)
    right, left = shard_sum(
        back, STEPS_ALONG, {"core1": sent_1, "z1": sent_2, "z4": sent_3}
    )
    from_right, from_left = neighbours(right, left)
    next_right, next_left = right - from_right, from_left - left

    total = received[1] + decoded(received[0])
    kept = lax.dynamic_slice_in_dim(total, core * rows, rows, 0)
    given = lax.dynamic_slice_in_dim(total, (1 - core) * rows, rows, 0)
    taken = partner(given, "core", 1)
    grads = jnp.where(
        core == 0, jnp.concatenate([kept, taken], 1), jnp.concatenate([taken, kept], 1)
    )

    basis_rows = basis.T
    moves = (
        basis_rows[:, 0:1] * next_right[0:1]
        + basis_rows[:, 1:2] * next_right[1:2]
        - basis_rows[:, 2:3] * next_left[0:1]
        - basis_rows[:, 3:4] * next_left[1:2]
    )
    new_weight = weight_bf.astype(jnp.float32) - LEARN * grads - GOSSIP * moves
    return (grad_in[None], new_weight[None], next_right.T[None])


def solution(mesh):
    fine = Mesh(mesh.devices.reshape(2, 4, 2, 8, 2), CYCLE + SHARD)
    tokens = P(CYCLE, SHARD, None)
    return jax.shard_map(
        on_device,
        mesh=fine,
        in_specs=(tokens, tokens, tokens, P()),
        out_specs=(tokens, tokens, P(CYCLE, None, None)),
        check_vma=False,
    )
```

```python
import functools

import jax
import jax.numpy as jnp
from jax import lax
from jax.experimental import pallas as pl
from jax.experimental.pallas import tpu as pltpu
from jax.sharding import Mesh
from jax.sharding import PartitionSpec as P

LEARN = 0.002
GOSSIP = 0.5
EPS = 1e-06
LANES = 128
LEVELS = 64.0
STEPS = 32767.0
VMEM = 32 * 2**20
MARK = jax.ShapeDtypeStruct((8, 128), jnp.float32)
NO_COST = pl.CostEstimate(flops=0, bytes_accessed=0, transcendentals=0)
STEPS_ALONG = (("core", 1), ("xl", 1), ("z", 1), ("z", 2), ("z", 4))

CYCLE = ("xh", "y")
SHARD = ("xl", "z", "core")
NT = (((1,), (1,)), ((), ()))
NN = (((1,), (0,)), ((), ()))
TN = (((0,), (0,)), ((), ()))


def dot(left, right, dims):
    return lax.dot_general(left, right, dims, preferred_element_type=jnp.float32)


def terms(value):
    high = value.astype(jnp.bfloat16)
    rest = value - high.astype(jnp.float32)
    middle = rest.astype(jnp.bfloat16)
    low = (rest - middle.astype(jnp.float32)).astype(jnp.bfloat16)
    parts = [part.astype(jnp.float32) for part in (high, middle, low)]
    return jnp.concatenate(parts, 0).astype(jnp.bfloat16)


def summed(value):
    return value[:8] + (value[8:16] + value[16:])


def thin(left, right, dims):
    return summed(dot(left, right, dims))


def own_columns(own, rows, width):
    row = lax.broadcasted_iota(jnp.int32, (rows, width), 0) + own * rows
    column = lax.broadcasted_iota(jnp.int32, (rows, width), 1)
    return jnp.where(row == column, 1.0, 0.0).astype(jnp.bfloat16)


def kernel_call(kernel, operands, out_shape, scalars=None, after=()):
    whole = pl.BlockSpec(memory_space=pltpu.VMEM)
    specs = [whole] * len(operands) + [pl.BlockSpec(memory_space=pl.ANY)] * len(after)
    first = []
    if scalars is not None:
        specs, first = [pl.BlockSpec(memory_space=pltpu.SMEM)] + specs, [scalars]
    lead, unused = len(first) + len(operands), len(after)

    def body(*refs):
        kernel(*refs[:lead], *refs[lead + unused :])

    return pl.pallas_call(
        body,
        in_specs=specs,
        out_specs=jax.tree.map(lambda _: whole, out_shape),
        out_shape=out_shape,
        cost_estimate=NO_COST,
        compiler_params=pltpu.CompilerParams(vmem_limit_bytes=VMEM),
    )(*first, *operands, *after)


def f32(*shape):
    return jax.ShapeDtypeStruct(shape, jnp.float32)


def probe_kernel(own, probes, acts, cotan, weight, out):
    rows, width = weight.shape
    from_grads = thin(terms(dot(probes[...], cotan[...], NT)[:8]), acts[...], NN)
    from_weight = terms(dot(probes[...], weight[...], NT)[:8])
    placed = thin(from_weight, own_columns(own[0], rows, width), NN)
    out[...] = (placed - LEARN * from_grads)[:4]


def unit_vectors(proj):
    first, second = proj[0:1], proj[1:2]
    unit_first = first * lax.rsqrt(jnp.sum(first * first, keepdims=True) + EPS)
    remain = second - jnp.sum(unit_first * second, keepdims=True) * unit_first
    unit_second = remain * lax.rsqrt(jnp.sum(remain * remain, keepdims=True) + EPS)
    return [unit_first, unit_second]


def basis_kernel(
    own, right, left, from_right, from_left, acts, cotan, weight, out, out_basis
):
    rows, width = weight.shape
    units = unit_vectors(right[...] - from_right[...])
    units += unit_vectors(from_left[...] - left[...])
    row = lax.broadcasted_iota(jnp.int32, (8, width), 0)
    basis = jnp.zeros((8, width), jnp.float32)
    for k, unit in enumerate(units):
        basis = jnp.where(row == k, jnp.broadcast_to(unit, (8, width)), basis)
    parts = terms(basis)
    own_parts = dot(parts, own_columns(own[0], rows, width), NT)
    out_basis[...] = summed(own_parts)
    from_weight = thin(own_parts.astype(jnp.bfloat16), weight[...], NN)
    from_grads = thin(terms(thin(parts, acts[...], NT)), cotan[...], NN)
    out[...] = (from_weight - LEARN * from_grads)[:4]


def add_kernel(left, right, out):
    out[...] = left[...] + right[...]


def add_split_kernel(left, right, out_right, out_left):
    total = left[...] + right[...]
    out_right[...] = total[:2]
    out_left[...] = total[2:]


def partner(value, axis, step):
    count = lax.axis_size(axis)
    return lax.ppermute(value, axis, [(i, i ^ step) for i in range(count)])


def shard_sum(value, steps, after):
    for axis, step in steps:
        key = axis + str(step)
        operands = (value, partner(value, axis, step))
        if key == "z4":
            halves = (f32(2, value.shape[1]), f32(2, value.shape[1]))
            value = kernel_call(add_split_kernel, operands, halves, after=after.get(key, ()))
        else:
            value = kernel_call(add_kernel, operands, f32(*value.shape), after=after.get(key, ()))
    return value


def passed_along(value, steps):
    count = lax.axis_size(CYCLE)
    return lax.ppermute(value, CYCLE, [(i, (i + steps) % count) for i in range(count)])


def neighbours(right, left):
    return passed_along(left, -1), passed_along(right, 1)


def coded(value):
    largest = jnp.maximum(jnp.max(jnp.abs(value), 1, keepdims=True), 1e-30)
    level = jnp.ceil(jnp.log2(largest) * LEVELS + 0.01)
    steps = jnp.floor(value * (STEPS * jnp.exp2(level * (-1.0 / LEVELS))) + 0.5)
    steps = jnp.clip(steps, -STEPS, STEPS).astype(jnp.int32)
    level = jnp.broadcast_to(level, (value.shape[0], LANES)).astype(jnp.int32)
    return jnp.concatenate([steps, level], 1).astype(jnp.int16)


def decoded(code):
    code = code.astype(jnp.int32).astype(jnp.float32)
    size = jnp.exp2(code[:, -1:] * (1.0 / LEVELS)) * (1.0 / STEPS)
    return code[:, :-LANES] * size


def product(place, first, count, acts, other_acts, cotan, other_cotan):
    rows = acts.shape[1] // 8

    def columns(ref):
        return jnp.concatenate(
            [ref[:, pl.ds(pl.multiple_of(place[first + k] * rows, rows), rows)] for k in range(count)], 1
        )

    return dot(columns(acts), cotan[...], TN) + dot(columns(other_acts), other_cotan[...], TN)


def chunk_kernel(first, place, acts, other_acts, cotan, other_cotan, *outs):
    rows = acts.shape[1] // 8
    outs, mark = outs[:-1], outs[-1]
    mark[...] = jnp.zeros_like(mark)
    for k, out in enumerate(outs):
        value = product(place, first + 2 * k, 2, acts, other_acts, cotan, other_cotan)
        out[0] = coded(value[:rows])
        out[1] = coded(value[rows:])


def mine_kernel(place, acts, other_acts, cotan, other_cotan, out, mark):
    rows = acts.shape[1] // 8
    mark[...] = jnp.zeros_like(mark)
    for k in range(2):
        value = product(place, 4 * k, 4, acts, other_acts, cotan, other_cotan)
        for j in range(4):
            out[4 * k + j] = value[rows * j : rows * (j + 1)]


def chunks(kernel, out_shape, scalars, acts, other_acts, cotan, other_cotan, after):
    tokens, width = acts.shape
    half = width // 2
    unused = len(after)

    def body(place, *refs):
        kernel(place, *refs[:4], *refs[4 + unused :])

    def spec(shape):
        return pl.BlockSpec(shape, lambda i, at: (0,) * len(shape))

    return pl.pallas_call(
        body,
        grid_spec=pltpu.PrefetchScalarGridSpec(
            num_scalar_prefetch=1,
            grid=(1,),
            in_specs=[
                pl.BlockSpec((tokens, half), lambda i, at: (0, at[8])),
                pl.BlockSpec((tokens, half), lambda i, at: (0, at[8])),
                pl.BlockSpec((tokens, half), lambda i, at: (0, at[9])),
                pl.BlockSpec((tokens, half), lambda i, at: (0, at[9])),
            ]
            + [pl.BlockSpec(memory_space=pl.ANY)] * unused,
            out_specs=jax.tree.map(lambda a: spec(a.shape), out_shape),
        ),
        out_shape=out_shape,
        cost_estimate=NO_COST,
        compiler_params=pltpu.CompilerParams(vmem_limit_bytes=VMEM),
    )(scalars, acts, other_acts, cotan, other_cotan, *after)


def hop_kernel(step, unused, *refs):
    mine, from_x = refs[:2]
    down = mine[0] + decoded(from_x[0])
    up = mine[1] + decoded(from_x[1])
    if step > 0:
        down = down + decoded(refs[2][...])
        up = up + decoded(refs[3][...])
    refs[-3][...] = coded(down)
    refs[-2][...] = up if step == 3 else coded(up)
    refs[-1][...] = jnp.zeros_like(refs[-1])


def hop(step, mine, from_x, received, after):
    _, rows, columns = mine.shape
    wide = columns + LANES
    whole = pl.BlockSpec((rows, wide), lambda i: (0, 0))
    sent = jax.ShapeDtypeStruct((rows, wide), jnp.int16)
    last = jax.ShapeDtypeStruct((rows, columns), jnp.float32) if step == 3 else sent
    return pl.pallas_call(
        functools.partial(hop_kernel, step, len(after)),
        grid=(1,),
        in_specs=[
            pl.BlockSpec((2, rows, columns), lambda i: (step, 0, 0)),
            pl.BlockSpec((2, rows, wide), lambda i: (0, 0, 0)),
        ]
        + [whole] * len(received)
        + [pl.BlockSpec(memory_space=pl.ANY)] * len(after),
        out_specs=[whole] + [pl.BlockSpec(a.shape, lambda i: (0, 0)) for a in (last, MARK)],
        out_shape=[sent, last, MARK],
        cost_estimate=NO_COST,
        compiler_params=pltpu.CompilerParams(vmem_limit_bytes=VMEM),
    )(mine, from_x, *received, *after)


def total_kernel(core, up, down, kept, given, mark):
    total = up[...] + decoded(down[...])
    mark[...] = jnp.zeros_like(mark)
    rows = kept.shape[0]
    mine = jnp.where(core[0] == 0, 1.0, 0.0)
    kept[...] = jnp.where(mine > 0.5, total[:rows], total[rows:])
    given[...] = jnp.where(mine > 0.5, total[rows:], total[:rows])


def shifted(value, axis, steps):
    count = lax.axis_size(axis)
    return lax.ppermute(value, axis, [(i, (i + steps) % count) for i in range(count)])


def column_half(value, core):
    columns = value.shape[1] // 2
    kept = lax.dynamic_slice_in_dim(value, core * columns, columns, 1)
    given = lax.dynamic_slice_in_dim(value, (1 - core) * columns, columns, 1)
    taken = partner(given, "core", 1)
    return jnp.concatenate(
        [jnp.where(core == 0, kept, taken), jnp.where(core == 0, taken, kept)], 0
    )


def held(value, after):
    def body(*refs):
        pass

    anywhere = pl.BlockSpec(memory_space=pl.ANY)
    return pl.pallas_call(
        body,
        in_specs=[anywhere] * (1 + len(after)),
        out_specs=anywhere,
        out_shape=jax.ShapeDtypeStruct(value.shape, value.dtype),
        input_output_aliases={0: 0},
        cost_estimate=NO_COST,
    )(value, *after)


def input_kernel(unused, at, cotan, other_half, weights, other_weights, *refs):
    out = refs[unused]
    value = dot(cotan[...], weights[...], NT) + dot(other_half[...], other_weights[...], NT)
    out[...] = value.astype(jnp.bfloat16)


def backward_input(core, cotan, weights, other_weights, after):
    tokens, width = cotan.shape
    half, tile = width // 2, width // 8
    return pl.pallas_call(
        functools.partial(input_kernel, len(after)),
        grid_spec=pltpu.PrefetchScalarGridSpec(
            num_scalar_prefetch=1,
            grid=(8,),
            in_specs=[
                pl.BlockSpec((tokens, half), lambda i, at: (0, at[0])),
                pl.BlockSpec((tokens, half), lambda i, at: (0, 1 - at[0])),
                pl.BlockSpec((tile, half), lambda i, at: (i, 0)),
                pl.BlockSpec((tile, half), lambda i, at: (i, 0)),
            ]
            + [pl.BlockSpec(memory_space=pl.ANY)] * len(after),
            out_specs=pl.BlockSpec((tokens, tile), lambda i, at: (0, i)),
        ),
        out_shape=jax.ShapeDtypeStruct((tokens, width), jnp.bfloat16),
        cost_estimate=NO_COST,
        compiler_params=pltpu.CompilerParams(vmem_limit_bytes=VMEM),
    )(core[None].astype(jnp.int32), cotan, cotan, weights, other_weights, *after)


def on_device(activ, grad_out, weight, q_seed):
    acts = activ[0]
    cotan = grad_out[0]
    weight_bf = weight[0]
    rows, width = weight_bf.shape
    columns = width // 2
    core, x, z = lax.axis_index("core"), lax.axis_index("xl"), lax.axis_index("z")
    own = lax.axis_index(SHARD)
    replica = lax.axis_index(CYCLE)
    cycle_size = lax.axis_size(CYCLE)

    half = column_half(weight_bf, core)
    weights = lax.all_gather(half, ("xl", "z"), axis=0, tiled=True)

    other_acts = partner(acts, "core", 1)
    other_cotan = partner(cotan, "core", 1)
    tokens = (acts, other_acts, cotan, other_cotan)

    q_right = lax.dynamic_index_in_dim(q_seed, replica, 0, keepdims=False)
    q_left = lax.dynamic_index_in_dim(
        q_seed, (replica + cycle_size - 1) % cycle_size, 0, keepdims=False
    )
    probes = jnp.concatenate([q_right, q_left], 1).astype(jnp.bfloat16).T
    probes = jnp.pad(probes, ((0, 12), (0, 0)))
    at = own[None].astype(jnp.int32)
    part = kernel_call(probe_kernel, (probes, acts, cotan, weight_bf), f32(4, width), at)

    place = [(z + offset) % 8 for step in range(4) for offset in (4 + step, 3 - step)]
    scalars = jnp.stack(place + [1 - x, core]).astype(jnp.int32)
    mine_scalars = jnp.stack(place + [x, core]).astype(jnp.int32)
    piece = jax.ShapeDtypeStruct((2, 2 * rows, columns + LANES), jnp.int16)
    *first, mark_0 = chunks(
        functools.partial(chunk_kernel, 0), (piece, MARK), scalars, *tokens, (part,)
    )
    *others, mark_1 = chunks(
        functools.partial(chunk_kernel, 2), (piece, piece, piece, MARK), scalars, *tokens, (mark_0,)
    )
    from_x = [partner(value, "xl", 1) for value in (*first, *others)]
    mine, mark_2 = chunks(
        mine_kernel, (f32(8, 2 * rows, columns), MARK), mine_scalars, *tokens, (mark_1,)
    )

    def hops(step, received, after):
        down, up, mark = hop(step, mine, from_x[step], received, after)
        return (shifted(down, "z", -1), shifted(up, "z", 1) if step < 3 else up), (mark,)

    value = shard_sum(part, STEPS_ALONG[:3], {"core1": (mark_0,), "xl1": (mark_1,), "z1": (mark_2,)})
    received, sent = hops(0, (), (value,))
    right, left = shard_sum(value, STEPS_ALONG[3:], {"z2": sent})
    received, sent = hops(1, received, (right,))
    back, basis = kernel_call(
        basis_kernel,
        (right, left, *neighbours(right, left), acts, cotan, weight_bf),
        (f32(4, width), f32(8, rows)),
        at,
        sent,
    )
    value = shard_sum(back, STEPS_ALONG[:1], {})
    received, sent = hops(2, received, (value,))
    value = shard_sum(value, STEPS_ALONG[1:4], {"xl1": sent})
    received, sent = hops(3, received, (value,))
    weights = held(weights, sent)
    kept, given, mark = kernel_call(
        total_kernel,
        (received[1], received[0]),
        (f32(rows, columns), f32(rows, columns), MARK),
        core[None].astype(jnp.int32),
    )
    right, left = shard_sum(value, STEPS_ALONG[4:], {"z4": (mark,)})
    grad_in = backward_input(core, cotan, weights, partner(weights, "core", 1), (mark,))
    from_right, from_left = neighbours(right, left)
    next_right, next_left = right - from_right, from_left - left

    taken = partner(given, "core", 1)
    grads = jnp.where(
        core == 0, jnp.concatenate([kept, taken], 1), jnp.concatenate([taken, kept], 1)
    )

    basis_rows = basis.T
    moves = (
        basis_rows[:, 0:1] * next_right[0:1]
        + basis_rows[:, 1:2] * next_right[1:2]
        - basis_rows[:, 2:3] * next_left[0:1]
        - basis_rows[:, 3:4] * next_left[1:2]
    )
    new_weight = weight_bf.astype(jnp.float32) - LEARN * grads - GOSSIP * moves
    return (grad_in[None], new_weight[None], next_right.T[None])


def solution(mesh):
    fine = Mesh(mesh.devices.reshape(2, 4, 2, 8, 2), CYCLE + SHARD)
    tokens = P(CYCLE, SHARD, None)
    return jax.shard_map(
        on_device,
        mesh=fine,
        in_specs=(tokens, tokens, tokens, P()),
        out_specs=(tokens, tokens, P(CYCLE, None, None)),
        check_vma=False,
    )
```

```python
import functools

import jax
import jax.numpy as jnp
from jax import lax
from jax.experimental import pallas as pl
from jax.experimental.pallas import tpu as pltpu
from jax.sharding import Mesh
from jax.sharding import PartitionSpec as P

LEARN = 0.002
GOSSIP = 0.5
EPS = 1e-06
LANES = 128
LEVELS = 64.0
STEPS = 32767.0
VMEM = 32 * 2**20
MARK = jax.ShapeDtypeStruct((8, 128), jnp.float32)
NO_COST = pl.CostEstimate(flops=0, bytes_accessed=0, transcendentals=0)
STEPS_ALONG = (("core", 1), ("xl", 1), ("z", 1), ("z", 2), ("z", 4))

CYCLE = ("xh", "y")
SHARD = ("xl", "z", "core")
NT = (((1,), (1,)), ((), ()))
NN = (((1,), (0,)), ((), ()))
TN = (((0,), (0,)), ((), ()))


def dot(left, right, dims):
    return lax.dot_general(left, right, dims, preferred_element_type=jnp.float32)


def terms(value):
    high = value.astype(jnp.bfloat16)
    rest = value - high.astype(jnp.float32)
    middle = rest.astype(jnp.bfloat16)
    low = (rest - middle.astype(jnp.float32)).astype(jnp.bfloat16)
    parts = [part.astype(jnp.float32) for part in (high, middle, low)]
    return jnp.concatenate(parts, 0).astype(jnp.bfloat16)


def summed(value):
    return value[:8] + (value[8:16] + value[16:])


def thin(left, right, dims):
    return summed(dot(left, right, dims))


def own_columns(own, rows, width):
    row = lax.broadcasted_iota(jnp.int32, (rows, width), 0) + own * rows
    column = lax.broadcasted_iota(jnp.int32, (rows, width), 1)
    return jnp.where(row == column, 1.0, 0.0).astype(jnp.bfloat16)


def kernel_call(kernel, operands, out_shape, scalars=None, after=()):
    whole = pl.BlockSpec(memory_space=pltpu.VMEM)
    specs = [whole] * len(operands) + [pl.BlockSpec(memory_space=pl.ANY)] * len(after)
    first = []
    if scalars is not None:
        specs, first = [pl.BlockSpec(memory_space=pltpu.SMEM)] + specs, [scalars]
    lead, unused = len(first) + len(operands), len(after)

    def body(*refs):
        kernel(*refs[:lead], *refs[lead + unused :])

    return pl.pallas_call(
        body,
        in_specs=specs,
        out_specs=jax.tree.map(lambda _: whole, out_shape),
        out_shape=out_shape,
        cost_estimate=NO_COST,
        compiler_params=pltpu.CompilerParams(vmem_limit_bytes=VMEM),
    )(*first, *operands, *after)


def f32(*shape):
    return jax.ShapeDtypeStruct(shape, jnp.float32)


def probe_kernel(own, probes, acts, cotan, weight, out):
    rows, width = weight.shape
    from_grads = thin(terms(dot(probes[...], cotan[...], NT)[:8]), acts[...], NN)
    from_weight = terms(dot(probes[...], weight[...], NT)[:8])
    placed = thin(from_weight, own_columns(own[0], rows, width), NN)
    out[...] = (placed - LEARN * from_grads)[:4]


def unit_vectors(proj):
    first, second = proj[0:1], proj[1:2]
    unit_first = first * lax.rsqrt(jnp.sum(first * first, keepdims=True) + EPS)
    remain = second - jnp.sum(unit_first * second, keepdims=True) * unit_first
    unit_second = remain * lax.rsqrt(jnp.sum(remain * remain, keepdims=True) + EPS)
    return [unit_first, unit_second]


def basis_kernel(
    own, right, left, from_right, from_left, acts, cotan, weight, out, out_basis
):
    rows, width = weight.shape
    units = unit_vectors(right[...] - from_right[...])
    units += unit_vectors(from_left[...] - left[...])
    row = lax.broadcasted_iota(jnp.int32, (8, width), 0)
    basis = jnp.zeros((8, width), jnp.float32)
    for k, unit in enumerate(units):
        basis = jnp.where(row == k, jnp.broadcast_to(unit, (8, width)), basis)
    parts = terms(basis)
    own_parts = dot(parts, own_columns(own[0], rows, width), NT)
    out_basis[...] = summed(own_parts)
    from_weight = thin(own_parts.astype(jnp.bfloat16), weight[...], NN)
    from_grads = thin(terms(thin(parts, acts[...], NT)), cotan[...], NN)
    out[...] = (from_weight - LEARN * from_grads)[:4]


def add_kernel(left, right, out):
    out[...] = left[...] + right[...]


def add_split_kernel(left, right, out_right, out_left):
    total = left[...] + right[...]
    out_right[...] = total[:2]
    out_left[...] = total[2:]


def partner(value, axis, step):
    count = lax.axis_size(axis)
    return lax.ppermute(value, axis, [(i, i ^ step) for i in range(count)])


def shard_sum(value, steps, after):
    for axis, step in steps:
        key = axis + str(step)
        operands = (value, partner(value, axis, step))
        if key == "z4":
            halves = (f32(2, value.shape[1]), f32(2, value.shape[1]))
            value = kernel_call(add_split_kernel, operands, halves, after=after.get(key, ()))
        else:
            value = kernel_call(add_kernel, operands, f32(*value.shape), after=after.get(key, ()))
    return value


def passed_along(value, steps):
    count = lax.axis_size(CYCLE)
    return lax.ppermute(value, CYCLE, [(i, (i + steps) % count) for i in range(count)])


def neighbours(right, left):
    return passed_along(left, -1), passed_along(right, 1)


def coded(value):
    largest = jnp.maximum(jnp.max(jnp.abs(value), 1, keepdims=True), 1e-30)
    level = jnp.ceil(jnp.log2(largest) * LEVELS + 0.01)
    steps = jnp.floor(value * (STEPS * jnp.exp2(level * (-1.0 / LEVELS))) + 0.5)
    steps = jnp.clip(steps, -STEPS, STEPS).astype(jnp.int32)
    level = jnp.broadcast_to(level, (value.shape[0], LANES)).astype(jnp.int32)
    return jnp.concatenate([steps, level], 1).astype(jnp.int16)


def decoded(code):
    code = code.astype(jnp.int32).astype(jnp.float32)
    size = jnp.exp2(code[:, -1:] * (1.0 / LEVELS)) * (1.0 / STEPS)
    return code[:, :-LANES] * size


def product(place, first, count, acts, other_acts, cotan, other_cotan):
    rows = acts.shape[1] // 8

    def columns(ref):
        return jnp.concatenate(
            [ref[:, pl.ds(pl.multiple_of(place[first + k] * rows, rows), rows)] for k in range(count)], 1
        )

    return dot(columns(acts), cotan[...], TN) + dot(columns(other_acts), other_cotan[...], TN)


def chunk_kernel(first, place, acts, other_acts, cotan, other_cotan, *outs):
    rows = acts.shape[1] // 8
    outs, mark = outs[:-1], outs[-1]
    mark[...] = jnp.zeros_like(mark)
    for k, out in enumerate(outs):
        value = product(place, first + 2 * k, 2, acts, other_acts, cotan, other_cotan)
        out[0] = coded(value[:rows])
        out[1] = coded(value[rows:])


def mine_kernel(place, acts, other_acts, cotan, other_cotan, out, mark):
    rows = acts.shape[1] // 8
    mark[...] = jnp.zeros_like(mark)
    for k in range(2):
        value = product(place, 4 * k, 4, acts, other_acts, cotan, other_cotan)
        for j in range(4):
            out[4 * k + j] = value[rows * j : rows * (j + 1)]


def chunks(kernel, out_shape, scalars, acts, other_acts, cotan, other_cotan, after):
    tokens, width = acts.shape
    half = width // 2
    unused = len(after)

    def body(place, *refs):
        kernel(place, *refs[:4], *refs[4 + unused :])

    def spec(shape):
        return pl.BlockSpec(shape, lambda i, at: (0,) * len(shape))

    return pl.pallas_call(
        body,
        grid_spec=pltpu.PrefetchScalarGridSpec(
            num_scalar_prefetch=1,
            grid=(1,),
            in_specs=[
                pl.BlockSpec((tokens, half), lambda i, at: (0, at[8])),
                pl.BlockSpec((tokens, half), lambda i, at: (0, at[8])),
                pl.BlockSpec((tokens, half), lambda i, at: (0, at[9])),
                pl.BlockSpec((tokens, half), lambda i, at: (0, at[9])),
            ]
            + [pl.BlockSpec(memory_space=pl.ANY)] * unused,
            out_specs=jax.tree.map(lambda a: spec(a.shape), out_shape),
        ),
        out_shape=out_shape,
        cost_estimate=NO_COST,
        compiler_params=pltpu.CompilerParams(vmem_limit_bytes=VMEM),
    )(scalars, acts, other_acts, cotan, other_cotan, *after)


def hop_kernel(step, unused, *refs):
    mine, from_x = refs[:2]
    down = mine[0] + decoded(from_x[0])
    up = mine[1] + decoded(from_x[1])
    if step > 0:
        down = down + decoded(refs[2][...])
        up = up + decoded(refs[3][...])
    refs[-3][...] = coded(down)
    refs[-2][...] = up if step == 3 else coded(up)
    refs[-1][...] = jnp.zeros_like(refs[-1])


def hop(step, mine, from_x, received, after):
    _, rows, columns = mine.shape
    wide = columns + LANES
    whole = pl.BlockSpec((rows, wide), lambda i: (0, 0))
    sent = jax.ShapeDtypeStruct((rows, wide), jnp.int16)
    last = jax.ShapeDtypeStruct((rows, columns), jnp.float32) if step == 3 else sent
    return pl.pallas_call(
        functools.partial(hop_kernel, step, len(after)),
        grid=(1,),
        in_specs=[
            pl.BlockSpec((2, rows, columns), lambda i: (step, 0, 0)),
            pl.BlockSpec((2, rows, wide), lambda i: (0, 0, 0)),
        ]
        + [whole] * len(received)
        + [pl.BlockSpec(memory_space=pl.ANY)] * len(after),
        out_specs=[whole] + [pl.BlockSpec(a.shape, lambda i: (0, 0)) for a in (last, MARK)],
        out_shape=[sent, last, MARK],
        cost_estimate=NO_COST,
        compiler_params=pltpu.CompilerParams(vmem_limit_bytes=VMEM),
    )(mine, from_x, *received, *after)


def total_kernel(core, up, down, kept, given, mark):
    total = up[...] + decoded(down[...])
    mark[...] = jnp.zeros_like(mark)
    rows = kept.shape[0]
    mine = jnp.where(core[0] == 0, 1.0, 0.0)
    kept[...] = jnp.where(mine > 0.5, total[:rows], total[rows:])
    given[...] = jnp.where(mine > 0.5, total[rows:], total[:rows])


def shifted(value, axis, steps):
    count = lax.axis_size(axis)
    return lax.ppermute(value, axis, [(i, (i + steps) % count) for i in range(count)])


def held(value, after):
    def body(*refs):
        pass

    anywhere = pl.BlockSpec(memory_space=pl.ANY)
    return pl.pallas_call(
        body,
        in_specs=[anywhere] * (1 + len(after)),
        out_specs=anywhere,
        out_shape=jax.ShapeDtypeStruct(value.shape, value.dtype),
        input_output_aliases={0: 0},
        cost_estimate=NO_COST,
    )(value, *after)


def input_kernel(unused, at, cotan, weights, other_weights, *refs):
    out, mark = refs[unused:]
    mark[...] = jnp.zeros_like(mark)
    core, x, z = at[0], at[1], pl.program_id(0)
    mine, theirs = weights[...], other_weights[...]
    rows = mine.shape[1]
    swapped = jnp.broadcast_to(core, (rows, mine.shape[2])) == 1
    blocks = []
    for column in range(2):
        first, second = mine[column], theirs[column]
        blocks += [jnp.where(swapped, second, first), jnp.where(swapped, first, second)]
    value = dot(cotan[...], jnp.concatenate(blocks, 0), NT).astype(jnp.bfloat16)
    wide = 2 * rows
    for column in range(2):
        chip = (x * (1 - column) + (1 - x) * column) * 8 + z
        place = pl.ds(pl.multiple_of(chip * wide, wide), wide)
        out[:, place] = value[:, column * wide : (column + 1) * wide]


def backward_input(core, x, cotan, weights, other_weights, after):
    tokens, width = cotan.shape
    rows = weights.shape[1]
    plane = pl.BlockSpec((2, rows, width), lambda i, at: (i, 0, 0))
    return pl.pallas_call(
        functools.partial(input_kernel, len(after)),
        grid_spec=pltpu.PrefetchScalarGridSpec(
            num_scalar_prefetch=1,
            grid=(8,),
            in_specs=[pl.BlockSpec((tokens, width), lambda i, at: (0, 0)), plane, plane]
            + [pl.BlockSpec(memory_space=pl.ANY)] * len(after),
            out_specs=[
                pl.BlockSpec((tokens, width), lambda i, at: (0, 0)),
                pl.BlockSpec(MARK.shape, lambda i, at: (0, 0)),
            ],
        ),
        out_shape=[jax.ShapeDtypeStruct((tokens, width), jnp.bfloat16), MARK],
        cost_estimate=NO_COST,
        compiler_params=pltpu.CompilerParams(vmem_limit_bytes=VMEM),
    )(jnp.stack([core, x]).astype(jnp.int32), cotan, weights, other_weights, *after)


def update_kernel(core, weight, kept, taken, basis, right, left, from_right, from_left, out, out_q):
    next_right = right[...] - from_right[...]
    next_left = from_left[...] - left[...]
    out_q[...] = next_right
    moves = (
        basis[:, 0:1] * next_right[0:1]
        + basis[:, 1:2] * next_right[1:2]
        - basis[:, 2:3] * next_left[0:1]
        - basis[:, 3:4] * next_left[1:2]
    )
    stepped = weight[...].astype(jnp.float32) - GOSSIP * moves
    columns = kept.shape[1]
    swapped = jnp.broadcast_to(core[0], kept.shape) == 1
    first = jnp.where(swapped, taken[...], kept[...])
    second = jnp.where(swapped, kept[...], taken[...])
    out[:, :columns] = stepped[:, :columns] - LEARN * first
    out[:, columns:] = stepped[:, columns:] - LEARN * second


def on_device(activ, grad_out, weight, q_seed):
    acts = activ[0]
    cotan = grad_out[0]
    weight_bf = weight[0]
    rows, width = weight_bf.shape
    columns = width // 2
    core, x, z = lax.axis_index("core"), lax.axis_index("xl"), lax.axis_index("z")
    own = lax.axis_index(SHARD)
    replica = lax.axis_index(CYCLE)
    cycle_size = lax.axis_size(CYCLE)

    pair = jnp.stack([weight_bf, partner(weight_bf, "xl", 1)], 0)
    weights = lax.all_gather(pair, "z", axis=0, tiled=True)

    other_acts = partner(acts, "core", 1)
    other_cotan = partner(cotan, "core", 1)
    tokens = (acts, other_acts, cotan, other_cotan)

    q_right = lax.dynamic_index_in_dim(q_seed, replica, 0, keepdims=False)
    q_left = lax.dynamic_index_in_dim(
        q_seed, (replica + cycle_size - 1) % cycle_size, 0, keepdims=False
    )
    probes = jnp.concatenate([q_right, q_left], 1).astype(jnp.bfloat16).T
    probes = jnp.pad(probes, ((0, 12), (0, 0)))
    at = own[None].astype(jnp.int32)
    part = kernel_call(probe_kernel, (probes, acts, cotan, weight_bf), f32(4, width), at)

    place = [(z + offset) % 8 for step in range(4) for offset in (4 + step, 3 - step)]
    scalars = jnp.stack(place + [1 - x, core]).astype(jnp.int32)
    mine_scalars = jnp.stack(place + [x, core]).astype(jnp.int32)
    piece = jax.ShapeDtypeStruct((2, 2 * rows, columns + LANES), jnp.int16)
    value = shard_sum(part, STEPS_ALONG[:1], {})
    *first, mark_0 = chunks(
        functools.partial(chunk_kernel, 0), (piece, MARK), scalars, *tokens, (value,)
    )
    value = shard_sum(value, STEPS_ALONG[1:2], {"xl1": (mark_0,)})
    first = [held(first[0], (value,))]
    *others, mark_1 = chunks(
        functools.partial(chunk_kernel, 2), (piece, piece, piece, MARK), scalars, *tokens, (value,)
    )
    from_x = [partner(value, "xl", 1) for value in (*first, *others)]
    mine, mark_2 = chunks(
        mine_kernel, (f32(8, 2 * rows, columns), MARK), mine_scalars, *tokens, (mark_1,)
    )

    def hops(step, received, after):
        down, up, mark = hop(step, mine, from_x[step], received, after)
        return (shifted(down, "z", -1), shifted(up, "z", 1) if step < 3 else up), (mark,)

    value = shard_sum(value, STEPS_ALONG[2:4], {"z1": (mark_1,), "z2": (mark_2,)})
    received, sent = hops(0, (), (value,))
    right, left = shard_sum(value, STEPS_ALONG[4:], {"z4": sent})
    received, sent = hops(1, received, (right,))
    back, basis = kernel_call(
        basis_kernel,
        (right, left, *neighbours(right, left), acts, cotan, weight_bf),
        (f32(4, width), f32(8, rows)),
        at,
        sent,
    )
    value = shard_sum(back, STEPS_ALONG[:1], {})
    received, sent = hops(2, received, (value,))
    value = shard_sum(value, STEPS_ALONG[1:4], {"xl1": sent})
    received, sent = hops(3, received, (value,))
    weights = held(weights, sent)
    kept, given, mark = kernel_call(
        total_kernel,
        (received[1], received[0]),
        (f32(rows, columns), f32(rows, columns), MARK),
        core[None].astype(jnp.int32),
    )
    right, left = shard_sum(value, STEPS_ALONG[4:], {"z4": (mark,)})
    grad_in, mark = backward_input(
        core, x, cotan, weights, partner(weights, "core", 1), (right,)
    )
    new_weight, next_q = kernel_call(
        update_kernel,
        (weight_bf, kept, partner(given, "core", 1), basis.T, right, left, *neighbours(right, left)),
        (f32(rows, width), f32(2, width)),
        core[None].astype(jnp.int32),
        (mark,),
    )
    return (grad_in[None], new_weight[None], next_q.T[None])


def solution(mesh):
    fine = Mesh(mesh.devices.reshape(2, 4, 2, 8, 2), CYCLE + SHARD)
    tokens = P(CYCLE, SHARD, None)
    return jax.shard_map(
        on_device,
        mesh=fine,
        in_specs=(tokens, tokens, tokens, P()),
        out_specs=(tokens, tokens, P(CYCLE, None, None)),
        check_vma=False,
    )
```

```python
import functools

import jax
import jax.numpy as jnp
from jax import lax
from jax.experimental import pallas as pl
from jax.experimental.pallas import tpu as pltpu
from jax.sharding import Mesh
from jax.sharding import PartitionSpec as P

LEARN = 0.002
GOSSIP = 0.5
EPS = 1e-06
LANES = 128
LEVELS = 64.0
STEPS = 32767.0
VMEM = 16 * 2**20
MOST_VMEM = 24 * 2**20
MARK = jax.ShapeDtypeStruct((8, 128), jnp.float32)
NO_COST = pl.CostEstimate(flops=0, bytes_accessed=0, transcendentals=0)
STEPS_ALONG = (("core", 1), ("xl", 1), ("z", 1), ("z", 2), ("z", 4))

CYCLE = ("xh", "y")
SHARD = ("xl", "z", "core")
NT = (((1,), (1,)), ((), ()))
NN = (((1,), (0,)), ((), ()))
TN = (((0,), (0,)), ((), ()))


def dot(left, right, dims):
    return lax.dot_general(left, right, dims, preferred_element_type=jnp.float32)


def terms(value):
    high = value.astype(jnp.bfloat16)
    rest = value - high.astype(jnp.float32)
    middle = rest.astype(jnp.bfloat16)
    low = (rest - middle.astype(jnp.float32)).astype(jnp.bfloat16)
    parts = [part.astype(jnp.float32) for part in (high, middle, low)]
    return jnp.concatenate(parts, 0).astype(jnp.bfloat16)


def summed(value):
    return value[:8] + (value[8:16] + value[16:])


def thin(left, right, dims):
    return summed(dot(left, right, dims))


def own_columns(own, rows, width):
    row = lax.broadcasted_iota(jnp.int32, (rows, width), 0) + own * rows
    column = lax.broadcasted_iota(jnp.int32, (rows, width), 1)
    return jnp.where(row == column, 1.0, 0.0).astype(jnp.bfloat16)


def kernel_call(kernel, operands, out_shape, scalars=None, after=()):
    whole = pl.BlockSpec(memory_space=pltpu.VMEM)
    specs = [whole] * len(operands) + [pl.BlockSpec(memory_space=pl.ANY)] * len(after)
    first = []
    if scalars is not None:
        specs, first = [pl.BlockSpec(memory_space=pltpu.SMEM)] + specs, [scalars]
    lead, unused = len(first) + len(operands), len(after)

    def body(*refs):
        kernel(*refs[:lead], *refs[lead + unused :])

    return pl.pallas_call(
        body,
        in_specs=specs,
        out_specs=jax.tree.map(lambda _: whole, out_shape),
        out_shape=out_shape,
        cost_estimate=NO_COST,
        compiler_params=pltpu.CompilerParams(vmem_limit_bytes=VMEM),
    )(*first, *operands, *after)


def f32(*shape):
    return jax.ShapeDtypeStruct(shape, jnp.float32)


def probe_kernel(own, probes, acts, cotan, weight, out):
    rows, width = weight.shape
    from_grads = thin(terms(dot(probes[...], cotan[...], NT)[:8]), acts[...], NN)
    from_weight = terms(dot(probes[...], weight[...], NT)[:8])
    placed = thin(from_weight, own_columns(own[0], rows, width), NN)
    out[...] = (placed - LEARN * from_grads)[:4]


def unit_vectors(proj):
    first, second = proj[0:1], proj[1:2]
    unit_first = first * lax.rsqrt(jnp.sum(first * first, keepdims=True) + EPS)
    remain = second - jnp.sum(unit_first * second, keepdims=True) * unit_first
    unit_second = remain * lax.rsqrt(jnp.sum(remain * remain, keepdims=True) + EPS)
    return [unit_first, unit_second]


def basis_kernel(
    own, right, left, from_right, from_left, acts, cotan, weight, out, out_basis
):
    rows, width = weight.shape
    units = unit_vectors(right[...] - from_right[...])
    units += unit_vectors(from_left[...] - left[...])
    row = lax.broadcasted_iota(jnp.int32, (8, width), 0)
    basis = jnp.zeros((8, width), jnp.float32)
    for k, unit in enumerate(units):
        basis = jnp.where(row == k, jnp.broadcast_to(unit, (8, width)), basis)
    parts = terms(basis)
    own_parts = dot(parts, own_columns(own[0], rows, width), NT)
    out_basis[...] = summed(own_parts)
    from_weight = thin(own_parts.astype(jnp.bfloat16), weight[...], NN)
    from_grads = thin(terms(thin(parts, acts[...], NT)), cotan[...], NN)
    out[...] = (from_weight - LEARN * from_grads)[:4]


def add_kernel(left, right, out):
    out[...] = left[...] + right[...]


def add_split_kernel(left, right, out_right, out_left):
    total = left[...] + right[...]
    out_right[...] = total[:2]
    out_left[...] = total[2:]


def partner(value, axis, step):
    count = lax.axis_size(axis)
    return lax.ppermute(value, axis, [(i, i ^ step) for i in range(count)])


def shard_sum(value, steps, after):
    for axis, step in steps:
        key = axis + str(step)
        operands = (value, partner(value, axis, step))
        if key == "z4":
            halves = (f32(2, value.shape[1]), f32(2, value.shape[1]))
            value = kernel_call(add_split_kernel, operands, halves, after=after.get(key, ()))
        else:
            value = kernel_call(add_kernel, operands, f32(*value.shape), after=after.get(key, ()))
    return value


def passed_along(value, steps):
    count = lax.axis_size(CYCLE)
    return lax.ppermute(value, CYCLE, [(i, (i + steps) % count) for i in range(count)])


def neighbours(right, left):
    return passed_along(left, -1), passed_along(right, 1)


def coded(value):
    largest = jnp.maximum(jnp.max(jnp.abs(value), 1, keepdims=True), 1e-30)
    level = jnp.ceil(jnp.log2(largest) * LEVELS + 0.01)
    steps = jnp.floor(value * (STEPS * jnp.exp2(level * (-1.0 / LEVELS))) + 0.5)
    steps = jnp.clip(steps, -STEPS, STEPS).astype(jnp.int32)
    level = jnp.broadcast_to(level, (value.shape[0], LANES)).astype(jnp.int32)
    return jnp.concatenate([steps, level], 1).astype(jnp.int16)


def decoded(code):
    code = code.astype(jnp.int32).astype(jnp.float32)
    size = jnp.exp2(code[:, -1:] * (1.0 / LEVELS)) * (1.0 / STEPS)
    return code[:, :-LANES] * size


def product(place, first, count, acts, other_acts, cotan, other_cotan):
    rows = acts.shape[1] // 8

    def columns(ref):
        return jnp.concatenate(
            [ref[:, pl.ds(pl.multiple_of(place[first + k] * rows, rows), rows)] for k in range(count)], 1
        )

    return dot(columns(acts), cotan[...], TN) + dot(columns(other_acts), other_cotan[...], TN)


def chunk_kernel(first, place, acts, other_acts, cotan, other_cotan, *outs):
    rows = acts.shape[1] // 8
    outs, mark = outs[:-1], outs[-1]
    mark[...] = jnp.zeros_like(mark)
    for out in outs:
        count = out.shape[0]
        value = product(place, first, count, acts, other_acts, cotan, other_cotan)
        for k in range(count):
            out[k] = coded(value[k * rows : (k + 1) * rows])
        first += count


def mine_kernel(place, acts, other_acts, cotan, other_cotan, out, mark):
    rows = acts.shape[1] // 8
    mark[...] = jnp.zeros_like(mark)
    for k in range(2):
        value = product(place, 4 * k, 4, acts, other_acts, cotan, other_cotan)
        for j in range(4):
            out[4 * k + j] = value[rows * j : rows * (j + 1)]


def chunks(kernel, out_shape, scalars, acts, other_acts, cotan, other_cotan, after):
    tokens, width = acts.shape
    half = width // 2
    unused = len(after)

    def body(place, *refs):
        kernel(place, *refs[:4], *refs[4 + unused :])

    def spec(shape):
        return pl.BlockSpec(shape, lambda i, at: (0,) * len(shape))

    return pl.pallas_call(
        body,
        grid_spec=pltpu.PrefetchScalarGridSpec(
            num_scalar_prefetch=1,
            grid=(1,),
            in_specs=[
                pl.BlockSpec((tokens, half), lambda i, at: (0, at[8])),
                pl.BlockSpec((tokens, half), lambda i, at: (0, at[8])),
                pl.BlockSpec((tokens, half), lambda i, at: (0, at[9])),
                pl.BlockSpec((tokens, half), lambda i, at: (0, at[9])),
            ]
            + [pl.BlockSpec(memory_space=pl.ANY)] * unused,
            out_specs=jax.tree.map(lambda a: spec(a.shape), out_shape),
        ),
        out_shape=out_shape,
        cost_estimate=NO_COST,
        compiler_params=pltpu.CompilerParams(vmem_limit_bytes=MOST_VMEM),
    )(scalars, acts, other_acts, cotan, other_cotan, *after)


def hop_kernel(step, unused, *refs):
    mine, from_x = refs[:2]
    down = mine[0] + decoded(from_x[0])
    up = mine[1] + decoded(from_x[1])
    if step > 0:
        down = down + decoded(refs[2][...])
        up = up + decoded(refs[3][...])
    refs[-3][...] = coded(down)
    refs[-2][...] = up if step == 3 else coded(up)
    refs[-1][...] = jnp.zeros_like(refs[-1])


def hop(step, mine, from_x, received, after):
    _, rows, columns = mine.shape
    wide = columns + LANES
    whole = pl.BlockSpec((rows, wide), lambda i: (0, 0))
    sent = jax.ShapeDtypeStruct((rows, wide), jnp.int16)
    last = jax.ShapeDtypeStruct((rows, columns), jnp.float32) if step == 3 else sent
    return pl.pallas_call(
        functools.partial(hop_kernel, step, len(after)),
        grid=(1,),
        in_specs=[
            pl.BlockSpec((2, rows, columns), lambda i: (step, 0, 0)),
            pl.BlockSpec((2, rows, wide), lambda i: (max(step - 2, 0), 0, 0)),
        ]
        + [whole] * len(received)
        + [pl.BlockSpec(memory_space=pl.ANY)] * len(after),
        out_specs=[whole] + [pl.BlockSpec(a.shape, lambda i: (0, 0)) for a in (last, MARK)],
        out_shape=[sent, last, MARK],
        cost_estimate=NO_COST,
        compiler_params=pltpu.CompilerParams(vmem_limit_bytes=VMEM),
    )(mine, from_x, *received, *after)


def total_kernel(core, up, down, kept, given, mark):
    total = up[...] + decoded(down[...])
    mark[...] = jnp.zeros_like(mark)
    rows = kept.shape[0]
    mine = jnp.where(core[0] == 0, 1.0, 0.0)
    kept[...] = jnp.where(mine > 0.5, total[:rows], total[rows:])
    given[...] = jnp.where(mine > 0.5, total[rows:], total[:rows])


def shifted(value, axis, steps):
    count = lax.axis_size(axis)
    return lax.ppermute(value, axis, [(i, (i + steps) % count) for i in range(count)])


def held(value, after):
    def body(*refs):
        pass

    anywhere = pl.BlockSpec(memory_space=pl.ANY)
    return pl.pallas_call(
        body,
        in_specs=[anywhere] * (1 + len(after)),
        out_specs=anywhere,
        out_shape=jax.ShapeDtypeStruct(value.shape, value.dtype),
        input_output_aliases={0: 0},
        cost_estimate=NO_COST,
    )(value, *after)


def input_kernel(unused, at, cotan, weights, other_weights, *refs):
    out, mark = refs[unused:]
    mark[...] = jnp.zeros_like(mark)
    core, x, z = at[0], at[1], pl.program_id(0)
    wide = 2 * weights.shape[1]

    def planes(first, second):
        blocks = [first[0], second[0], first[1], second[1]]
        value = dot(cotan[...], jnp.concatenate(blocks, 0), NT).astype(jnp.bfloat16)
        for column in range(2):
            chip = (x * (1 - column) + (1 - x) * column) * 8 + z
            place = pl.ds(pl.multiple_of(chip * wide, wide), wide)
            out[:, place] = value[:, column * wide : (column + 1) * wide]

    @pl.when(core == 0)
    def _():
        planes(weights, other_weights)

    @pl.when(core == 1)
    def _():
        planes(other_weights, weights)


def backward_input(core, x, cotan, weights, other_weights, after):
    tokens, width = cotan.shape
    rows = weights.shape[1]
    plane = pl.BlockSpec((2, rows, width), lambda i, at: (i, 0, 0))
    return pl.pallas_call(
        functools.partial(input_kernel, len(after)),
        grid_spec=pltpu.PrefetchScalarGridSpec(
            num_scalar_prefetch=1,
            grid=(8,),
            in_specs=[pl.BlockSpec((tokens, width), lambda i, at: (0, 0)), plane, plane]
            + [pl.BlockSpec(memory_space=pl.ANY)] * len(after),
            out_specs=[
                pl.BlockSpec((tokens, width), lambda i, at: (0, 0)),
                pl.BlockSpec(MARK.shape, lambda i, at: (0, 0)),
            ],
        ),
        out_shape=[jax.ShapeDtypeStruct((tokens, width), jnp.bfloat16), MARK],
        cost_estimate=NO_COST,
        compiler_params=pltpu.CompilerParams(vmem_limit_bytes=MOST_VMEM),
    )(jnp.stack([core, x]).astype(jnp.int32), cotan, weights, other_weights, *after)


def update_kernel(core, weight, kept, taken, basis, right, left, from_right, from_left, out, out_q):
    next_right = right[...] - from_right[...]
    next_left = from_left[...] - left[...]
    out_q[...] = next_right
    moves = (
        basis[:, 0:1] * next_right[0:1]
        + basis[:, 1:2] * next_right[1:2]
        - basis[:, 2:3] * next_left[0:1]
        - basis[:, 3:4] * next_left[1:2]
    )
    stepped = weight[...].astype(jnp.float32) - GOSSIP * moves
    columns = kept.shape[1]
    swapped = jnp.broadcast_to(core[0], kept.shape) == 1
    first = jnp.where(swapped, taken[...], kept[...])
    second = jnp.where(swapped, kept[...], taken[...])
    out[:, :columns] = stepped[:, :columns] - LEARN * first
    out[:, columns:] = stepped[:, columns:] - LEARN * second


def on_device(activ, grad_out, weight, q_seed):
    acts = activ[0]
    cotan = grad_out[0]
    weight_bf = weight[0]
    rows, width = weight_bf.shape
    columns = width // 2
    core, x, z = lax.axis_index("core"), lax.axis_index("xl"), lax.axis_index("z")
    own = lax.axis_index(SHARD)
    replica = lax.axis_index(CYCLE)
    cycle_size = lax.axis_size(CYCLE)

    other_acts = partner(acts, "core", 1)
    other_cotan = partner(cotan, "core", 1)
    tokens = (acts, other_acts, cotan, other_cotan)

    q_right = lax.dynamic_index_in_dim(q_seed, replica, 0, keepdims=False)
    q_left = lax.dynamic_index_in_dim(
        q_seed, (replica + cycle_size - 1) % cycle_size, 0, keepdims=False
    )
    probes = jnp.concatenate([q_right, q_left], 1).astype(jnp.bfloat16).T
    probes = jnp.pad(probes, ((0, 12), (0, 0)))
    at = own[None].astype(jnp.int32)
    part = kernel_call(probe_kernel, (probes, acts, cotan, weight_bf), f32(4, width), at)

    place = [(z + offset) % 8 for step in range(4) for offset in (4 + step, 3 - step)]
    scalars = jnp.stack(place + [1 - x, core]).astype(jnp.int32)
    mine_scalars = jnp.stack(place + [x, core]).astype(jnp.int32)
    piece = jax.ShapeDtypeStruct((2, 2 * rows, columns + LANES), jnp.int16)
    two_pieces = jax.ShapeDtypeStruct((4, 2 * rows, columns + LANES), jnp.int16)
    value = shard_sum(part, STEPS_ALONG[:1], {})

    pair = held(jnp.stack([weight_bf, partner(weight_bf, "xl", 1)], 0), (value, other_acts, other_cotan))
    weights = lax.all_gather(pair, "z", axis=0, tiled=True)

    *first, mark_0 = chunks(
        functools.partial(chunk_kernel, 0), (piece, MARK), scalars, *tokens, (value,)
    )
    value = shard_sum(value, STEPS_ALONG[1:2], {"xl1": (mark_0,)})
    first = [held(first[0], (value,))]
    second, mark_1 = chunks(
        functools.partial(chunk_kernel, 2), (piece, MARK), scalars, *tokens, (value,)
    )
    value = shard_sum(value, STEPS_ALONG[2:3], {"z1": (mark_1,)})
    last, mark_2 = chunks(
        functools.partial(chunk_kernel, 4), (two_pieces, MARK), scalars, *tokens, (value,)
    )
    from_x = [partner(sent, "xl", 1) for sent in (*first, second, last)]
    mine, mark_3 = chunks(
        mine_kernel, (f32(8, 2 * rows, columns), MARK), mine_scalars, *tokens, (mark_2,)
    )

    def hops(step, received, after):
        down, up, mark = hop(step, mine, from_x[min(step, 2)], received, after)
        return (shifted(down, "z", -1), shifted(up, "z", 1) if step < 3 else up), (mark,)

    value = shard_sum(value, STEPS_ALONG[3:4], {"z2": (mark_3,)})
    received, sent = hops(0, (), (value,))
    right, left = shard_sum(value, STEPS_ALONG[4:], {"z4": sent})
    received, sent = hops(1, received, (right,))
    back, basis = kernel_call(
        basis_kernel,
        (right, left, *neighbours(right, left), acts, cotan, weight_bf),
        (f32(4, width), f32(8, rows)),
        at,
        sent,
    )
    value = shard_sum(back, STEPS_ALONG[:1], {})
    received, sent = hops(2, received, (value,))
    value = shard_sum(value, STEPS_ALONG[1:4], {"xl1": sent})
    received, sent = hops(3, received, (value,))
    weights = held(weights, sent)
    right, left = shard_sum(value, STEPS_ALONG[4:], {"z4": sent})
    kept, given, mark = kernel_call(
        total_kernel,
        (received[1], received[0]),
        (f32(rows, columns), f32(rows, columns), MARK),
        core[None].astype(jnp.int32),
        (right,),
    )
    grad_in, mark = backward_input(
        core, x, cotan, weights, partner(weights, "core", 1), (mark,)
    )
    new_weight, next_q = kernel_call(
        update_kernel,
        (weight_bf, kept, partner(given, "core", 1), basis.T, right, left, *neighbours(right, left)),
        (f32(rows, width), f32(2, width)),
        core[None].astype(jnp.int32),
        (mark,),
    )
    return (grad_in[None], new_weight[None], next_q.T[None])


def solution(mesh):
    fine = Mesh(mesh.devices.reshape(2, 4, 2, 8, 2), CYCLE + SHARD)
    tokens = P(CYCLE, SHARD, None)
    return jax.shard_map(
        on_device,
        mesh=fine,
        in_specs=(tokens, tokens, tokens, P()),
        out_specs=(tokens, tokens, P(CYCLE, None, None)),
        check_vma=False,
    )
```

```python
import functools

import jax
import jax.numpy as jnp
from jax import lax
from jax.experimental import pallas as pl
from jax.experimental.pallas import tpu as pltpu
from jax.sharding import Mesh
from jax.sharding import PartitionSpec as P

LEARN = 0.002
GOSSIP = 0.5
EPS = 1e-06
LANES = 128
LEVELS = 64.0
STEPS = 32767.0
VMEM = 16 * 2**20
MOST_VMEM = 24 * 2**20
NO_ROOM = 56 * 2**20
MARK = jax.ShapeDtypeStruct((8, 128), jnp.float32)
NO_COST = pl.CostEstimate(flops=0, bytes_accessed=0, transcendentals=0)
STEPS_ALONG = (("core", 1), ("xl", 1), ("z", 1), ("z", 2), ("z", 4))

CYCLE = ("xh", "y")
SHARD = ("xl", "z", "core")
NT = (((1,), (1,)), ((), ()))
NN = (((1,), (0,)), ((), ()))
TN = (((0,), (0,)), ((), ()))


def dot(left, right, dims):
    return lax.dot_general(left, right, dims, preferred_element_type=jnp.float32)


def terms(value):
    high = value.astype(jnp.bfloat16)
    rest = value - high.astype(jnp.float32)
    middle = rest.astype(jnp.bfloat16)
    low = (rest - middle.astype(jnp.float32)).astype(jnp.bfloat16)
    parts = [part.astype(jnp.float32) for part in (high, middle, low)]
    return jnp.concatenate(parts, 0).astype(jnp.bfloat16)


def summed(value):
    return value[:8] + (value[8:16] + value[16:])


def thin(left, right, dims):
    return summed(dot(left, right, dims))


def own_columns(own, rows, width):
    row = lax.broadcasted_iota(jnp.int32, (rows, width), 0) + own * rows
    column = lax.broadcasted_iota(jnp.int32, (rows, width), 1)
    return jnp.where(row == column, 1.0, 0.0).astype(jnp.bfloat16)


def kernel_call(kernel, operands, out_shape, scalars=None, after=()):
    whole = pl.BlockSpec(memory_space=pltpu.VMEM)
    specs = [whole] * (len(operands) + len(after))
    first = []
    if scalars is not None:
        specs, first = [pl.BlockSpec(memory_space=pltpu.SMEM)] + specs, [scalars]
    lead, unused = len(first) + len(operands), len(after)

    def body(*refs):
        kernel(*refs[:lead], *refs[lead + unused :])

    return pl.pallas_call(
        body,
        in_specs=specs,
        out_specs=jax.tree.map(lambda _: whole, out_shape),
        out_shape=out_shape,
        cost_estimate=NO_COST,
        compiler_params=pltpu.CompilerParams(vmem_limit_bytes=VMEM),
    )(*first, *operands, *after)


def f32(*shape):
    return jax.ShapeDtypeStruct(shape, jnp.float32)


def probe_kernel(own, probes, acts, cotan, weight, out):
    rows, width = weight.shape
    from_grads = thin(terms(dot(probes[...], cotan[...], NT)[:8]), acts[...], NN)
    from_weight = terms(dot(probes[...], weight[...], NT)[:8])
    placed = thin(from_weight, own_columns(own[0], rows, width), NN)
    out[...] = (placed - LEARN * from_grads)[:4]


def unit_vectors(proj):
    first, second = proj[0:1], proj[1:2]
    unit_first = first * lax.rsqrt(jnp.sum(first * first, keepdims=True) + EPS)
    remain = second - jnp.sum(unit_first * second, keepdims=True) * unit_first
    unit_second = remain * lax.rsqrt(jnp.sum(remain * remain, keepdims=True) + EPS)
    return [unit_first, unit_second]


def basis_kernel(
    own, right, left, from_right, from_left, acts, cotan, weight, out, out_basis
):
    rows, width = weight.shape
    units = unit_vectors(right[...] - from_right[...])
    units += unit_vectors(from_left[...] - left[...])
    row = lax.broadcasted_iota(jnp.int32, (8, width), 0)
    basis = jnp.zeros((8, width), jnp.float32)
    for k, unit in enumerate(units):
        basis = jnp.where(row == k, jnp.broadcast_to(unit, (8, width)), basis)
    parts = terms(basis)
    own_parts = dot(parts, own_columns(own[0], rows, width), NT)
    out_basis[...] = summed(own_parts)
    from_weight = thin(own_parts.astype(jnp.bfloat16), weight[...], NN)
    from_grads = thin(terms(thin(parts, acts[...], NT)), cotan[...], NN)
    out[...] = (from_weight - LEARN * from_grads)[:4]


def add_kernel(left, right, out):
    out[...] = left[...] + right[...]


def add_split_kernel(left, right, out_right, out_left):
    total = left[...] + right[...]
    out_right[...] = total[:2]
    out_left[...] = total[2:]


def partner(value, axis, step):
    count = lax.axis_size(axis)
    return lax.ppermute(value, axis, [(i, i ^ step) for i in range(count)])


def shard_sum(value, steps, after):
    for axis, step in steps:
        key = axis + str(step)
        operands = (value, partner(value, axis, step))
        if key == "z4":
            halves = (f32(2, value.shape[1]), f32(2, value.shape[1]))
            value = kernel_call(add_split_kernel, operands, halves, after=after.get(key, ()))
        else:
            value = kernel_call(add_kernel, operands, f32(*value.shape), after=after.get(key, ()))
    return value


def passed_along(value, steps):
    count = lax.axis_size(CYCLE)
    return lax.ppermute(value, CYCLE, [(i, (i + steps) % count) for i in range(count)])


def neighbours(right, left):
    return passed_along(left, -1), passed_along(right, 1)


def coded(value):
    largest = jnp.maximum(jnp.max(jnp.abs(value), 1, keepdims=True), 1e-30)
    level = jnp.ceil(jnp.log2(largest) * LEVELS + 0.01)
    steps = jnp.floor(value * (STEPS * jnp.exp2(level * (-1.0 / LEVELS))) + 0.5)
    steps = jnp.clip(steps, -STEPS, STEPS).astype(jnp.int32)
    level = jnp.broadcast_to(level, (value.shape[0], LANES)).astype(jnp.int32)
    return jnp.concatenate([steps, level], 1).astype(jnp.int16)


def decoded(code):
    code = code.astype(jnp.int32).astype(jnp.float32)
    size = jnp.exp2(code[:, -1:] * (1.0 / LEVELS)) * (1.0 / STEPS)
    return code[:, :-LANES] * size


def product(place, first, count, acts, other_acts, cotan, other_cotan):
    rows = acts.shape[1] // 8

    def columns(ref):
        return jnp.concatenate(
            [ref[:, pl.ds(pl.multiple_of(place[first + k] * rows, rows), rows)] for k in range(count)], 1
        )

    return dot(columns(acts), cotan[...], TN) + dot(columns(other_acts), other_cotan[...], TN)


def chunk_kernel(first, place, acts, other_acts, cotan, other_cotan, *outs):
    rows = acts.shape[1] // 8
    outs, mark = outs[:-1], outs[-1]
    mark[...] = jnp.zeros_like(mark)
    for out in outs:
        count = out.shape[0]
        value = product(place, first, count, acts, other_acts, cotan, other_cotan)
        for k in range(count):
            out[k] = coded(value[k * rows : (k + 1) * rows])
        first += count


def mine_kernel(place, acts, other_acts, cotan, other_cotan, out, mark):
    rows = acts.shape[1] // 8
    mark[...] = jnp.zeros_like(mark)
    for k in range(2):
        value = product(place, 4 * k, 4, acts, other_acts, cotan, other_cotan)
        for j in range(4):
            out[4 * k + j] = value[rows * j : rows * (j + 1)]


def chunks(kernel, out_shape, scalars, acts, other_acts, cotan, other_cotan, after):
    tokens, width = acts.shape
    half = width // 2
    unused = len(after)

    def body(place, *refs):
        kernel(place, *refs[:4], *refs[4 + unused :])

    def spec(shape):
        return pl.BlockSpec(shape, lambda i, at: (0,) * len(shape))

    return pl.pallas_call(
        body,
        grid_spec=pltpu.PrefetchScalarGridSpec(
            num_scalar_prefetch=1,
            grid=(1,),
            in_specs=[
                pl.BlockSpec((tokens, half), lambda i, at: (0, at[8])),
                pl.BlockSpec((tokens, half), lambda i, at: (0, at[8])),
                pl.BlockSpec((tokens, half), lambda i, at: (0, at[9])),
                pl.BlockSpec((tokens, half), lambda i, at: (0, at[9])),
            ]
            + [pl.BlockSpec(memory_space=pltpu.VMEM)] * unused,
            out_specs=jax.tree.map(lambda a: spec(a.shape), out_shape),
        ),
        out_shape=out_shape,
        cost_estimate=NO_COST,
        compiler_params=pltpu.CompilerParams(vmem_limit_bytes=MOST_VMEM),
    )(scalars, acts, other_acts, cotan, other_cotan, *after)


def hop_kernel(step, unused, *refs):
    mine, from_x = refs[:2]
    down = mine[0] + decoded(from_x[0])
    up = mine[1] + decoded(from_x[1])
    if step > 0:
        down = down + decoded(refs[2][...])
        up = up + decoded(refs[3][...])
    refs[-3][...] = coded(down)
    refs[-2][...] = up if step == 3 else coded(up)
    refs[-1][...] = jnp.zeros_like(refs[-1])


def hop(step, mine, from_x, received, after):
    _, rows, columns = mine.shape
    wide = columns + LANES
    whole = pl.BlockSpec((rows, wide), lambda i: (0, 0))
    sent = jax.ShapeDtypeStruct((rows, wide), jnp.int16)
    last = jax.ShapeDtypeStruct((rows, columns), jnp.float32) if step == 3 else sent
    return pl.pallas_call(
        functools.partial(hop_kernel, step, len(after)),
        grid=(1,),
        in_specs=[
            pl.BlockSpec((2, rows, columns), lambda i: (step, 0, 0)),
            pl.BlockSpec((2, rows, wide), lambda i: (step % 2, 0, 0)),
        ]
        + [whole] * len(received)
        + [pl.BlockSpec(memory_space=pltpu.VMEM)] * len(after),
        out_specs=[whole] + [pl.BlockSpec(a.shape, lambda i: (0, 0)) for a in (last, MARK)],
        out_shape=[sent, last, MARK],
        cost_estimate=NO_COST,
        compiler_params=pltpu.CompilerParams(vmem_limit_bytes=VMEM),
    )(mine, from_x, *received, *after)


def total_kernel(core, up, down, kept, given, mark):
    total = up[...] + decoded(down[...])
    mark[...] = jnp.zeros_like(mark)
    rows = kept.shape[0]
    mine = jnp.where(core[0] == 0, 1.0, 0.0)
    kept[...] = jnp.where(mine > 0.5, total[:rows], total[rows:])
    given[...] = jnp.where(mine > 0.5, total[rows:], total[:rows])


def shifted(value, axis, steps):
    count = lax.axis_size(axis)
    return lax.ppermute(value, axis, [(i, (i + steps) % count) for i in range(count)])


def held(value, after, arrays=(), limit=VMEM):
    def body(*refs):
        pass

    anywhere = pl.BlockSpec(memory_space=pl.ANY)
    return pl.pallas_call(
        body,
        in_specs=[anywhere] * (1 + len(arrays))
        + [pl.BlockSpec(memory_space=pltpu.VMEM)] * len(after),
        out_specs=anywhere,
        out_shape=jax.ShapeDtypeStruct(value.shape, value.dtype),
        input_output_aliases={0: 0},
        cost_estimate=NO_COST,
        compiler_params=pltpu.CompilerParams(vmem_limit_bytes=limit),
    )(value, *arrays, *after)


def input_kernel(unused, at, cotan, weights, other_weights, *refs):
    out, mark = refs[unused:]
    mark[...] = jnp.zeros_like(mark)
    core, x, z = at[0], at[1], pl.program_id(0)
    wide = 2 * weights.shape[1]

    def planes(first, second):
        blocks = [first[0], second[0], first[1], second[1]]
        value = dot(cotan[...], jnp.concatenate(blocks, 0), NT).astype(jnp.bfloat16)
        for column in range(2):
            chip = (x * (1 - column) + (1 - x) * column) * 8 + z
            place = pl.ds(pl.multiple_of(chip * wide, wide), wide)
            out[:, place] = value[:, column * wide : (column + 1) * wide]

    @pl.when(core == 0)
    def _():
        planes(weights, other_weights)

    @pl.when(core == 1)
    def _():
        planes(other_weights, weights)


def backward_input(core, x, cotan, weights, other_weights, after):
    tokens, width = cotan.shape
    rows = weights.shape[1]
    plane = pl.BlockSpec((2, rows, width), lambda i, at: (i, 0, 0))
    return pl.pallas_call(
        functools.partial(input_kernel, len(after)),
        grid_spec=pltpu.PrefetchScalarGridSpec(
            num_scalar_prefetch=1,
            grid=(8,),
            in_specs=[pl.BlockSpec((tokens, width), lambda i, at: (0, 0)), plane, plane]
            + [pl.BlockSpec(memory_space=pltpu.VMEM)] * len(after),
            out_specs=[
                pl.BlockSpec((tokens, width), lambda i, at: (0, 0)),
                pl.BlockSpec(MARK.shape, lambda i, at: (0, 0)),
            ],
        ),
        out_shape=[jax.ShapeDtypeStruct((tokens, width), jnp.bfloat16), MARK],
        cost_estimate=NO_COST,
        compiler_params=pltpu.CompilerParams(vmem_limit_bytes=NO_ROOM),
    )(jnp.stack([core, x]).astype(jnp.int32), cotan, weights, other_weights, *after)


def update_kernel(core, weight, kept, taken, basis, right, left, from_right, from_left, out, out_q):
    next_right = right[...] - from_right[...]
    next_left = from_left[...] - left[...]
    out_q[...] = next_right
    moves = (
        basis[:, 0:1] * next_right[0:1]
        + basis[:, 1:2] * next_right[1:2]
        - basis[:, 2:3] * next_left[0:1]
        - basis[:, 3:4] * next_left[1:2]
    )
    stepped = weight[...].astype(jnp.float32) - GOSSIP * moves
    columns = kept.shape[1]
    swapped = jnp.broadcast_to(core[0], kept.shape) == 1
    first = jnp.where(swapped, taken[...], kept[...])
    second = jnp.where(swapped, kept[...], taken[...])
    out[:, :columns] = stepped[:, :columns] - LEARN * first
    out[:, columns:] = stepped[:, columns:] - LEARN * second


def on_device(activ, grad_out, weight, q_seed):
    acts = activ[0]
    cotan = grad_out[0]
    weight_bf = weight[0]
    rows, width = weight_bf.shape
    columns = width // 2
    core, x, z = lax.axis_index("core"), lax.axis_index("xl"), lax.axis_index("z")
    own = lax.axis_index(SHARD)
    replica = lax.axis_index(CYCLE)
    cycle_size = lax.axis_size(CYCLE)

    other_acts = partner(acts, "core", 1)
    other_cotan = partner(cotan, "core", 1)
    tokens = (acts, other_acts, cotan, other_cotan)

    q_right = lax.dynamic_index_in_dim(q_seed, replica, 0, keepdims=False)
    q_left = lax.dynamic_index_in_dim(
        q_seed, (replica + cycle_size - 1) % cycle_size, 0, keepdims=False
    )
    probes = jnp.concatenate([q_right, q_left], 1).astype(jnp.bfloat16).T
    probes = jnp.pad(probes, ((0, 12), (0, 0)))
    at = own[None].astype(jnp.int32)
    part = kernel_call(probe_kernel, (probes, acts, cotan, weight_bf), f32(4, width), at)

    place = [(z + offset) % 8 for step in range(4) for offset in (4 + step, 3 - step)]
    scalars = jnp.stack(place + [1 - x, core]).astype(jnp.int32)
    mine_scalars = jnp.stack(place + [x, core]).astype(jnp.int32)
    pieces = jax.ShapeDtypeStruct((4, 2 * rows, columns + LANES), jnp.int16)
    value = shard_sum(part, STEPS_ALONG[:1], {})

    pair = held(
        jnp.stack([weight_bf, partner(weight_bf, "xl", 1)], 0), (value,), (other_acts, other_cotan)
    )
    weights = lax.all_gather(pair, "z", axis=0, tiled=True)

    first, mark = chunks(
        functools.partial(chunk_kernel, 0), (pieces, MARK), scalars, *tokens, (value,)
    )
    value = shard_sum(value, STEPS_ALONG[1:2], {"xl1": (mark,)})
    first = held(first, (value,))
    second, mark = chunks(
        functools.partial(chunk_kernel, 4), (pieces, MARK), scalars, *tokens, (value,)
    )
    from_x = [partner(sent, "xl", 1) for sent in (first, second)]
    value = shard_sum(value, STEPS_ALONG[2:3], {"z1": (mark,)})
    mine, mark = chunks(
        mine_kernel, (f32(8, 2 * rows, columns), MARK), mine_scalars, *tokens, (value,)
    )

    def hops(step, received, after):
        down, up, mark = hop(step, mine, from_x[step // 2], received, after)
        return (shifted(down, "z", -1), shifted(up, "z", 1) if step < 3 else up), (mark,)

    right, left = shard_sum(value, STEPS_ALONG[3:], {"z2": (mark,)})
    arrived = neighbours(right, left)
    received, sent = hops(0, (), arrived)
    back, basis = kernel_call(
        basis_kernel,
        (right, left, *arrived, acts, cotan, weight_bf),
        (f32(4, width), f32(8, rows)),
        at,
        sent,
    )
    value = shard_sum(back, STEPS_ALONG[:3], {})
    received, sent = hops(1, received, (value,))
    right, left = shard_sum(value, STEPS_ALONG[3:], {"z2": sent})
    received, sent = hops(2, received, (right,))
    weights = held(weights, sent, (), NO_ROOM)
    arrived = neighbours(right, left)
    received, sent = hops(3, received, arrived)
    grad_in, mark = backward_input(core, x, cotan, weights, partner(weights, "core", 1), sent)
    kept, given, _ = kernel_call(
        total_kernel,
        (received[1], received[0]),
        (f32(rows, columns), f32(rows, columns), MARK),
        core[None].astype(jnp.int32),
        (mark,),
    )
    new_weight, next_q = kernel_call(
        update_kernel,
        (weight_bf, kept, partner(given, "core", 1), basis.T, right, left, *arrived),
        (f32(rows, width), f32(2, width)),
        core[None].astype(jnp.int32),
        (mark,),
    )
    return (grad_in[None], new_weight[None], next_q.T[None])


def solution(mesh):
    fine = Mesh(mesh.devices.reshape(2, 4, 2, 8, 2), CYCLE + SHARD)
    tokens = P(CYCLE, SHARD, None)
    return jax.shard_map(
        on_device,
        mesh=fine,
        in_specs=(tokens, tokens, tokens, P()),
        out_specs=(tokens, tokens, P(CYCLE, None, None)),
        check_vma=False,
    )
```

```python
import functools

import jax
import jax.numpy as jnp
from jax import lax
from jax.experimental import pallas as pl
from jax.experimental.pallas import tpu as pltpu
from jax.sharding import Mesh
from jax.sharding import PartitionSpec as P

LEARN = 0.002
GOSSIP = 0.5
EPS = 1e-06
LANES = 128
LEVELS = 64.0
STEPS = 32767.0
VMEM = 16 * 2**20
MOST_VMEM = 24 * 2**20
NO_ROOM = 56 * 2**20
MARK = jax.ShapeDtypeStruct((8, 128), jnp.float32)
NO_COST = pl.CostEstimate(flops=0, bytes_accessed=0, transcendentals=0)
STEPS_BACK = (("core", 1), ("z", 1), ("z", 2), ("z", 4), ("xl", 1))
STEPS_ALONG = (("core", 1), ("xl", 1), ("z", 1), ("z", 2), ("z", 4))

CYCLE = ("xh", "y")
SHARD = ("xl", "z", "core")
NT = (((1,), (1,)), ((), ()))
NN = (((1,), (0,)), ((), ()))
TN = (((0,), (0,)), ((), ()))


def dot(left, right, dims):
    return lax.dot_general(left, right, dims, preferred_element_type=jnp.float32)


def terms(value):
    high = value.astype(jnp.bfloat16)
    rest = value - high.astype(jnp.float32)
    middle = rest.astype(jnp.bfloat16)
    low = (rest - middle.astype(jnp.float32)).astype(jnp.bfloat16)
    parts = [part.astype(jnp.float32) for part in (high, middle, low)]
    return jnp.concatenate(parts, 0).astype(jnp.bfloat16)


def summed(value):
    return value[:8] + (value[8:16] + value[16:])


def thin(left, right, dims):
    return summed(dot(left, right, dims))


def own_columns(own, rows, width):
    row = lax.broadcasted_iota(jnp.int32, (rows, width), 0) + own * rows
    column = lax.broadcasted_iota(jnp.int32, (rows, width), 1)
    return jnp.where(row == column, 1.0, 0.0).astype(jnp.bfloat16)


def kernel_call(kernel, operands, out_shape, scalars=None, after=()):
    whole = pl.BlockSpec(memory_space=pltpu.VMEM)
    specs = [whole] * (len(operands) + len(after))
    first = []
    if scalars is not None:
        specs, first = [pl.BlockSpec(memory_space=pltpu.SMEM)] + specs, [scalars]
    lead, unused = len(first) + len(operands), len(after)

    def body(*refs):
        kernel(*refs[:lead], *refs[lead + unused :])

    return pl.pallas_call(
        body,
        in_specs=specs,
        out_specs=jax.tree.map(lambda _: whole, out_shape),
        out_shape=out_shape,
        cost_estimate=NO_COST,
        compiler_params=pltpu.CompilerParams(vmem_limit_bytes=VMEM),
    )(*first, *operands, *after)


def f32(*shape):
    return jax.ShapeDtypeStruct(shape, jnp.float32)


def probe_kernel(own, probes, acts, cotan, weight, out):
    rows, width = weight.shape
    from_grads = thin(terms(dot(probes[...], cotan[...], NT)[:8]), acts[...], NN)
    from_weight = terms(dot(probes[...], weight[...], NT)[:8])
    placed = thin(from_weight, own_columns(own[0], rows, width), NN)
    out[...] = (placed - LEARN * from_grads)[:4]


def unit_vectors(proj):
    first, second = proj[0:1], proj[1:2]
    unit_first = first * lax.rsqrt(jnp.sum(first * first, keepdims=True) + EPS)
    remain = second - jnp.sum(unit_first * second, keepdims=True) * unit_first
    unit_second = remain * lax.rsqrt(jnp.sum(remain * remain, keepdims=True) + EPS)
    return [unit_first, unit_second]


def basis_kernel(
    own, right, left, from_right, from_left, acts, cotan, weight, out, out_basis
):
    rows, width = weight.shape
    units = unit_vectors(right[...] - from_right[...])
    units += unit_vectors(from_left[...] - left[...])
    row = lax.broadcasted_iota(jnp.int32, (8, width), 0)
    basis = jnp.zeros((8, width), jnp.float32)
    for k, unit in enumerate(units):
        basis = jnp.where(row == k, jnp.broadcast_to(unit, (8, width)), basis)
    parts = terms(basis)
    own_parts = dot(parts, own_columns(own[0], rows, width), NT)
    out_basis[...] = summed(own_parts)
    from_weight = thin(own_parts.astype(jnp.bfloat16), weight[...], NN)
    from_grads = thin(terms(thin(parts, acts[...], NT)), cotan[...], NN)
    out[...] = (from_weight - LEARN * from_grads)[:4]


def add_kernel(left, right, out):
    out[...] = left[...] + right[...]


def add_split_kernel(left, right, out_right, out_left):
    total = left[...] + right[...]
    out_right[...] = total[:2]
    out_left[...] = total[2:]


def partner(value, axis, step):
    count = lax.axis_size(axis)
    return lax.ppermute(value, axis, [(i, i ^ step) for i in range(count)])


def shard_sum(value, steps, after, split=None):
    for axis, step in steps:
        key = axis + str(step)
        operands = (value, partner(value, axis, step))
        if key == split:
            halves = (f32(2, value.shape[1]), f32(2, value.shape[1]))
            value = kernel_call(add_split_kernel, operands, halves, after=after.get(key, ()))
        else:
            value = kernel_call(add_kernel, operands, f32(*value.shape), after=after.get(key, ()))
    return value


def passed_along(value, steps):
    count, row = lax.axis_size(CYCLE), lax.axis_size("y")
    pairs = []
    for source in range(count):
        target = (source + steps) % count
        crossed = int(source // row != target // row)
        pairs += [(2 * source + x, 2 * target + (x ^ crossed)) for x in range(2)]
    return lax.ppermute(value, CYCLE + ("xl",), pairs)


def neighbours(right, left):
    return passed_along(left, -1), passed_along(right, 1)


def coded(value):
    largest = jnp.maximum(jnp.max(jnp.abs(value), 1, keepdims=True), 1e-30)
    level = jnp.ceil(jnp.log2(largest) * LEVELS + 0.01)
    steps = jnp.floor(value * (STEPS * jnp.exp2(level * (-1.0 / LEVELS))) + 0.5)
    steps = jnp.clip(steps, -STEPS, STEPS).astype(jnp.int32)
    level = jnp.broadcast_to(level, (value.shape[0], LANES)).astype(jnp.int32)
    return jnp.concatenate([steps, level], 1).astype(jnp.int16)


def decoded(code):
    code = code.astype(jnp.int32).astype(jnp.float32)
    size = jnp.exp2(code[:, -1:] * (1.0 / LEVELS)) * (1.0 / STEPS)
    return code[:, :-LANES] * size


def product(place, first, count, acts, other_acts, cotan, other_cotan):
    rows = acts.shape[1] // 8

    def columns(ref):
        return jnp.concatenate(
            [ref[:, pl.ds(pl.multiple_of(place[first + k] * rows, rows), rows)] for k in range(count)], 1
        )

    return dot(columns(acts), cotan[...], TN) + dot(columns(other_acts), other_cotan[...], TN)


def chunk_kernel(first, place, acts, other_acts, cotan, other_cotan, *outs):
    rows = acts.shape[1] // 8
    outs, mark = outs[:-1], outs[-1]
    mark[...] = jnp.zeros_like(mark)
    for out in outs:
        count = out.shape[0]
        value = product(place, first, count, acts, other_acts, cotan, other_cotan)
        for k in range(count):
            out[k] = coded(value[k * rows : (k + 1) * rows])
        first += count


def mine_kernel(place, acts, other_acts, cotan, other_cotan, out, mark):
    rows = acts.shape[1] // 8
    mark[...] = jnp.zeros_like(mark)
    for k in range(2):
        value = product(place, 4 * k, 4, acts, other_acts, cotan, other_cotan)
        for j in range(4):
            out[4 * k + j] = value[rows * j : rows * (j + 1)]


def chunks(kernel, out_shape, scalars, acts, other_acts, cotan, other_cotan, after):
    tokens, width = acts.shape
    half = width // 2
    unused = len(after)

    def body(place, *refs):
        kernel(place, *refs[:4], *refs[4 + unused :])

    def spec(shape):
        return pl.BlockSpec(shape, lambda i, at: (0,) * len(shape))

    return pl.pallas_call(
        body,
        grid_spec=pltpu.PrefetchScalarGridSpec(
            num_scalar_prefetch=1,
            grid=(1,),
            in_specs=[
                pl.BlockSpec((tokens, half), lambda i, at: (0, at[8])),
                pl.BlockSpec((tokens, half), lambda i, at: (0, at[8])),
                pl.BlockSpec((tokens, half), lambda i, at: (0, at[9])),
                pl.BlockSpec((tokens, half), lambda i, at: (0, at[9])),
            ]
            + [pl.BlockSpec(memory_space=pltpu.VMEM)] * unused,
            out_specs=jax.tree.map(lambda a: spec(a.shape), out_shape),
        ),
        out_shape=out_shape,
        cost_estimate=NO_COST,
        compiler_params=pltpu.CompilerParams(vmem_limit_bytes=MOST_VMEM),
    )(scalars, acts, other_acts, cotan, other_cotan, *after)


def hop_kernel(step, unused, *refs):
    mine, from_x = refs[:2]
    down = mine[0] + decoded(from_x[0])
    up = mine[1] + decoded(from_x[1])
    if step > 0:
        down = down + decoded(refs[2][...])
        up = up + decoded(refs[3][...])
    refs[-3][...] = coded(down)
    refs[-2][...] = up if step == 3 else coded(up)
    refs[-1][...] = jnp.zeros_like(refs[-1])


def hop(step, mine, from_x, received, after):
    _, rows, columns = mine.shape
    wide = columns + LANES
    whole = pl.BlockSpec((rows, wide), lambda i: (0, 0))
    sent = jax.ShapeDtypeStruct((rows, wide), jnp.int16)
    last = jax.ShapeDtypeStruct((rows, columns), jnp.float32) if step == 3 else sent
    return pl.pallas_call(
        functools.partial(hop_kernel, step, len(after)),
        grid=(1,),
        in_specs=[
            pl.BlockSpec((2, rows, columns), lambda i: (step, 0, 0)),
            pl.BlockSpec((2, rows, wide), lambda i: (step % 2, 0, 0)),
        ]
        + [whole] * len(received)
        + [pl.BlockSpec(memory_space=pltpu.VMEM)] * len(after),
        out_specs=[whole] + [pl.BlockSpec(a.shape, lambda i: (0, 0)) for a in (last, MARK)],
        out_shape=[sent, last, MARK],
        cost_estimate=NO_COST,
        compiler_params=pltpu.CompilerParams(vmem_limit_bytes=VMEM),
    )(mine, from_x, *received, *after)


def total_kernel(core, up, down, kept, given, mark):
    total = up[...] + decoded(down[...])
    mark[...] = jnp.zeros_like(mark)
    rows = kept.shape[0]
    mine = jnp.where(core[0] == 0, 1.0, 0.0)
    kept[...] = jnp.where(mine > 0.5, total[:rows], total[rows:])
    given[...] = jnp.where(mine > 0.5, total[rows:], total[:rows])


def shifted(value, axis, steps):
    count = lax.axis_size(axis)
    return lax.ppermute(value, axis, [(i, (i + steps) % count) for i in range(count)])


def held(value, after, arrays=(), limit=VMEM):
    def body(*refs):
        pass

    anywhere = pl.BlockSpec(memory_space=pl.ANY)
    return pl.pallas_call(
        body,
        in_specs=[anywhere] * (1 + len(arrays))
        + [pl.BlockSpec(memory_space=pltpu.VMEM)] * len(after),
        out_specs=anywhere,
        out_shape=jax.ShapeDtypeStruct(value.shape, value.dtype),
        input_output_aliases={0: 0},
        cost_estimate=NO_COST,
        compiler_params=pltpu.CompilerParams(vmem_limit_bytes=limit),
    )(value, *arrays, *after)


def input_kernel(unused, at, cotan, weights, other_weights, *refs):
    out, mark = refs[unused:]
    mark[...] = jnp.zeros_like(mark)
    core, x, z = at[0], at[1], pl.program_id(0)
    wide = 2 * weights.shape[1]

    def planes(first, second):
        blocks = [first[0], second[0], first[1], second[1]]
        value = dot(cotan[...], jnp.concatenate(blocks, 0), NT).astype(jnp.bfloat16)
        for column in range(2):
            chip = (x * (1 - column) + (1 - x) * column) * 8 + z
            place = pl.ds(pl.multiple_of(chip * wide, wide), wide)
            out[:, place] = value[:, column * wide : (column + 1) * wide]

    @pl.when(core == 0)
    def _():
        planes(weights, other_weights)

    @pl.when(core == 1)
    def _():
        planes(other_weights, weights)


def backward_input(core, x, cotan, weights, other_weights, after):
    tokens, width = cotan.shape
    rows = weights.shape[1]
    plane = pl.BlockSpec((2, rows, width), lambda i, at: (i, 0, 0))
    return pl.pallas_call(
        functools.partial(input_kernel, len(after)),
        grid_spec=pltpu.PrefetchScalarGridSpec(
            num_scalar_prefetch=1,
            grid=(8,),
            in_specs=[pl.BlockSpec((tokens, width), lambda i, at: (0, 0)), plane, plane]
            + [pl.BlockSpec(memory_space=pltpu.VMEM)] * len(after),
            out_specs=[
                pl.BlockSpec((tokens, width), lambda i, at: (0, 0)),
                pl.BlockSpec(MARK.shape, lambda i, at: (0, 0)),
            ],
        ),
        out_shape=[jax.ShapeDtypeStruct((tokens, width), jnp.bfloat16), MARK],
        cost_estimate=NO_COST,
        compiler_params=pltpu.CompilerParams(vmem_limit_bytes=NO_ROOM),
    )(jnp.stack([core, x]).astype(jnp.int32), cotan, weights, other_weights, *after)


def update_kernel(core, weight, kept, taken, basis, right, left, from_right, from_left, out, out_q):
    next_right = right[...] - from_right[...]
    next_left = from_left[...] - left[...]
    out_q[...] = next_right
    moves = (
        basis[:, 0:1] * next_right[0:1]
        + basis[:, 1:2] * next_right[1:2]
        - basis[:, 2:3] * next_left[0:1]
        - basis[:, 3:4] * next_left[1:2]
    )
    stepped = weight[...].astype(jnp.float32) - GOSSIP * moves
    columns = kept.shape[1]
    swapped = jnp.broadcast_to(core[0], kept.shape) == 1
    first = jnp.where(swapped, taken[...], kept[...])
    second = jnp.where(swapped, kept[...], taken[...])
    out[:, :columns] = stepped[:, :columns] - LEARN * first
    out[:, columns:] = stepped[:, columns:] - LEARN * second


def on_device(activ, grad_out, weight, q_seed):
    acts = activ[0]
    cotan = grad_out[0]
    weight_bf = weight[0]
    rows, width = weight_bf.shape
    columns = width // 2
    core, x, z = lax.axis_index("core"), lax.axis_index("xl"), lax.axis_index("z")
    own = lax.axis_index(SHARD)
    replica = lax.axis_index(CYCLE)
    cycle_size = lax.axis_size(CYCLE)

    other_acts = partner(acts, "core", 1)
    other_cotan = partner(cotan, "core", 1)
    tokens = (acts, other_acts, cotan, other_cotan)

    q_right = lax.dynamic_index_in_dim(q_seed, replica, 0, keepdims=False)
    q_left = lax.dynamic_index_in_dim(
        q_seed, (replica + cycle_size - 1) % cycle_size, 0, keepdims=False
    )
    probes = jnp.concatenate([q_right, q_left], 1).astype(jnp.bfloat16).T
    probes = jnp.pad(probes, ((0, 12), (0, 0)))
    at = own[None].astype(jnp.int32)
    part = kernel_call(probe_kernel, (probes, acts, cotan, weight_bf), f32(4, width), at)

    place = [(z + offset) % 8 for step in range(4) for offset in (4 + step, 3 - step)]
    scalars = jnp.stack(place + [1 - x, core]).astype(jnp.int32)
    mine_scalars = jnp.stack(place + [x, core]).astype(jnp.int32)
    pieces = jax.ShapeDtypeStruct((4, 2 * rows, columns + LANES), jnp.int16)
    value = shard_sum(part, STEPS_ALONG[:1], {})

    pair = held(
        jnp.stack([weight_bf, partner(weight_bf, "xl", 1)], 0), (value,), (other_acts, other_cotan)
    )
    weights = lax.all_gather(pair, "z", axis=0, tiled=True)

    first, mark = chunks(
        functools.partial(chunk_kernel, 0), (pieces, MARK), scalars, *tokens, (value,)
    )
    value = shard_sum(value, STEPS_ALONG[1:2], {"xl1": (mark,)})
    first = held(first, (value,))
    value = shard_sum(value, STEPS_ALONG[2:3], {})
    mine, mark = chunks(
        mine_kernel, (f32(8, 2 * rows, columns), MARK), mine_scalars, *tokens, (value,)
    )

    def hops(step, received, after, from_x):
        down, up, mark = hop(step, mine, from_x, received, after)
        return (shifted(down, "z", -1), shifted(up, "z", 1) if step < 3 else up), (mark,)

    right, left = shard_sum(value, STEPS_ALONG[3:], {"z2": (mark,)}, "z4")
    arrived = neighbours(right, left)
    second, mark = chunks(
        functools.partial(chunk_kernel, 4), (pieces, MARK), scalars, *tokens, (right,)
    )
    from_x = partner(first, "xl", 1)
    received, sent = hops(0, (), (*arrived, mark), from_x)
    second = held(second, sent)
    back, basis = kernel_call(
        basis_kernel,
        (right, left, *arrived, acts, cotan, weight_bf),
        (f32(4, width), f32(8, rows)),
        at,
        sent,
    )
    value = shard_sum(back, STEPS_BACK[:2], {})
    received, sent = hops(1, received, (value,), from_x)
    right, left = shard_sum(value, STEPS_BACK[2:], {"z2": sent}, "xl1")
    from_x = partner(second, "xl", 1)
    received, sent = hops(2, received, (right,), from_x)
    weights = held(weights, sent, (), NO_ROOM)
    arrived = neighbours(right, left)
    received, sent = hops(3, received, arrived, from_x)
    grad_in, mark = backward_input(core, x, cotan, weights, partner(weights, "core", 1), sent)
    kept, given, _ = kernel_call(
        total_kernel,
        (received[1], received[0]),
        (f32(rows, columns), f32(rows, columns), MARK),
        core[None].astype(jnp.int32),
        (mark,),
    )
    new_weight, next_q = kernel_call(
        update_kernel,
        (weight_bf, kept, partner(given, "core", 1), basis.T, right, left, *arrived),
        (f32(rows, width), f32(2, width)),
        core[None].astype(jnp.int32),
        (mark,),
    )
    return (grad_in[None], new_weight[None], next_q.T[None])


def solution(mesh):
    fine = Mesh(mesh.devices.reshape(2, 4, 2, 8, 2), CYCLE + SHARD)
    tokens = P(CYCLE, SHARD, None)
    return jax.shard_map(
        on_device,
        mesh=fine,
        in_specs=(tokens, tokens, tokens, P()),
        out_specs=(tokens, tokens, P(CYCLE, None, None)),
        check_vma=False,
    )
```

```python
import functools

import jax
import jax.numpy as jnp
from jax import lax
from jax.experimental import pallas as pl
from jax.experimental.pallas import tpu as pltpu
from jax.sharding import Mesh
from jax.sharding import PartitionSpec as P

LEARN = 0.002
GOSSIP = 0.5
EPS = 1e-06
LANES = 128
LEVELS = 64.0
STEPS = 32767.0
VMEM = 16 * 2**20
MOST_VMEM = 24 * 2**20
NO_ROOM = 56 * 2**20
MARK = jax.ShapeDtypeStruct((8, 128), jnp.float32)
NO_COST = pl.CostEstimate(flops=0, bytes_accessed=0, transcendentals=0)
STEPS_BACK = (("core", 1), ("z", 1), ("z", 2), ("z", 4), ("xl", 1))
STEPS_ALONG = (("core", 1), ("xl", 1), ("z", 1), ("z", 2), ("z", 4))

CYCLE = ("xh", "y")
SHARD = ("xl", "z", "core")
NT = (((1,), (1,)), ((), ()))
NN = (((1,), (0,)), ((), ()))
TN = (((0,), (0,)), ((), ()))


def dot(left, right, dims):
    return lax.dot_general(left, right, dims, preferred_element_type=jnp.float32)


def terms(value):
    high = value.astype(jnp.bfloat16)
    rest = value - high.astype(jnp.float32)
    middle = rest.astype(jnp.bfloat16)
    low = (rest - middle.astype(jnp.float32)).astype(jnp.bfloat16)
    parts = [part.astype(jnp.float32) for part in (high, middle, low)]
    return jnp.concatenate(parts, 0).astype(jnp.bfloat16)


def summed(value):
    return value[:8] + (value[8:16] + value[16:])


def thin(left, right, dims):
    return summed(dot(left, right, dims))


def own_columns(own, rows, width):
    row = lax.broadcasted_iota(jnp.int32, (rows, width), 0) + own * rows
    column = lax.broadcasted_iota(jnp.int32, (rows, width), 1)
    return jnp.where(row == column, 1.0, 0.0).astype(jnp.bfloat16)


def kernel_call(kernel, operands, out_shape, scalars=None, after=()):
    whole = pl.BlockSpec(memory_space=pltpu.VMEM)
    specs = [whole] * (len(operands) + len(after))
    first = []
    if scalars is not None:
        specs, first = [pl.BlockSpec(memory_space=pltpu.SMEM)] + specs, [scalars]
    lead, unused = len(first) + len(operands), len(after)

    def body(*refs):
        kernel(*refs[:lead], *refs[lead + unused :])

    return pl.pallas_call(
        body,
        in_specs=specs,
        out_specs=jax.tree.map(lambda _: whole, out_shape),
        out_shape=out_shape,
        cost_estimate=NO_COST,
        compiler_params=pltpu.CompilerParams(vmem_limit_bytes=VMEM),
    )(*first, *operands, *after)


def f32(*shape):
    return jax.ShapeDtypeStruct(shape, jnp.float32)


def probe_kernel(own, probes, acts, cotan, weight, out):
    rows, width = weight.shape
    from_grads = thin(terms(dot(probes[...], cotan[...], NT)[:8]), acts[...], NN)
    from_weight = terms(dot(probes[...], weight[...], NT)[:8])
    placed = thin(from_weight, own_columns(own[0], rows, width), NN)
    out[...] = (placed - LEARN * from_grads)[:4]


def unit_vectors(proj):
    first, second = proj[0:1], proj[1:2]
    unit_first = first * lax.rsqrt(jnp.sum(first * first, keepdims=True) + EPS)
    remain = second - jnp.sum(unit_first * second, keepdims=True) * unit_first
    unit_second = remain * lax.rsqrt(jnp.sum(remain * remain, keepdims=True) + EPS)
    return [unit_first, unit_second]


def basis_kernel(
    own, right, left, from_right, from_left, acts, cotan, weight, out, out_basis
):
    rows, width = weight.shape
    units = unit_vectors(right[...] - from_right[...])
    units += unit_vectors(from_left[...] - left[...])
    row = lax.broadcasted_iota(jnp.int32, (8, width), 0)
    basis = jnp.zeros((8, width), jnp.float32)
    for k, unit in enumerate(units):
        basis = jnp.where(row == k, jnp.broadcast_to(unit, (8, width)), basis)
    parts = terms(basis)
    own_parts = dot(parts, own_columns(own[0], rows, width), NT)
    out_basis[...] = summed(own_parts)
    from_weight = thin(own_parts.astype(jnp.bfloat16), weight[...], NN)
    from_grads = thin(terms(thin(parts, acts[...], NT)), cotan[...], NN)
    out[...] = (from_weight - LEARN * from_grads)[:4]


def add_kernel(left, right, out):
    out[...] = left[...] + right[...]


def add_split_kernel(left, right, out_right, out_left):
    total = left[...] + right[...]
    out_right[...] = total[:2]
    out_left[...] = total[2:]


def partner(value, axis, step):
    count = lax.axis_size(axis)
    return lax.ppermute(value, axis, [(i, i ^ step) for i in range(count)])


def shard_sum(value, steps, after, split=None):
    for axis, step in steps:
        key = axis + str(step)
        operands = (value, partner(value, axis, step))
        if key == split:
            halves = (f32(2, value.shape[1]), f32(2, value.shape[1]))
            value = kernel_call(add_split_kernel, operands, halves, after=after.get(key, ()))
        else:
            value = kernel_call(add_kernel, operands, f32(*value.shape), after=after.get(key, ()))
    return value


def passed_along(value, steps):
    count, row = lax.axis_size(CYCLE), lax.axis_size("y")
    pairs = []
    for source in range(count):
        target = (source + steps) % count
        crossed = int(source // row != target // row)
        pairs += [(2 * source + x, 2 * target + (x ^ crossed)) for x in range(2)]
    return lax.ppermute(value, CYCLE + ("xl",), pairs)


def neighbours(right, left):
    return passed_along(left, -1), passed_along(right, 1)


def coded(value):
    largest = jnp.maximum(jnp.max(jnp.abs(value), 1, keepdims=True), 1e-30)
    level = jnp.ceil(jnp.log2(largest) * LEVELS + 0.01)
    steps = jnp.floor(value * (STEPS * jnp.exp2(level * (-1.0 / LEVELS))) + 0.5)
    steps = jnp.clip(steps, -STEPS, STEPS).astype(jnp.int32)
    level = jnp.broadcast_to(level, (value.shape[0], LANES)).astype(jnp.int32)
    return jnp.concatenate([steps, level], 1).astype(jnp.int16)


def decoded(code):
    code = code.astype(jnp.int32).astype(jnp.float32)
    size = jnp.exp2(code[:, -1:] * (1.0 / LEVELS)) * (1.0 / STEPS)
    return code[:, :-LANES] * size


def product(place, first, count, acts, other_acts, cotan, other_cotan):
    rows = acts.shape[1] // 8

    def columns(ref):
        return jnp.concatenate(
            [ref[:, pl.ds(pl.multiple_of(place[first + k] * rows, rows), rows)] for k in range(count)], 1
        )

    return dot(columns(acts), cotan[...], TN) + dot(columns(other_acts), other_cotan[...], TN)


def chunk_kernel(first, place, acts, other_acts, cotan, other_cotan, *outs):
    rows = acts.shape[1] // 8
    outs, mark = outs[:-1], outs[-1]
    mark[...] = jnp.zeros_like(mark)
    for out in outs:
        count = out.shape[0]
        value = product(place, first, count, acts, other_acts, cotan, other_cotan)
        for k in range(count):
            out[k] = coded(value[k * rows : (k + 1) * rows])
        first += count


def mine_kernel(place, acts, other_acts, cotan, other_cotan, out, mark):
    rows = acts.shape[1] // 8
    mark[...] = jnp.zeros_like(mark)
    for k in range(2):
        value = product(place, 4 * k, 4, acts, other_acts, cotan, other_cotan)
        for j in range(4):
            out[4 * k + j] = value[rows * j : rows * (j + 1)]


def chunks(kernel, out_shape, scalars, acts, other_acts, cotan, other_cotan, after):
    tokens, width = acts.shape
    half = width // 2
    unused = len(after)

    def body(place, *refs):
        kernel(place, *refs[:4], *refs[4 + unused :])

    def spec(shape):
        return pl.BlockSpec(shape, lambda i, at: (0,) * len(shape))

    return pl.pallas_call(
        body,
        grid_spec=pltpu.PrefetchScalarGridSpec(
            num_scalar_prefetch=1,
            grid=(1,),
            in_specs=[
                pl.BlockSpec((tokens, half), lambda i, at: (0, at[8])),
                pl.BlockSpec((tokens, half), lambda i, at: (0, at[8])),
                pl.BlockSpec((tokens, half), lambda i, at: (0, at[9])),
                pl.BlockSpec((tokens, half), lambda i, at: (0, at[9])),
            ]
            + [pl.BlockSpec(memory_space=pltpu.VMEM)] * unused,
            out_specs=jax.tree.map(lambda a: spec(a.shape), out_shape),
        ),
        out_shape=out_shape,
        cost_estimate=NO_COST,
        compiler_params=pltpu.CompilerParams(vmem_limit_bytes=MOST_VMEM),
    )(scalars, acts, other_acts, cotan, other_cotan, *after)


def hop_kernel(step, unused, *refs):
    mine, from_x = refs[:2]
    down = mine[0] + decoded(from_x[0])
    up = mine[1] + decoded(from_x[1])
    if step > 0:
        down = down + decoded(refs[2][...])
        up = up + decoded(refs[3][...])
    refs[-3][...] = coded(down)
    refs[-2][...] = up if step == 3 else coded(up)
    refs[-1][...] = jnp.zeros_like(refs[-1])


def hop(step, mine, from_x, received, after):
    _, rows, columns = mine.shape
    wide = columns + LANES
    whole = pl.BlockSpec((rows, wide), lambda i: (0, 0))
    sent = jax.ShapeDtypeStruct((rows, wide), jnp.int16)
    last = jax.ShapeDtypeStruct((rows, columns), jnp.float32) if step == 3 else sent
    return pl.pallas_call(
        functools.partial(hop_kernel, step, len(after)),
        grid=(1,),
        in_specs=[
            pl.BlockSpec((2, rows, columns), lambda i: (step, 0, 0)),
            pl.BlockSpec((2, rows, wide), lambda i: (step % 2, 0, 0)),
        ]
        + [whole] * len(received)
        + [pl.BlockSpec(memory_space=pltpu.VMEM)] * len(after),
        out_specs=[whole] + [pl.BlockSpec(a.shape, lambda i: (0, 0)) for a in (last, MARK)],
        out_shape=[sent, last, MARK],
        cost_estimate=NO_COST,
        compiler_params=pltpu.CompilerParams(vmem_limit_bytes=VMEM),
    )(mine, from_x, *received, *after)


def total_kernel(core, up, down, kept, given, mark):
    total = up[...] + decoded(down[...])
    mark[...] = jnp.zeros_like(mark)
    rows = kept.shape[0]
    mine = jnp.where(core[0] == 0, 1.0, 0.0)
    kept[...] = jnp.where(mine > 0.5, total[:rows], total[rows:])
    given[...] = jnp.where(mine > 0.5, total[rows:], total[:rows])


def shifted(value, axis, steps):
    count = lax.axis_size(axis)
    return lax.ppermute(value, axis, [(i, (i + steps) % count) for i in range(count)])


def held(value, after, arrays=(), limit=VMEM):
    def body(*refs):
        pass

    anywhere = pl.BlockSpec(memory_space=pl.ANY)
    return pl.pallas_call(
        body,
        in_specs=[anywhere] * (1 + len(arrays))
        + [pl.BlockSpec(memory_space=pltpu.VMEM)] * len(after),
        out_specs=anywhere,
        out_shape=jax.ShapeDtypeStruct(value.shape, value.dtype),
        input_output_aliases={0: 0},
        cost_estimate=NO_COST,
        compiler_params=pltpu.CompilerParams(vmem_limit_bytes=limit),
    )(value, *arrays, *after)


def input_kernel(at, cotan, weights, *refs):
    out, mark = refs[-2:]
    mark[...] = jnp.zeros_like(mark)
    out[...] = dot(cotan[...], weights[...], NT).astype(jnp.bfloat16)


def backward_input(half, cotan, weights, after, into=()):
    tokens, width = cotan.shape
    tile = width // 8
    return pl.pallas_call(
        input_kernel,
        grid_spec=pltpu.PrefetchScalarGridSpec(
            num_scalar_prefetch=1,
            grid=(4,),
            in_specs=[
                pl.BlockSpec((tokens, width), lambda i, at: (0, 0)),
                pl.BlockSpec((tile, width), lambda i, at: (i, 0)),
            ]
            + [pl.BlockSpec(memory_space=pl.ANY)] * len(into)
            + [pl.BlockSpec(memory_space=pltpu.VMEM)] * len(after),
            out_specs=[
                pl.BlockSpec((tokens, tile), lambda i, at: (0, 4 * at[0] + i)),
                pl.BlockSpec(MARK.shape, lambda i, at: (0, 0)),
            ],
        ),
        out_shape=[jax.ShapeDtypeStruct((tokens, width), jnp.bfloat16), MARK],
        input_output_aliases={3: 0} if into else {},
        cost_estimate=NO_COST,
        compiler_params=pltpu.CompilerParams(vmem_limit_bytes=NO_ROOM),
    )(half[None].astype(jnp.int32), cotan, weights, *into, *after)


def update_kernel(core, weight, kept, taken, basis, right, left, from_right, from_left, out, out_q):
    next_right = right[...] - from_right[...]
    next_left = from_left[...] - left[...]
    out_q[...] = next_right
    moves = (
        basis[:, 0:1] * next_right[0:1]
        + basis[:, 1:2] * next_right[1:2]
        - basis[:, 2:3] * next_left[0:1]
        - basis[:, 3:4] * next_left[1:2]
    )
    stepped = weight[...].astype(jnp.float32) - GOSSIP * moves
    columns = kept.shape[1]
    swapped = jnp.broadcast_to(core[0], kept.shape) == 1
    first = jnp.where(swapped, taken[...], kept[...])
    second = jnp.where(swapped, kept[...], taken[...])
    out[:, :columns] = stepped[:, :columns] - LEARN * first
    out[:, columns:] = stepped[:, columns:] - LEARN * second


def on_device(activ, grad_out, weight, q_seed):
    acts = activ[0]
    cotan = grad_out[0]
    weight_bf = weight[0]
    rows, width = weight_bf.shape
    columns = width // 2
    core, x, z = lax.axis_index("core"), lax.axis_index("xl"), lax.axis_index("z")
    own = lax.axis_index(SHARD)
    replica = lax.axis_index(CYCLE)
    cycle_size = lax.axis_size(CYCLE)

    other_acts = partner(acts, "core", 1)
    other_cotan = partner(cotan, "core", 1)
    tokens = (acts, other_acts, cotan, other_cotan)

    q_right = lax.dynamic_index_in_dim(q_seed, replica, 0, keepdims=False)
    q_left = lax.dynamic_index_in_dim(
        q_seed, (replica + cycle_size - 1) % cycle_size, 0, keepdims=False
    )
    probes = jnp.concatenate([q_right, q_left], 1).astype(jnp.bfloat16).T
    probes = jnp.pad(probes, ((0, 12), (0, 0)))
    at = own[None].astype(jnp.int32)
    part = kernel_call(probe_kernel, (probes, acts, cotan, weight_bf), f32(4, width), at)

    place = [(z + offset) % 8 for step in range(4) for offset in (4 + step, 3 - step)]
    scalars = jnp.stack(place + [1 - x, core]).astype(jnp.int32)
    mine_scalars = jnp.stack(place + [x, core]).astype(jnp.int32)
    pieces = jax.ShapeDtypeStruct((4, 2 * rows, columns + LANES), jnp.int16)
    value = shard_sum(part, STEPS_ALONG[:1], {})

    taken = partner(weight_bf, "core", 1)
    chip = jnp.where(
        core == 0, jnp.concatenate([weight_bf, taken], 0), jnp.concatenate([taken, weight_bf], 0)
    )
    crossed = lax.ppermute(chip, ("xl", "core"), [(0, 2), (3, 1)])
    column = held(jnp.where(core == x, chip, crossed), (value,), (other_acts, other_cotan))
    weights = lax.all_gather(column, "z", axis=0, tiled=True)

    first, mark = chunks(
        functools.partial(chunk_kernel, 0), (pieces, MARK), scalars, *tokens, (value,)
    )
    value = shard_sum(value, STEPS_ALONG[1:2], {"xl1": (mark,)})
    first = partner(held(first, (value,)), "xl", 1)
    value = shard_sum(value, STEPS_ALONG[2:3], {})
    mine, mark = chunks(
        mine_kernel, (f32(8, 2 * rows, columns), MARK), mine_scalars, *tokens, (value,)
    )

    def hops(step, received, after, from_x):
        down, up, mark = hop(step, mine, from_x, received, after)
        return (shifted(down, "z", -1), shifted(up, "z", 1) if step < 3 else up), (mark,)

    value = shard_sum(value, STEPS_ALONG[3:4], {"z2": (mark,)})
    second, mark = chunks(
        functools.partial(chunk_kernel, 4), (pieces, MARK), scalars, *tokens, (value,)
    )
    right, left = shard_sum(value, STEPS_ALONG[4:], {"z4": (mark,)}, "z4")
    arrived = neighbours(right, left)
    received, sent = hops(0, (), arrived, first)
    second = partner(held(second, sent), "xl", 1)
    back, basis = kernel_call(
        basis_kernel,
        (right, left, *arrived, acts, cotan, weight_bf),
        (f32(4, width), f32(8, rows)),
        at,
        sent,
    )
    value = shard_sum(back, STEPS_BACK[:2], {})
    received, sent = hops(1, received, (value,), first)
    value = shard_sum(value, STEPS_BACK[2:3], {"z2": sent})
    received, sent = hops(2, received, (value,), second)
    weights = held(weights, sent, (), NO_ROOM)
    half, mark = backward_input(core, cotan, weights, sent)
    right, left = shard_sum(value, STEPS_BACK[3:], {"z4": (mark,)}, "xl1")
    received, sent = hops(3, received, (right,), second)
    arrived = neighbours(right, left)
    grad_in, mark = backward_input(
        1 - core, cotan, partner(weights, "core", 1), sent, (half,)
    )
    kept, given, _ = kernel_call(
        total_kernel,
        (received[1], received[0]),
        (f32(rows, columns), f32(rows, columns), MARK),
        core[None].astype(jnp.int32),
        (mark, *arrived),
    )
    new_weight, next_q = kernel_call(
        update_kernel,
        (weight_bf, kept, partner(given, "core", 1), basis.T, right, left, *arrived),
        (f32(rows, width), f32(2, width)),
        core[None].astype(jnp.int32),
        (mark,),
    )
    return (grad_in[None], new_weight[None], next_q.T[None])


def solution(mesh):
    fine = Mesh(mesh.devices.reshape(2, 4, 2, 8, 2), CYCLE + SHARD)
    tokens = P(CYCLE, SHARD, None)
    return jax.shard_map(
        on_device,
        mesh=fine,
        in_specs=(tokens, tokens, tokens, P()),
        out_specs=(tokens, tokens, P(CYCLE, None, None)),
        check_vma=False,
    )
```

```python
import functools

import jax
import jax.numpy as jnp
from jax import lax
from jax.experimental import pallas as pl
from jax.experimental.pallas import tpu as pltpu
from jax.sharding import Mesh
from jax.sharding import PartitionSpec as P

LEARN = 0.002
GOSSIP = 0.5
EPS = 1e-06
LANES = 128
LEVELS = 64.0
STEPS = 32767.0
VMEM = 16 * 2**20
MOST_VMEM = 24 * 2**20
NO_ROOM = 56 * 2**20
MARK = jax.ShapeDtypeStruct((8, 128), jnp.float32)
NO_COST = pl.CostEstimate(flops=0, bytes_accessed=0, transcendentals=0)
STEPS_BACK = (("core", 1), ("z", 1), ("z", 2), ("z", 4), ("xl", 1))
STEPS_ALONG = (("core", 1), ("xl", 1), ("z", 1), ("z", 2), ("z", 4))

CYCLE = ("xh", "y")
SHARD = ("xl", "z", "core")
NT = (((1,), (1,)), ((), ()))
NN = (((1,), (0,)), ((), ()))
TN = (((0,), (0,)), ((), ()))


def dot(left, right, dims):
    return lax.dot_general(left, right, dims, preferred_element_type=jnp.float32)


def terms(value):
    high = value.astype(jnp.bfloat16)
    rest = value - high.astype(jnp.float32)
    middle = rest.astype(jnp.bfloat16)
    low = (rest - middle.astype(jnp.float32)).astype(jnp.bfloat16)
    parts = [part.astype(jnp.float32) for part in (high, middle, low)]
    return jnp.concatenate(parts, 0).astype(jnp.bfloat16)


def summed(value):
    return value[:8] + (value[8:16] + value[16:])


def thin(left, right, dims):
    return summed(dot(left, right, dims))


def own_columns(own, rows, width):
    row = lax.broadcasted_iota(jnp.int32, (rows, width), 0) + own * rows
    column = lax.broadcasted_iota(jnp.int32, (rows, width), 1)
    return jnp.where(row == column, 1.0, 0.0).astype(jnp.bfloat16)


def kernel_call(kernel, operands, out_shape, scalars=None, after=()):
    whole = pl.BlockSpec(memory_space=pltpu.VMEM)
    specs = [whole] * (len(operands) + len(after))
    first = []
    if scalars is not None:
        specs, first = [pl.BlockSpec(memory_space=pltpu.SMEM)] + specs, [scalars]
    lead, unused = len(first) + len(operands), len(after)

    def body(*refs):
        kernel(*refs[:lead], *refs[lead + unused :])

    return pl.pallas_call(
        body,
        in_specs=specs,
        out_specs=jax.tree.map(lambda _: whole, out_shape),
        out_shape=out_shape,
        cost_estimate=NO_COST,
        compiler_params=pltpu.CompilerParams(vmem_limit_bytes=VMEM),
    )(*first, *operands, *after)


def f32(*shape):
    return jax.ShapeDtypeStruct(shape, jnp.float32)


def probe_kernel(own, probes, acts, cotan, weight, out):
    rows, width = weight.shape
    from_grads = thin(terms(dot(probes[...], cotan[...], NT)[:8]), acts[...], NN)
    from_weight = terms(dot(probes[...], weight[...], NT)[:8])
    placed = thin(from_weight, own_columns(own[0], rows, width), NN)
    out[...] = (placed - LEARN * from_grads)[:4]


def unit_vectors(proj):
    first, second = proj[0:1], proj[1:2]
    unit_first = first * lax.rsqrt(jnp.sum(first * first, keepdims=True) + EPS)
    remain = second - jnp.sum(unit_first * second, keepdims=True) * unit_first
    unit_second = remain * lax.rsqrt(jnp.sum(remain * remain, keepdims=True) + EPS)
    return [unit_first, unit_second]


def basis_kernel(
    own, right, left, from_right, from_left, acts, cotan, weight, out, out_basis
):
    rows, width = weight.shape
    units = unit_vectors(right[...] - from_right[...])
    units += unit_vectors(from_left[...] - left[...])
    row = lax.broadcasted_iota(jnp.int32, (8, width), 0)
    basis = jnp.zeros((8, width), jnp.float32)
    for k, unit in enumerate(units):
        basis = jnp.where(row == k, jnp.broadcast_to(unit, (8, width)), basis)
    parts = terms(basis)
    own_parts = dot(parts, own_columns(own[0], rows, width), NT)
    out_basis[...] = summed(own_parts)
    from_weight = thin(own_parts.astype(jnp.bfloat16), weight[...], NN)
    from_grads = thin(terms(thin(parts, acts[...], NT)), cotan[...], NN)
    out[...] = (from_weight - LEARN * from_grads)[:4]


def add_kernel(left, right, out):
    out[...] = left[...] + right[...]


def add_split_kernel(left, right, out_right, out_left):
    total = left[...] + right[...]
    out_right[...] = total[:2]
    out_left[...] = total[2:]


def partner(value, axis, step):
    count = lax.axis_size(axis)
    return lax.ppermute(value, axis, [(i, i ^ step) for i in range(count)])


def shard_sum(value, steps, after, split=None):
    for axis, step in steps:
        key = axis + str(step)
        operands = (value, partner(value, axis, step))
        if key == split:
            halves = (f32(2, value.shape[1]), f32(2, value.shape[1]))
            value = kernel_call(add_split_kernel, operands, halves, after=after.get(key, ()))
        else:
            value = kernel_call(add_kernel, operands, f32(*value.shape), after=after.get(key, ()))
    return value


def passed_along(value, steps):
    count, row = lax.axis_size(CYCLE), lax.axis_size("y")
    pairs = []
    for source in range(count):
        target = (source + steps) % count
        crossed = int(source // row != target // row)
        pairs += [(2 * source + x, 2 * target + (x ^ crossed)) for x in range(2)]
    return lax.ppermute(value, CYCLE + ("xl",), pairs)


def neighbours(right, left):
    return passed_along(left, -1), passed_along(right, 1)


def coded(value):
    largest = jnp.maximum(jnp.max(jnp.abs(value), 1, keepdims=True), 1e-30)
    level = jnp.ceil(jnp.log2(largest) * LEVELS + 0.01)
    steps = jnp.floor(value * (STEPS * jnp.exp2(level * (-1.0 / LEVELS))) + 0.5)
    steps = jnp.clip(steps, -STEPS, STEPS).astype(jnp.int32)
    level = jnp.broadcast_to(level, (value.shape[0], LANES)).astype(jnp.int32)
    return jnp.concatenate([steps, level], 1).astype(jnp.int16)


def decoded(code):
    code = code.astype(jnp.int32).astype(jnp.float32)
    size = jnp.exp2(code[:, -1:] * (1.0 / LEVELS)) * (1.0 / STEPS)
    return code[:, :-LANES] * size


def product(place, first, count, acts, other_acts, cotan, other_cotan):
    rows = acts.shape[1] // 8

    def columns(ref):
        return jnp.concatenate(
            [ref[:, pl.ds(pl.multiple_of(place[first + k] * rows, rows), rows)] for k in range(count)], 1
        )

    return dot(columns(acts), cotan[...], TN) + dot(columns(other_acts), other_cotan[...], TN)


def chunk_kernel(first, place, acts, other_acts, cotan, other_cotan, *outs):
    rows = acts.shape[1] // 8
    outs, mark = outs[:-1], outs[-1]
    mark[...] = jnp.zeros_like(mark)
    for out in outs:
        count = out.shape[0]
        value = product(place, first, count, acts, other_acts, cotan, other_cotan)
        for k in range(count):
            out[k] = coded(value[k * rows : (k + 1) * rows])
        first += count


def mine_kernel(place, acts, other_acts, cotan, other_cotan, out, mark):
    rows = acts.shape[1] // 8
    mark[...] = jnp.zeros_like(mark)
    for k in range(2):
        value = product(place, 4 * k, 4, acts, other_acts, cotan, other_cotan)
        for j in range(4):
            out[4 * k + j] = value[rows * j : rows * (j + 1)]


def chunks(kernel, out_shape, scalars, acts, other_acts, cotan, other_cotan, after):
    tokens, width = acts.shape
    half = width // 2
    unused = len(after)

    def body(place, *refs):
        kernel(place, *refs[:4], *refs[4 + unused :])

    def spec(shape):
        return pl.BlockSpec(shape, lambda i, at: (0,) * len(shape))

    return pl.pallas_call(
        body,
        grid_spec=pltpu.PrefetchScalarGridSpec(
            num_scalar_prefetch=1,
            grid=(1,),
            in_specs=[
                pl.BlockSpec((tokens, half), lambda i, at: (0, at[8])),
                pl.BlockSpec((tokens, half), lambda i, at: (0, at[8])),
                pl.BlockSpec((tokens, half), lambda i, at: (0, at[9])),
                pl.BlockSpec((tokens, half), lambda i, at: (0, at[9])),
            ]
            + [pl.BlockSpec(memory_space=pltpu.VMEM)] * unused,
            out_specs=jax.tree.map(lambda a: spec(a.shape), out_shape),
        ),
        out_shape=out_shape,
        cost_estimate=NO_COST,
        compiler_params=pltpu.CompilerParams(vmem_limit_bytes=MOST_VMEM),
    )(scalars, acts, other_acts, cotan, other_cotan, *after)


def hop_kernel(step, unused, *refs):
    mine, from_x = refs[:2]
    down = mine[0] + decoded(from_x[0])
    up = mine[1] + decoded(from_x[1])
    if step > 0:
        down = down + decoded(refs[2][...])
        up = up + decoded(refs[3][...])
    refs[-3][...] = coded(down)
    refs[-2][...] = up if step == 3 else coded(up)
    refs[-1][...] = jnp.zeros_like(refs[-1])


def hop(step, mine, from_x, received, after):
    _, rows, columns = mine.shape
    wide = columns + LANES
    whole = pl.BlockSpec((rows, wide), lambda i: (0, 0))
    sent = jax.ShapeDtypeStruct((rows, wide), jnp.int16)
    last = jax.ShapeDtypeStruct((rows, columns), jnp.float32) if step == 3 else sent
    return pl.pallas_call(
        functools.partial(hop_kernel, step, len(after)),
        grid=(1,),
        in_specs=[
            pl.BlockSpec((2, rows, columns), lambda i: (step, 0, 0)),
            pl.BlockSpec((2, rows, wide), lambda i: (step % 2, 0, 0)),
        ]
        + [whole] * len(received)
        + [pl.BlockSpec(memory_space=pltpu.VMEM)] * len(after),
        out_specs=[whole] + [pl.BlockSpec(a.shape, lambda i: (0, 0)) for a in (last, MARK)],
        out_shape=[sent, last, MARK],
        cost_estimate=NO_COST,
        compiler_params=pltpu.CompilerParams(vmem_limit_bytes=VMEM),
    )(mine, from_x, *received, *after)


def total_kernel(core, up, down, kept, given, mark):
    total = up[...] + decoded(down[...])
    mark[...] = jnp.zeros_like(mark)
    rows = kept.shape[0]
    mine = jnp.where(core[0] == 0, 1.0, 0.0)
    kept[...] = jnp.where(mine > 0.5, total[:rows], total[rows:])
    given[...] = jnp.where(mine > 0.5, total[rows:], total[:rows])


def shifted(value, axis, steps):
    count = lax.axis_size(axis)
    return lax.ppermute(value, axis, [(i, (i + steps) % count) for i in range(count)])


def held(value, after, arrays=(), limit=VMEM):
    def body(*refs):
        pass

    anywhere = pl.BlockSpec(memory_space=pl.ANY)
    return pl.pallas_call(
        body,
        in_specs=[anywhere] * (1 + len(arrays))
        + [pl.BlockSpec(memory_space=pltpu.VMEM)] * len(after),
        out_specs=anywhere,
        out_shape=jax.ShapeDtypeStruct(value.shape, value.dtype),
        input_output_aliases={0: 0},
        cost_estimate=NO_COST,
        compiler_params=pltpu.CompilerParams(vmem_limit_bytes=limit),
    )(value, *arrays, *after)


def input_kernel(unused, at, cotan, weights, other_weights, *refs):
    out, mark = refs[unused:]
    mark[...] = jnp.zeros_like(mark)
    core, x, z = at[0], at[1], pl.program_id(0)
    wide = 2 * weights.shape[1]

    def planes(first, second):
        blocks = [first[0], second[0], first[1], second[1]]
        value = dot(cotan[...], jnp.concatenate(blocks, 0), NT).astype(jnp.bfloat16)
        for column in range(2):
            chip = (x * (1 - column) + (1 - x) * column) * 8 + z
            place = pl.ds(pl.multiple_of(chip * wide, wide), wide)
            out[:, place] = value[:, column * wide : (column + 1) * wide]

    @pl.when(core == 0)
    def _():
        planes(weights, other_weights)

    @pl.when(core == 1)
    def _():
        planes(other_weights, weights)


def backward_input(core, x, cotan, weights, other_weights, after):
    tokens, width = cotan.shape
    rows = weights.shape[1]
    plane = pl.BlockSpec((2, rows, width), lambda i, at: (i, 0, 0))
    return pl.pallas_call(
        functools.partial(input_kernel, len(after)),
        grid_spec=pltpu.PrefetchScalarGridSpec(
            num_scalar_prefetch=1,
            grid=(8,),
            in_specs=[pl.BlockSpec((tokens, width), lambda i, at: (0, 0)), plane, plane]
            + [pl.BlockSpec(memory_space=pltpu.VMEM)] * len(after),
            out_specs=[
                pl.BlockSpec((tokens, width), lambda i, at: (0, 0)),
                pl.BlockSpec(MARK.shape, lambda i, at: (0, 0)),
            ],
        ),
        out_shape=[jax.ShapeDtypeStruct((tokens, width), jnp.bfloat16), MARK],
        cost_estimate=NO_COST,
        compiler_params=pltpu.CompilerParams(vmem_limit_bytes=NO_ROOM),
    )(jnp.stack([core, x]).astype(jnp.int32), cotan, weights, other_weights, *after)


def update_kernel(core, weight, kept, taken, basis, right, left, from_right, from_left, out, out_q):
    next_right = right[...] - from_right[...]
    next_left = from_left[...] - left[...]
    out_q[...] = next_right
    moves = (
        basis[:, 0:1] * next_right[0:1]
        + basis[:, 1:2] * next_right[1:2]
        - basis[:, 2:3] * next_left[0:1]
        - basis[:, 3:4] * next_left[1:2]
    )
    stepped = weight[...].astype(jnp.float32) - GOSSIP * moves
    columns = kept.shape[1]
    swapped = jnp.broadcast_to(core[0], kept.shape) == 1
    first = jnp.where(swapped, taken[...], kept[...])
    second = jnp.where(swapped, kept[...], taken[...])
    out[:, :columns] = stepped[:, :columns] - LEARN * first
    out[:, columns:] = stepped[:, columns:] - LEARN * second


def on_device(activ, grad_out, weight, q_seed):
    acts = activ[0]
    cotan = grad_out[0]
    weight_bf = weight[0]
    rows, width = weight_bf.shape
    columns = width // 2
    core, x, z = lax.axis_index("core"), lax.axis_index("xl"), lax.axis_index("z")
    own = lax.axis_index(SHARD)
    replica = lax.axis_index(CYCLE)
    cycle_size = lax.axis_size(CYCLE)

    other_acts = partner(acts, "core", 1)
    other_cotan = partner(cotan, "core", 1)
    tokens = (acts, other_acts, cotan, other_cotan)

    q_right = lax.dynamic_index_in_dim(q_seed, replica, 0, keepdims=False)
    q_left = lax.dynamic_index_in_dim(
        q_seed, (replica + cycle_size - 1) % cycle_size, 0, keepdims=False
    )
    probes = jnp.concatenate([q_right, q_left], 1).astype(jnp.bfloat16).T
    probes = jnp.pad(probes, ((0, 12), (0, 0)))
    at = own[None].astype(jnp.int32)
    part = kernel_call(probe_kernel, (probes, acts, cotan, weight_bf), f32(4, width), at)

    place = [(z + offset) % 8 for step in range(4) for offset in (4 + step, 3 - step)]
    scalars = jnp.stack(place + [1 - x, core]).astype(jnp.int32)
    mine_scalars = jnp.stack(place + [x, core]).astype(jnp.int32)
    pieces = jax.ShapeDtypeStruct((4, 2 * rows, columns + LANES), jnp.int16)
    value = shard_sum(part, STEPS_ALONG[:1], {})

    pair = held(
        jnp.stack([weight_bf, partner(weight_bf, "xl", 1)], 0), (value,), (other_acts, other_cotan)
    )
    weights = lax.all_gather(pair, "z", axis=0, tiled=True)

    first, mark = chunks(
        functools.partial(chunk_kernel, 0), (pieces, MARK), scalars, *tokens, (value,)
    )
    value = shard_sum(value, STEPS_ALONG[1:2], {"xl1": (mark,)})
    first = partner(held(first, (value,)), "xl", 1)
    value = shard_sum(value, STEPS_ALONG[2:3], {})
    mine, mark = chunks(
        mine_kernel, (f32(8, 2 * rows, columns), MARK), mine_scalars, *tokens, (value,)
    )

    def hops(step, received, after, from_x):
        down, up, mark = hop(step, mine, from_x, received, after)
        return (shifted(down, "z", -1), shifted(up, "z", 1) if step < 3 else up), (mark,)

    value = shard_sum(value, STEPS_ALONG[3:4], {"z2": (mark,)})
    second, mark = chunks(
        functools.partial(chunk_kernel, 4), (pieces, MARK), scalars, *tokens, (value,)
    )
    right, left = shard_sum(value, STEPS_ALONG[4:], {"z4": (mark,)}, "z4")
    arrived = neighbours(right, left)
    received, sent = hops(0, (), arrived, first)
    second = partner(held(second, sent), "xl", 1)
    back, basis = kernel_call(
        basis_kernel,
        (right, left, *arrived, acts, cotan, weight_bf),
        (f32(4, width), f32(8, rows)),
        at,
        sent,
    )
    value = shard_sum(back, STEPS_BACK[:2], {})
    received, sent = hops(1, received, (value,), first)
    value = shard_sum(value, STEPS_BACK[2:3], {"z2": sent})
    received, sent = hops(2, received, (value,), second)
    weights = held(weights, sent, (), NO_ROOM)
    right, left = shard_sum(value, STEPS_BACK[3:], {"z4": sent}, "xl1")
    received, sent = hops(3, received, (right,), second)
    arrived = neighbours(right, left)
    grad_in, mark = backward_input(
        core, x, cotan, weights, partner(weights, "core", 1), sent
    )
    kept, given, _ = kernel_call(
        total_kernel,
        (received[1], received[0]),
        (f32(rows, columns), f32(rows, columns), MARK),
        core[None].astype(jnp.int32),
        (mark, *arrived),
    )
    new_weight, next_q = kernel_call(
        update_kernel,
        (weight_bf, kept, partner(given, "core", 1), basis.T, right, left, *arrived),
        (f32(rows, width), f32(2, width)),
        core[None].astype(jnp.int32),
        (mark,),
    )
    return (grad_in[None], new_weight[None], next_q.T[None])


def solution(mesh):
    fine = Mesh(mesh.devices.reshape(2, 4, 2, 8, 2), CYCLE + SHARD)
    tokens = P(CYCLE, SHARD, None)
    return jax.shard_map(
        on_device,
        mesh=fine,
        in_specs=(tokens, tokens, tokens, P()),
        out_specs=(tokens, tokens, P(CYCLE, None, None)),
        check_vma=False,
    )
```

```python
import functools

import jax
import jax.numpy as jnp
from jax import lax
from jax.experimental import pallas as pl
from jax.experimental.pallas import tpu as pltpu
from jax.sharding import Mesh
from jax.sharding import PartitionSpec as P

LEARN = 0.002
GOSSIP = 0.5
EPS = 1e-06
LANES = 128
LEVELS = 64.0
STEPS = 32767.0
VMEM = 16 * 2**20
MOST_VMEM = 24 * 2**20
NO_ROOM = 56 * 2**20
MARK = jax.ShapeDtypeStruct((8, 128), jnp.float32)
NO_COST = pl.CostEstimate(flops=0, bytes_accessed=0, transcendentals=0)
STEPS_BACK = (("core", 1), ("z", 1), ("z", 2), ("z", 4), ("xl", 1))
STEPS_ALONG = (("core", 1), ("xl", 1), ("z", 1), ("z", 2), ("z", 4))

CYCLE = ("xh", "y")
SHARD = ("xl", "z", "core")
NT = (((1,), (1,)), ((), ()))
NN = (((1,), (0,)), ((), ()))
TN = (((0,), (0,)), ((), ()))


def dot(left, right, dims):
    return lax.dot_general(left, right, dims, preferred_element_type=jnp.float32)


def terms(value):
    high = value.astype(jnp.bfloat16)
    rest = value - high.astype(jnp.float32)
    middle = rest.astype(jnp.bfloat16)
    low = (rest - middle.astype(jnp.float32)).astype(jnp.bfloat16)
    parts = [part.astype(jnp.float32) for part in (high, middle, low)]
    return jnp.concatenate(parts, 0).astype(jnp.bfloat16)


def summed(value):
    return value[:8] + (value[8:16] + value[16:])


def thin(left, right, dims):
    return summed(dot(left, right, dims))


def own_columns(own, rows, width):
    row = lax.broadcasted_iota(jnp.int32, (rows, width), 0) + own * rows
    column = lax.broadcasted_iota(jnp.int32, (rows, width), 1)
    return jnp.where(row == column, 1.0, 0.0).astype(jnp.bfloat16)


def kernel_call(kernel, operands, out_shape, scalars=None, after=()):
    whole = pl.BlockSpec(memory_space=pltpu.VMEM)
    specs = [whole] * (len(operands) + len(after))
    first = []
    if scalars is not None:
        specs, first = [pl.BlockSpec(memory_space=pltpu.SMEM)] + specs, [scalars]
    lead, unused = len(first) + len(operands), len(after)

    def body(*refs):
        kernel(*refs[:lead], *refs[lead + unused :])

    return pl.pallas_call(
        body,
        in_specs=specs,
        out_specs=jax.tree.map(lambda _: whole, out_shape),
        out_shape=out_shape,
        cost_estimate=NO_COST,
        compiler_params=pltpu.CompilerParams(vmem_limit_bytes=VMEM),
    )(*first, *operands, *after)


def f32(*shape):
    return jax.ShapeDtypeStruct(shape, jnp.float32)


def probe_kernel(own, probes, acts, cotan, weight, out):
    rows, width = weight.shape
    from_grads = thin(terms(dot(probes[...], cotan[...], NT)[:8]), acts[...], NN)
    from_weight = terms(dot(probes[...], weight[...], NT)[:8])
    placed = thin(from_weight, own_columns(own[0], rows, width), NN)
    out[...] = (placed - LEARN * from_grads)[:4]


def unit_vectors(proj):
    first, second = proj[0:1], proj[1:2]
    unit_first = first * lax.rsqrt(jnp.sum(first * first, keepdims=True) + EPS)
    remain = second - jnp.sum(unit_first * second, keepdims=True) * unit_first
    unit_second = remain * lax.rsqrt(jnp.sum(remain * remain, keepdims=True) + EPS)
    return [unit_first, unit_second]


def basis_kernel(
    own, right, left, from_right, from_left, acts, cotan, weight, out, out_basis
):
    rows, width = weight.shape
    units = unit_vectors(right[...] - from_right[...])
    units += unit_vectors(from_left[...] - left[...])
    row = lax.broadcasted_iota(jnp.int32, (8, width), 0)
    basis = jnp.zeros((8, width), jnp.float32)
    for k, unit in enumerate(units):
        basis = jnp.where(row == k, jnp.broadcast_to(unit, (8, width)), basis)
    parts = terms(basis)
    own_parts = dot(parts, own_columns(own[0], rows, width), NT)
    out_basis[...] = summed(own_parts)
    from_weight = thin(own_parts.astype(jnp.bfloat16), weight[...], NN)
    from_grads = thin(terms(thin(parts, acts[...], NT)), cotan[...], NN)
    out[...] = (from_weight - LEARN * from_grads)[:4]


def add_kernel(left, right, out):
    out[...] = left[...] + right[...]


def add_split_kernel(left, right, out_right, out_left):
    total = left[...] + right[...]
    out_right[...] = total[:2]
    out_left[...] = total[2:]


def partner(value, axis, step):
    count = lax.axis_size(axis)
    return lax.ppermute(value, axis, [(i, i ^ step) for i in range(count)])


def shard_sum(value, steps, after, split=None):
    for axis, step in steps:
        key = axis + str(step)
        operands = (value, partner(value, axis, step))
        if key == split:
            halves = (f32(2, value.shape[1]), f32(2, value.shape[1]))
            value = kernel_call(add_split_kernel, operands, halves, after=after.get(key, ()))
        else:
            value = kernel_call(add_kernel, operands, f32(*value.shape), after=after.get(key, ()))
    return value


def passed_along(value, steps):
    count, row = lax.axis_size(CYCLE), lax.axis_size("y")
    pairs = []
    for source in range(count):
        target = (source + steps) % count
        crossed = int(source // row != target // row)
        pairs += [(2 * source + x, 2 * target + (x ^ crossed)) for x in range(2)]
    return lax.ppermute(value, CYCLE + ("xl",), pairs)


def neighbours(right, left):
    return passed_along(left, -1), passed_along(right, 1)


def coded(value):
    largest = jnp.maximum(jnp.max(jnp.abs(value), 1, keepdims=True), 1e-30)
    level = jnp.ceil(jnp.log2(largest) * LEVELS + 0.01)
    steps = jnp.floor(value * (STEPS * jnp.exp2(level * (-1.0 / LEVELS))) + 0.5)
    steps = jnp.clip(steps, -STEPS, STEPS).astype(jnp.int32)
    level = jnp.broadcast_to(level, (value.shape[0], LANES)).astype(jnp.int32)
    return jnp.concatenate([steps, level], 1).astype(jnp.int16)


def decoded(code):
    code = code.astype(jnp.int32).astype(jnp.float32)
    size = jnp.exp2(code[:, -1:] * (1.0 / LEVELS)) * (1.0 / STEPS)
    return code[:, :-LANES] * size


def product(place, first, count, acts, other_acts, cotan, other_cotan):
    rows = acts.shape[1] // 8

    def columns(ref):
        return jnp.concatenate(
            [ref[:, pl.ds(pl.multiple_of(place[first + k] * rows, rows), rows)] for k in range(count)], 1
        )

    return dot(columns(acts), cotan[...], TN) + dot(columns(other_acts), other_cotan[...], TN)


def chunk_kernel(first, place, acts, other_acts, cotan, other_cotan, *outs):
    rows = acts.shape[1] // 8
    outs, mark = outs[:-1], outs[-1]
    mark[...] = jnp.zeros_like(mark)
    for out in outs:
        count = out.shape[0]
        value = product(place, first, count, acts, other_acts, cotan, other_cotan)
        for k in range(count):
            out[k] = coded(value[k * rows : (k + 1) * rows])
        first += count


def mine_kernel(place, acts, other_acts, cotan, other_cotan, out, mark):
    rows = acts.shape[1] // 8
    mark[...] = jnp.zeros_like(mark)
    for k in range(2):
        value = product(place, 4 * k, 4, acts, other_acts, cotan, other_cotan)
        for j in range(4):
            out[4 * k + j] = value[rows * j : rows * (j + 1)]


def chunks(kernel, out_shape, scalars, acts, other_acts, cotan, other_cotan, after):
    tokens, width = acts.shape
    half = width // 2
    unused = len(after)

    def body(place, *refs):
        kernel(place, *refs[:4], *refs[4 + unused :])

    def spec(shape):
        return pl.BlockSpec(shape, lambda i, at: (0,) * len(shape))

    return pl.pallas_call(
        body,
        grid_spec=pltpu.PrefetchScalarGridSpec(
            num_scalar_prefetch=1,
            grid=(1,),
            in_specs=[
                pl.BlockSpec((tokens, half), lambda i, at: (0, at[8])),
                pl.BlockSpec((tokens, half), lambda i, at: (0, at[8])),
                pl.BlockSpec((tokens, half), lambda i, at: (0, at[9])),
                pl.BlockSpec((tokens, half), lambda i, at: (0, at[9])),
            ]
            + [pl.BlockSpec(memory_space=pltpu.VMEM)] * unused,
            out_specs=jax.tree.map(lambda a: spec(a.shape), out_shape),
        ),
        out_shape=out_shape,
        cost_estimate=NO_COST,
        compiler_params=pltpu.CompilerParams(vmem_limit_bytes=MOST_VMEM),
    )(scalars, acts, other_acts, cotan, other_cotan, *after)


def hop_kernel(step, unused, *refs):
    mine, from_x = refs[:2]
    down = mine[0] + decoded(from_x[0])
    up = mine[1] + decoded(from_x[1])
    if step > 0:
        down = down + decoded(refs[2][...])
        up = up + decoded(refs[3][...])
    refs[-3][...] = coded(down)
    refs[-2][...] = up if step == 3 else coded(up)
    refs[-1][...] = jnp.zeros_like(refs[-1])


def hop(step, mine, from_x, received, after):
    _, rows, columns = mine.shape
    wide = columns + LANES
    whole = pl.BlockSpec((rows, wide), lambda i: (0, 0))
    sent = jax.ShapeDtypeStruct((rows, wide), jnp.int16)
    last = jax.ShapeDtypeStruct((rows, columns), jnp.float32) if step == 3 else sent
    return pl.pallas_call(
        functools.partial(hop_kernel, step, len(after)),
        grid=(1,),
        in_specs=[
            pl.BlockSpec((2, rows, columns), lambda i: (step, 0, 0)),
            pl.BlockSpec((2, rows, wide), lambda i: (step % 2, 0, 0)),
        ]
        + [whole] * len(received)
        + [pl.BlockSpec(memory_space=pltpu.VMEM)] * len(after),
        out_specs=[whole] + [pl.BlockSpec(a.shape, lambda i: (0, 0)) for a in (last, MARK)],
        out_shape=[sent, last, MARK],
        cost_estimate=NO_COST,
        compiler_params=pltpu.CompilerParams(vmem_limit_bytes=VMEM),
    )(mine, from_x, *received, *after)


def total_kernel(core, up, down, kept, given, mark):
    total = up[...] + decoded(down[...])
    mark[...] = jnp.zeros_like(mark)
    rows = kept.shape[0]
    mine = jnp.where(core[0] == 0, 1.0, 0.0)
    kept[...] = jnp.where(mine > 0.5, total[:rows], total[rows:])
    given[...] = jnp.where(mine > 0.5, total[rows:], total[:rows])


def shifted(value, axis, steps):
    count = lax.axis_size(axis)
    return lax.ppermute(value, axis, [(i, (i + steps) % count) for i in range(count)])


def held(value, after, arrays=(), limit=VMEM):
    def body(*refs):
        pass

    anywhere = pl.BlockSpec(memory_space=pl.ANY)
    return pl.pallas_call(
        body,
        in_specs=[anywhere] * (1 + len(arrays))
        + [pl.BlockSpec(memory_space=pltpu.VMEM)] * len(after),
        out_specs=anywhere,
        out_shape=jax.ShapeDtypeStruct(value.shape, value.dtype),
        input_output_aliases={0: 0},
        cost_estimate=NO_COST,
        compiler_params=pltpu.CompilerParams(vmem_limit_bytes=limit),
    )(value, *arrays, *after)


def input_kernel(at, cotan, weights, other_weights, *refs):
    out, mark = refs[-2:]
    mark[...] = jnp.zeros_like(mark)
    column = pl.program_id(1)

    def planes(first, second):
        blocks = [first[column], second[column], first[2 + column], second[2 + column]]
        value = dot(cotan[...], jnp.concatenate(blocks, 0), NT)
        out[...] = value.astype(jnp.bfloat16)

    @pl.when(at[0] == 0)
    def _():
        planes(weights, other_weights)

    @pl.when(at[0] == 1)
    def _():
        planes(other_weights, weights)


def backward_input(core, x, first, cotan, weights, other_weights, after, into=()):
    tokens, width = cotan.shape
    rows = weights.shape[1]
    planes = pl.BlockSpec((4, rows, width), lambda i, j, at: (at[2] + i, 0, 0))
    scalars = jnp.stack([core, x, jnp.full_like(core, first)]).astype(jnp.int32)
    return pl.pallas_call(
        input_kernel,
        grid_spec=pltpu.PrefetchScalarGridSpec(
            num_scalar_prefetch=1,
            grid=(2, 2),
            in_specs=[pl.BlockSpec((tokens, width), lambda i, j, at: (0, 0)), planes, planes]
            + [pl.BlockSpec(memory_space=pl.ANY)] * len(into)
            + [pl.BlockSpec(memory_space=pltpu.VMEM)] * len(after),
            out_specs=[
                pl.BlockSpec(
                    (tokens, width // 8),
                    lambda i, j, at: (0, 4 * (at[1] * (1 - j) + (1 - at[1]) * j) + at[2] + i),
                ),
                pl.BlockSpec(MARK.shape, lambda i, j, at: (0, 0)),
            ],
        ),
        out_shape=[jax.ShapeDtypeStruct((tokens, width), jnp.bfloat16), MARK],
        input_output_aliases={4: 0} if into else {},
        cost_estimate=NO_COST,
        compiler_params=pltpu.CompilerParams(vmem_limit_bytes=NO_ROOM),
    )(scalars, cotan, weights, other_weights, *into, *after)


def update_kernel(core, weight, kept, taken, basis, right, left, from_right, from_left, out, out_q):
    next_right = right[...] - from_right[...]
    next_left = from_left[...] - left[...]
    out_q[...] = next_right
    moves = (
        basis[:, 0:1] * next_right[0:1]
        + basis[:, 1:2] * next_right[1:2]
        - basis[:, 2:3] * next_left[0:1]
        - basis[:, 3:4] * next_left[1:2]
    )
    stepped = weight[...].astype(jnp.float32) - GOSSIP * moves
    columns = kept.shape[1]
    swapped = jnp.broadcast_to(core[0], kept.shape) == 1
    first = jnp.where(swapped, taken[...], kept[...])
    second = jnp.where(swapped, kept[...], taken[...])
    out[:, :columns] = stepped[:, :columns] - LEARN * first
    out[:, columns:] = stepped[:, columns:] - LEARN * second


def on_device(activ, grad_out, weight, q_seed):
    acts = activ[0]
    cotan = grad_out[0]
    weight_bf = weight[0]
    rows, width = weight_bf.shape
    columns = width // 2
    core, x, z = lax.axis_index("core"), lax.axis_index("xl"), lax.axis_index("z")
    own = lax.axis_index(SHARD)
    replica = lax.axis_index(CYCLE)
    cycle_size = lax.axis_size(CYCLE)

    other_acts = partner(acts, "core", 1)
    other_cotan = partner(cotan, "core", 1)
    tokens = (acts, other_acts, cotan, other_cotan)

    q_right = lax.dynamic_index_in_dim(q_seed, replica, 0, keepdims=False)
    q_left = lax.dynamic_index_in_dim(
        q_seed, (replica + cycle_size - 1) % cycle_size, 0, keepdims=False
    )
    probes = jnp.concatenate([q_right, q_left], 1).astype(jnp.bfloat16).T
    probes = jnp.pad(probes, ((0, 12), (0, 0)))
    at = own[None].astype(jnp.int32)
    part = kernel_call(probe_kernel, (probes, acts, cotan, weight_bf), f32(4, width), at)

    place = [(z + offset) % 8 for step in range(4) for offset in (4 + step, 3 - step)]
    scalars = jnp.stack(place + [1 - x, core]).astype(jnp.int32)
    mine_scalars = jnp.stack(place + [x, core]).astype(jnp.int32)
    pieces = jax.ShapeDtypeStruct((4, 2 * rows, columns + LANES), jnp.int16)
    value = shard_sum(part, STEPS_ALONG[:1], {})

    pair = held(
        jnp.stack([weight_bf, partner(weight_bf, "xl", 1)], 0), (value,), (other_acts, other_cotan)
    )
    weights = lax.all_gather(pair, "z", axis=0, tiled=True)

    first, mark = chunks(
        functools.partial(chunk_kernel, 0), (pieces, MARK), scalars, *tokens, (value,)
    )
    value = shard_sum(value, STEPS_ALONG[1:2], {"xl1": (mark,)})
    first = partner(held(first, (value,)), "xl", 1)
    value = shard_sum(value, STEPS_ALONG[2:3], {})
    mine, mark = chunks(
        mine_kernel, (f32(8, 2 * rows, columns), MARK), mine_scalars, *tokens, (value,)
    )

    def hops(step, received, after, from_x):
        down, up, mark = hop(step, mine, from_x, received, after)
        return (shifted(down, "z", -1), shifted(up, "z", 1) if step < 3 else up), (mark,)

    value = shard_sum(value, STEPS_ALONG[3:4], {"z2": (mark,)})
    second, mark = chunks(
        functools.partial(chunk_kernel, 4), (pieces, MARK), scalars, *tokens, (value,)
    )
    right, left = shard_sum(value, STEPS_ALONG[4:], {"z4": (mark,)}, "z4")
    arrived = neighbours(right, left)
    received, sent = hops(0, (), arrived, first)
    second = partner(held(second, sent), "xl", 1)
    back, basis = kernel_call(
        basis_kernel,
        (right, left, *arrived, acts, cotan, weight_bf),
        (f32(4, width), f32(8, rows)),
        at,
        sent,
    )
    value = shard_sum(back, STEPS_BACK[:2], {})
    received, sent = hops(1, received, (value,), first)
    value = shard_sum(value, STEPS_BACK[2:3], {"z2": sent})
    received, sent = hops(2, received, (value,), second)
    weights = held(weights, sent, (), NO_ROOM)
    both = (cotan, weights, partner(weights, "core", 1))
    half, mark = backward_input(core, x, 0, *both, sent)
    right, left = shard_sum(value, STEPS_BACK[3:], {"z4": (mark,)}, "xl1")
    received, sent = hops(3, received, (right,), second)
    arrived = neighbours(right, left)
    grad_in, mark = backward_input(core, x, 2, *both, sent, (half,))
    kept, given, _ = kernel_call(
        total_kernel,
        (received[1], received[0]),
        (f32(rows, columns), f32(rows, columns), MARK),
        core[None].astype(jnp.int32),
        (mark, *arrived),
    )
    new_weight, next_q = kernel_call(
        update_kernel,
        (weight_bf, kept, partner(given, "core", 1), basis.T, right, left, *arrived),
        (f32(rows, width), f32(2, width)),
        core[None].astype(jnp.int32),
        (mark,),
    )
    return (grad_in[None], new_weight[None], next_q.T[None])


def solution(mesh):
    fine = Mesh(mesh.devices.reshape(2, 4, 2, 8, 2), CYCLE + SHARD)
    tokens = P(CYCLE, SHARD, None)
    return jax.shard_map(
        on_device,
        mesh=fine,
        in_specs=(tokens, tokens, tokens, P()),
        out_specs=(tokens, tokens, P(CYCLE, None, None)),
        check_vma=False,
    )
```

```python
import functools

import jax
import jax.numpy as jnp
from jax import lax
from jax.experimental import pallas as pl
from jax.experimental.pallas import tpu as pltpu
from jax.sharding import Mesh
from jax.sharding import PartitionSpec as P

LEARN = 0.002
GOSSIP = 0.5
EPS = 1e-06
LANES = 128
LEVELS = 64.0
STEPS = 32767.0
VMEM = 16 * 2**20
MOST_VMEM = 24 * 2**20
NO_ROOM = 56 * 2**20
MARK = jax.ShapeDtypeStruct((8, 128), jnp.float32)
NO_COST = pl.CostEstimate(flops=0, bytes_accessed=0, transcendentals=0)
STEPS_BACK = (("core", 1), ("z", 1), ("z", 2), ("z", 4), ("xl", 1))
STEPS_ALONG = (("core", 1), ("xl", 1), ("z", 1), ("z", 2), ("z", 4))

CYCLE = ("xh", "y")
SHARD = ("xl", "z", "core")
NT = (((1,), (1,)), ((), ()))
NN = (((1,), (0,)), ((), ()))
TN = (((0,), (0,)), ((), ()))


def dot(left, right, dims):
    return lax.dot_general(left, right, dims, preferred_element_type=jnp.float32)


def terms(value):
    high = value.astype(jnp.bfloat16)
    rest = value - high.astype(jnp.float32)
    middle = rest.astype(jnp.bfloat16)
    low = (rest - middle.astype(jnp.float32)).astype(jnp.bfloat16)
    parts = [part.astype(jnp.float32) for part in (high, middle, low)]
    return jnp.concatenate(parts, 0).astype(jnp.bfloat16)


def summed(value):
    return value[:8] + (value[8:16] + value[16:])


def thin(left, right, dims):
    return summed(dot(left, right, dims))


def own_columns(own, rows, width):
    row = lax.broadcasted_iota(jnp.int32, (rows, width), 0) + own * rows
    column = lax.broadcasted_iota(jnp.int32, (rows, width), 1)
    return jnp.where(row == column, 1.0, 0.0).astype(jnp.bfloat16)


def kernel_call(kernel, operands, out_shape, scalars=None, after=()):
    whole = pl.BlockSpec(memory_space=pltpu.VMEM)
    specs = [whole] * (len(operands) + len(after))
    first = []
    if scalars is not None:
        specs, first = [pl.BlockSpec(memory_space=pltpu.SMEM)] + specs, [scalars]
    lead, unused = len(first) + len(operands), len(after)

    def body(*refs):
        kernel(*refs[:lead], *refs[lead + unused :])

    return pl.pallas_call(
        body,
        in_specs=specs,
        out_specs=jax.tree.map(lambda _: whole, out_shape),
        out_shape=out_shape,
        cost_estimate=NO_COST,
        compiler_params=pltpu.CompilerParams(vmem_limit_bytes=VMEM),
    )(*first, *operands, *after)


def f32(*shape):
    return jax.ShapeDtypeStruct(shape, jnp.float32)


def probe_kernel(own, probes, acts, cotan, weight, out):
    rows, width = weight.shape
    from_grads = thin(terms(dot(probes[...], cotan[...], NT)[:8]), acts[...], NN)
    from_weight = terms(dot(probes[...], weight[...], NT)[:8])
    placed = thin(from_weight, own_columns(own[0], rows, width), NN)
    out[...] = (placed - LEARN * from_grads)[:4]


def unit_vectors(proj):
    first, second = proj[0:1], proj[1:2]
    unit_first = first * lax.rsqrt(jnp.sum(first * first, keepdims=True) + EPS)
    remain = second - jnp.sum(unit_first * second, keepdims=True) * unit_first
    unit_second = remain * lax.rsqrt(jnp.sum(remain * remain, keepdims=True) + EPS)
    return [unit_first, unit_second]


def basis_kernel(
    own, right, left, from_right, from_left, acts, cotan, weight, out, out_basis
):
    rows, width = weight.shape
    units = unit_vectors(right[...] - from_right[...])
    units += unit_vectors(from_left[...] - left[...])
    row = lax.broadcasted_iota(jnp.int32, (8, width), 0)
    basis = jnp.zeros((8, width), jnp.float32)
    for k, unit in enumerate(units):
        basis = jnp.where(row == k, jnp.broadcast_to(unit, (8, width)), basis)
    parts = terms(basis)
    own_parts = dot(parts, own_columns(own[0], rows, width), NT)
    out_basis[...] = summed(own_parts)
    from_weight = thin(own_parts.astype(jnp.bfloat16), weight[...], NN)
    from_grads = thin(terms(thin(parts, acts[...], NT)), cotan[...], NN)
    out[...] = (from_weight - LEARN * from_grads)[:4]


def add_kernel(left, right, out):
    out[...] = left[...] + right[...]


def add_split_kernel(left, right, out_right, out_left):
    total = left[...] + right[...]
    out_right[...] = total[:2]
    out_left[...] = total[2:]


def partner(value, axis, step):
    count = lax.axis_size(axis)
    return lax.ppermute(value, axis, [(i, i ^ step) for i in range(count)])


def shard_sum(value, steps, after, split=None):
    for axis, step in steps:
        key = axis + str(step)
        operands = (value, partner(value, axis, step))
        if key == split:
            halves = (f32(2, value.shape[1]), f32(2, value.shape[1]))
            value = kernel_call(add_split_kernel, operands, halves, after=after.get(key, ()))
        else:
            value = kernel_call(add_kernel, operands, f32(*value.shape), after=after.get(key, ()))
    return value


def passed_along(value, steps):
    count, row = lax.axis_size(CYCLE), lax.axis_size("y")
    pairs = []
    for source in range(count):
        target = (source + steps) % count
        crossed = int(source // row != target // row)
        pairs += [(2 * source + x, 2 * target + (x ^ crossed)) for x in range(2)]
    return lax.ppermute(value, CYCLE + ("xl",), pairs)


def neighbours(right, left):
    return passed_along(left, -1), passed_along(right, 1)


def coded(value):
    largest = jnp.maximum(jnp.max(jnp.abs(value), 1, keepdims=True), 1e-30)
    level = jnp.ceil(jnp.log2(largest) * LEVELS + 0.01)
    steps = jnp.floor(value * (STEPS * jnp.exp2(level * (-1.0 / LEVELS))) + 0.5)
    steps = jnp.clip(steps, -STEPS, STEPS).astype(jnp.int32)
    level = jnp.broadcast_to(level, (value.shape[0], LANES)).astype(jnp.int32)
    return jnp.concatenate([steps, level], 1).astype(jnp.int16)


def decoded(code):
    code = code.astype(jnp.int32).astype(jnp.float32)
    size = jnp.exp2(code[:, -1:] * (1.0 / LEVELS)) * (1.0 / STEPS)
    return code[:, :-LANES] * size


def product(place, first, count, acts, other_acts, cotan, other_cotan):
    rows = acts.shape[1] // 8

    def columns(ref):
        return jnp.concatenate(
            [ref[:, pl.ds(pl.multiple_of(place[first + k] * rows, rows), rows)] for k in range(count)], 1
        )

    return dot(columns(acts), cotan[...], TN) + dot(columns(other_acts), other_cotan[...], TN)


def chunk_kernel(first, place, acts, other_acts, cotan, other_cotan, *outs):
    rows = acts.shape[1] // 8
    outs, mark = outs[:-1], outs[-1]
    mark[...] = jnp.zeros_like(mark)
    for out in outs:
        count = out.shape[0]
        value = product(place, first, count, acts, other_acts, cotan, other_cotan)
        for k in range(count):
            out[k] = coded(value[k * rows : (k + 1) * rows])
        first += count


def mine_kernel(place, acts, other_acts, cotan, other_cotan, out, mark):
    rows = acts.shape[1] // 8
    mark[...] = jnp.zeros_like(mark)
    for k in range(2):
        value = product(place, 4 * k, 4, acts, other_acts, cotan, other_cotan)
        for j in range(4):
            out[4 * k + j] = value[rows * j : rows * (j + 1)]


def chunks(kernel, out_shape, scalars, acts, other_acts, cotan, other_cotan, after):
    tokens, width = acts.shape
    half = width // 2
    unused = len(after)

    def body(place, *refs):
        kernel(place, *refs[:4], *refs[4 + unused :])

    def spec(shape):
        return pl.BlockSpec(shape, lambda i, at: (0,) * len(shape))

    return pl.pallas_call(
        body,
        grid_spec=pltpu.PrefetchScalarGridSpec(
            num_scalar_prefetch=1,
            grid=(1,),
            in_specs=[
                pl.BlockSpec((tokens, half), lambda i, at: (0, at[8])),
                pl.BlockSpec((tokens, half), lambda i, at: (0, at[8])),
                pl.BlockSpec((tokens, half), lambda i, at: (0, at[9])),
                pl.BlockSpec((tokens, half), lambda i, at: (0, at[9])),
            ]
            + [pl.BlockSpec(memory_space=pltpu.VMEM)] * unused,
            out_specs=jax.tree.map(lambda a: spec(a.shape), out_shape),
        ),
        out_shape=out_shape,
        cost_estimate=NO_COST,
        compiler_params=pltpu.CompilerParams(vmem_limit_bytes=MOST_VMEM),
    )(scalars, acts, other_acts, cotan, other_cotan, *after)


def hop_kernel(step, unused, *refs):
    mine, from_x = refs[:2]
    down = mine[0] + decoded(from_x[0])
    up = mine[1] + decoded(from_x[1])
    if step > 0:
        down = down + decoded(refs[2][...])
        up = up + decoded(refs[3][...])
    refs[-3][...] = coded(down)
    refs[-2][...] = up if step == 3 else coded(up)
    refs[-1][...] = jnp.zeros_like(refs[-1])


def hop(step, mine, from_x, received, after):
    _, rows, columns = mine.shape
    wide = columns + LANES
    whole = pl.BlockSpec((rows, wide), lambda i: (0, 0))
    sent = jax.ShapeDtypeStruct((rows, wide), jnp.int16)
    last = jax.ShapeDtypeStruct((rows, columns), jnp.float32) if step == 3 else sent
    return pl.pallas_call(
        functools.partial(hop_kernel, step, len(after)),
        grid=(1,),
        in_specs=[
            pl.BlockSpec((2, rows, columns), lambda i: (step, 0, 0)),
            pl.BlockSpec((2, rows, wide), lambda i: (step % 2, 0, 0)),
        ]
        + [whole] * len(received)
        + [pl.BlockSpec(memory_space=pltpu.VMEM)] * len(after),
        out_specs=[whole] + [pl.BlockSpec(a.shape, lambda i: (0, 0)) for a in (last, MARK)],
        out_shape=[sent, last, MARK],
        cost_estimate=NO_COST,
        compiler_params=pltpu.CompilerParams(vmem_limit_bytes=VMEM),
    )(mine, from_x, *received, *after)


def total_kernel(core, up, down, kept, given, mark):
    total = up[...] + decoded(down[...])
    mark[...] = jnp.zeros_like(mark)
    rows = kept.shape[0]
    mine = jnp.where(core[0] == 0, 1.0, 0.0)
    kept[...] = jnp.where(mine > 0.5, total[:rows], total[rows:])
    given[...] = jnp.where(mine > 0.5, total[rows:], total[:rows])


def shifted(value, axis, steps):
    count = lax.axis_size(axis)
    return lax.ppermute(value, axis, [(i, (i + steps) % count) for i in range(count)])


def held(value, after, arrays=(), limit=VMEM):
    def body(*refs):
        pass

    anywhere = pl.BlockSpec(memory_space=pl.ANY)
    return pl.pallas_call(
        body,
        in_specs=[anywhere] * (1 + len(arrays))
        + [pl.BlockSpec(memory_space=pltpu.VMEM)] * len(after),
        out_specs=anywhere,
        out_shape=jax.ShapeDtypeStruct(value.shape, value.dtype),
        input_output_aliases={0: 0},
        cost_estimate=NO_COST,
        compiler_params=pltpu.CompilerParams(vmem_limit_bytes=limit),
    )(value, *arrays, *after)


def input_kernel(at, cotan, weights, other_weights, *refs):
    out, mark = refs[-2:]
    mark[...] = jnp.zeros_like(mark)
    column = pl.program_id(1)

    def planes(first, second):
        blocks = [first[column], second[column], first[2 + column], second[2 + column]]
        value = dot(cotan[...], jnp.concatenate(blocks, 0), NT)
        out[...] = value.astype(jnp.bfloat16)

    @pl.when(at[0] == 0)
    def _():
        planes(weights, other_weights)

    @pl.when(at[0] == 1)
    def _():
        planes(other_weights, weights)


def backward_input(core, x, first, cotan, weights, other_weights, after, into=()):
    tokens, width = cotan.shape
    rows = weights.shape[1]
    planes = pl.BlockSpec((4, rows, width), lambda i, j, at: (at[2] + i, 0, 0))
    scalars = jnp.stack([core, x, jnp.full_like(core, first)]).astype(jnp.int32)
    return pl.pallas_call(
        input_kernel,
        grid_spec=pltpu.PrefetchScalarGridSpec(
            num_scalar_prefetch=1,
            grid=(2, 2),
            in_specs=[pl.BlockSpec((tokens, width), lambda i, j, at: (0, 0)), planes, planes]
            + [pl.BlockSpec(memory_space=pl.ANY)] * len(into)
            + [pl.BlockSpec(memory_space=pltpu.VMEM)] * len(after),
            out_specs=[
                pl.BlockSpec(
                    (tokens, width // 8),
                    lambda i, j, at: (0, 4 * (at[1] * (1 - j) + (1 - at[1]) * j) + at[2] + i),
                ),
                pl.BlockSpec(MARK.shape, lambda i, j, at: (0, 0)),
            ],
        ),
        out_shape=[jax.ShapeDtypeStruct((tokens, width), jnp.bfloat16), MARK],
        input_output_aliases={4: 0} if into else {},
        cost_estimate=NO_COST,
        compiler_params=pltpu.CompilerParams(vmem_limit_bytes=NO_ROOM),
    )(scalars, cotan, weights, other_weights, *into, *after)


def update_kernel(core, weight, kept, taken, basis, right, left, from_right, from_left, out, out_q):
    next_right = right[...] - from_right[...]
    next_left = from_left[...] - left[...]
    out_q[...] = next_right
    moves = (
        basis[:, 0:1] * next_right[0:1]
        + basis[:, 1:2] * next_right[1:2]
        - basis[:, 2:3] * next_left[0:1]
        - basis[:, 3:4] * next_left[1:2]
    )
    stepped = weight[...].astype(jnp.float32) - GOSSIP * moves
    columns = kept.shape[1]
    swapped = jnp.broadcast_to(core[0], kept.shape) == 1
    first = jnp.where(swapped, taken[...], kept[...])
    second = jnp.where(swapped, kept[...], taken[...])
    out[:, :columns] = stepped[:, :columns] - LEARN * first
    out[:, columns:] = stepped[:, columns:] - LEARN * second


def on_device(activ, grad_out, weight, q_seed):
    acts = activ[0]
    cotan = grad_out[0]
    weight_bf = weight[0]
    rows, width = weight_bf.shape
    columns = width // 2
    core, x, z = lax.axis_index("core"), lax.axis_index("xl"), lax.axis_index("z")
    own = lax.axis_index(SHARD)
    replica = lax.axis_index(CYCLE)
    cycle_size = lax.axis_size(CYCLE)

    other_acts = partner(acts, "core", 1)
    other_cotan = partner(cotan, "core", 1)
    tokens = (acts, other_acts, cotan, other_cotan)

    q_right = lax.dynamic_index_in_dim(q_seed, replica, 0, keepdims=False)
    q_left = lax.dynamic_index_in_dim(
        q_seed, (replica + cycle_size - 1) % cycle_size, 0, keepdims=False
    )
    probes = jnp.concatenate([q_right, q_left], 1).astype(jnp.bfloat16).T
    probes = jnp.pad(probes, ((0, 12), (0, 0)))
    at = own[None].astype(jnp.int32)
    part = kernel_call(probe_kernel, (probes, acts, cotan, weight_bf), f32(4, width), at)

    place = [(z + offset) % 8 for step in range(4) for offset in (4 + step, 3 - step)]
    scalars = jnp.stack(place + [1 - x, core]).astype(jnp.int32)
    mine_scalars = jnp.stack(place + [x, core]).astype(jnp.int32)
    pieces = jax.ShapeDtypeStruct((4, 2 * rows, columns + LANES), jnp.int16)
    value = shard_sum(part, STEPS_ALONG[:1], {})

    pair = held(
        jnp.stack([weight_bf, partner(weight_bf, "xl", 1)], 0), (value,), (other_acts, other_cotan)
    )
    weights = lax.all_gather(pair, "z", axis=0, tiled=True)

    first, mark = chunks(
        functools.partial(chunk_kernel, 0), (pieces, MARK), scalars, *tokens, (value,)
    )
    value = shard_sum(value, STEPS_ALONG[1:2], {"xl1": (mark,)})
    first = partner(held(first, (value,)), "xl", 1)
    value = shard_sum(value, STEPS_ALONG[2:3], {})
    mine, mark = chunks(
        mine_kernel, (f32(8, 2 * rows, columns), MARK), mine_scalars, *tokens, (value,)
    )

    def hops(step, received, after, from_x):
        down, up, mark = hop(step, mine, from_x, received, after)
        return (shifted(down, "z", -1), shifted(up, "z", 1) if step < 3 else up), (mark,)

    value = shard_sum(value, STEPS_ALONG[3:4], {"z2": (mark,)})
    second, mark = chunks(
        functools.partial(chunk_kernel, 4), (pieces, MARK), scalars, *tokens, (value,)
    )
    right, left = shard_sum(value, STEPS_ALONG[4:], {"z4": (mark,)}, "z4")
    arrived = neighbours(right, left)
    second = partner(held(second, arrived), "xl", 1)
    back, basis = kernel_call(
        basis_kernel,
        (right, left, *arrived, acts, cotan, weight_bf),
        (f32(4, width), f32(8, rows)),
        at,
    )
    value = shard_sum(back, STEPS_BACK[:2], {})
    received, sent = hops(0, (), (value,), first)
    value = shard_sum(value, STEPS_BACK[2:4], {"z2": sent})
    received, sent = hops(1, received, (value,), first)
    right, left = shard_sum(value, STEPS_BACK[4:], {"xl1": sent}, "xl1")
    arrived = neighbours(right, left)
    received, sent = hops(2, received, arrived, second)
    weights = held(weights, sent, (), NO_ROOM)
    both = (cotan, weights, partner(weights, "core", 1))
    half, mark = backward_input(core, x, 0, *both, sent)
    received, sent = hops(3, received, (mark,), second)
    grad_in, mark = backward_input(core, x, 2, *both, sent, (half,))
    kept, given, _ = kernel_call(
        total_kernel,
        (received[1], received[0]),
        (f32(rows, columns), f32(rows, columns), MARK),
        core[None].astype(jnp.int32),
        (mark, *arrived),
    )
    new_weight, next_q = kernel_call(
        update_kernel,
        (weight_bf, kept, partner(given, "core", 1), basis.T, right, left, *arrived),
        (f32(rows, width), f32(2, width)),
        core[None].astype(jnp.int32),
        (mark,),
    )
    return (grad_in[None], new_weight[None], next_q.T[None])


def solution(mesh):
    fine = Mesh(mesh.devices.reshape(2, 4, 2, 8, 2), CYCLE + SHARD)
    tokens = P(CYCLE, SHARD, None)
    return jax.shard_map(
        on_device,
        mesh=fine,
        in_specs=(tokens, tokens, tokens, P()),
        out_specs=(tokens, tokens, P(CYCLE, None, None)),
        check_vma=False,
    )
```

```python
import functools

import jax
import jax.numpy as jnp
from jax import lax
from jax.experimental import pallas as pl
from jax.experimental.pallas import tpu as pltpu
from jax.sharding import Mesh
from jax.sharding import PartitionSpec as P

LEARN = 0.002
GOSSIP = 0.5
EPS = 1e-06
LANES = 128
LEVELS = 64.0
STEPS = 32767.0
VMEM = 16 * 2**20
MOST_VMEM = 24 * 2**20
NO_ROOM = 56 * 2**20
MARK = jax.ShapeDtypeStruct((8, 128), jnp.float32)
NO_COST = pl.CostEstimate(flops=0, bytes_accessed=0, transcendentals=0)
STEPS_ALONG = (("core", 1), ("xl", 1), ("z", 1), ("z", 2), ("z", 4))

CYCLE = ("xh", "y")
SHARD = ("xl", "z", "core")
NT = (((1,), (1,)), ((), ()))
NN = (((1,), (0,)), ((), ()))
TN = (((0,), (0,)), ((), ()))


def dot(left, right, dims):
    return lax.dot_general(left, right, dims, preferred_element_type=jnp.float32)


def terms(value):
    high = value.astype(jnp.bfloat16)
    rest = value - high.astype(jnp.float32)
    middle = rest.astype(jnp.bfloat16)
    low = (rest - middle.astype(jnp.float32)).astype(jnp.bfloat16)
    parts = [part.astype(jnp.float32) for part in (high, middle, low)]
    return jnp.concatenate(parts, 0).astype(jnp.bfloat16)


def summed(value):
    return value[:8] + (value[8:16] + value[16:])


def thin(left, right, dims):
    return summed(dot(left, right, dims))


def own_columns(own, rows, width):
    row = lax.broadcasted_iota(jnp.int32, (rows, width), 0) + own * rows
    column = lax.broadcasted_iota(jnp.int32, (rows, width), 1)
    return jnp.where(row == column, 1.0, 0.0).astype(jnp.bfloat16)


def kernel_call(kernel, operands, out_shape, scalars=None, after=()):
    whole = pl.BlockSpec(memory_space=pltpu.VMEM)
    specs = [whole] * (len(operands) + len(after))
    first = []
    if scalars is not None:
        specs, first = [pl.BlockSpec(memory_space=pltpu.SMEM)] + specs, [scalars]
    lead, unused = len(first) + len(operands), len(after)

    def body(*refs):
        kernel(*refs[:lead], *refs[lead + unused :])

    return pl.pallas_call(
        body,
        in_specs=specs,
        out_specs=jax.tree.map(lambda _: whole, out_shape),
        out_shape=out_shape,
        cost_estimate=NO_COST,
        compiler_params=pltpu.CompilerParams(vmem_limit_bytes=VMEM),
    )(*first, *operands, *after)


def f32(*shape):
    return jax.ShapeDtypeStruct(shape, jnp.float32)


def probe_kernel(own, probes, acts, cotan, weight, out):
    rows, width = weight.shape
    from_grads = thin(terms(dot(probes[...], cotan[...], NT)[:8]), acts[...], NN)
    from_weight = terms(dot(probes[...], weight[...], NT)[:8])
    placed = thin(from_weight, own_columns(own[0], rows, width), NN)
    out[...] = (placed - LEARN * from_grads)[:4]


def unit_vectors(proj):
    first, second = proj[0:1], proj[1:2]
    unit_first = first * lax.rsqrt(jnp.sum(first * first, keepdims=True) + EPS)
    remain = second - jnp.sum(unit_first * second, keepdims=True) * unit_first
    unit_second = remain * lax.rsqrt(jnp.sum(remain * remain, keepdims=True) + EPS)
    return [unit_first, unit_second]


def basis_kernel(
    own, right, left, from_right, from_left, acts, cotan, weight, out, out_basis
):
    rows, width = weight.shape
    units = unit_vectors(right[...] - from_right[...])
    units += unit_vectors(from_left[...] - left[...])
    row = lax.broadcasted_iota(jnp.int32, (8, width), 0)
    basis = jnp.zeros((8, width), jnp.float32)
    for k, unit in enumerate(units):
        basis = jnp.where(row == k, jnp.broadcast_to(unit, (8, width)), basis)
    parts = terms(basis)
    own_parts = dot(parts, own_columns(own[0], rows, width), NT)
    out_basis[...] = summed(own_parts)
    from_weight = thin(own_parts.astype(jnp.bfloat16), weight[...], NN)
    from_grads = thin(terms(thin(parts, acts[...], NT)), cotan[...], NN)
    out[...] = (from_weight - LEARN * from_grads)[:4]


def add_kernel(left, right, out):
    out[...] = left[...] + right[...]


def add_split_kernel(left, right, out_right, out_left):
    total = left[...] + right[...]
    out_right[...] = total[:2]
    out_left[...] = total[2:]


def partner(value, axis, step):
    count = lax.axis_size(axis)
    return lax.ppermute(value, axis, [(i, i ^ step) for i in range(count)])


def shard_sum(value, steps, after, split=None):
    for axis, step in steps:
        key = axis + str(step)
        operands = (value, partner(value, axis, step))
        if key == split:
            halves = (f32(2, value.shape[1]), f32(2, value.shape[1]))
            value = kernel_call(add_split_kernel, operands, halves, after=after.get(key, ()))
        else:
            value = kernel_call(add_kernel, operands, f32(*value.shape), after=after.get(key, ()))
    return value


def passed_along(value, steps):
    count, row = lax.axis_size(CYCLE), lax.axis_size("y")
    pairs = []
    for source in range(count):
        target = (source + steps) % count
        crossed = int(source // row != target // row)
        pairs += [(2 * source + x, 2 * target + (x ^ crossed)) for x in range(2)]
    return lax.ppermute(value, CYCLE + ("xl",), pairs)


def neighbours(right, left):
    return passed_along(left, -1), passed_along(right, 1)


def coded(value):
    largest = jnp.maximum(jnp.max(jnp.abs(value), 1, keepdims=True), 1e-30)
    level = jnp.ceil(jnp.log2(largest) * LEVELS + 0.01)
    steps = jnp.floor(value * (STEPS * jnp.exp2(level * (-1.0 / LEVELS))) + 0.5)
    steps = jnp.clip(steps, -STEPS, STEPS).astype(jnp.int32)
    level = jnp.broadcast_to(level, (value.shape[0], LANES)).astype(jnp.int32)
    return jnp.concatenate([steps, level], 1).astype(jnp.int16)


def decoded(code):
    code = code.astype(jnp.int32).astype(jnp.float32)
    size = jnp.exp2(code[:, -1:] * (1.0 / LEVELS)) * (1.0 / STEPS)
    return code[:, :-LANES] * size


def product(place, first, count, acts, other_acts, cotan, other_cotan):
    rows = acts.shape[1] // 8

    def columns(ref):
        return jnp.concatenate(
            [ref[:, pl.ds(pl.multiple_of(place[first + k] * rows, rows), rows)] for k in range(count)], 1
        )

    return dot(columns(acts), cotan[...], TN) + dot(columns(other_acts), other_cotan[...], TN)


def chunk_kernel(first, place, acts, other_acts, cotan, other_cotan, *outs):
    rows = acts.shape[1] // 8
    outs, mark = outs[:-1], outs[-1]
    mark[...] = jnp.zeros_like(mark)
    for out in outs:
        count = out.shape[0]
        value = product(place, first, count, acts, other_acts, cotan, other_cotan)
        for k in range(count):
            out[k] = coded(value[k * rows : (k + 1) * rows])
        first += count


def mine_kernel(place, acts, other_acts, cotan, other_cotan, out, mark):
    rows = acts.shape[1] // 8
    mark[...] = jnp.zeros_like(mark)
    for k in range(2):
        value = product(place, 4 * k, 4, acts, other_acts, cotan, other_cotan)
        for j in range(4):
            out[4 * k + j] = value[rows * j : rows * (j + 1)]


def chunks(kernel, out_shape, scalars, acts, other_acts, cotan, other_cotan, after):
    tokens, width = acts.shape
    half = width // 2
    unused = len(after)

    def body(place, *refs):
        kernel(place, *refs[:4], *refs[4 + unused :])

    def spec(shape):
        return pl.BlockSpec(shape, lambda i, at: (0,) * len(shape))

    return pl.pallas_call(
        body,
        grid_spec=pltpu.PrefetchScalarGridSpec(
            num_scalar_prefetch=1,
            grid=(1,),
            in_specs=[
                pl.BlockSpec((tokens, half), lambda i, at: (0, at[8])),
                pl.BlockSpec((tokens, half), lambda i, at: (0, at[8])),
                pl.BlockSpec((tokens, half), lambda i, at: (0, at[9])),
                pl.BlockSpec((tokens, half), lambda i, at: (0, at[9])),
            ]
            + [pl.BlockSpec(memory_space=pltpu.VMEM)] * unused,
            out_specs=jax.tree.map(lambda a: spec(a.shape), out_shape),
        ),
        out_shape=out_shape,
        cost_estimate=NO_COST,
        compiler_params=pltpu.CompilerParams(vmem_limit_bytes=MOST_VMEM),
    )(scalars, acts, other_acts, cotan, other_cotan, *after)


def hop_kernel(step, unused, *refs):
    mine, from_x = refs[:2]
    down = mine[0] + decoded(from_x[0])
    up = mine[1] + decoded(from_x[1])
    if step > 0:
        down = down + decoded(refs[2][...])
        up = up + decoded(refs[3][...])
    refs[-3][...] = coded(down)
    refs[-2][...] = up if step == 3 else coded(up)
    refs[-1][...] = jnp.zeros_like(refs[-1])


def hop(step, mine, from_x, received, after):
    _, rows, columns = mine.shape
    wide = columns + LANES
    whole = pl.BlockSpec((rows, wide), lambda i: (0, 0))
    sent = jax.ShapeDtypeStruct((rows, wide), jnp.int16)
    last = jax.ShapeDtypeStruct((rows, columns), jnp.float32) if step == 3 else sent
    return pl.pallas_call(
        functools.partial(hop_kernel, step, len(after)),
        grid=(1,),
        in_specs=[
            pl.BlockSpec((2, rows, columns), lambda i: (step, 0, 0)),
            pl.BlockSpec((2, rows, wide), lambda i: (step if step < 2 else 0, 0, 0)),
        ]
        + [whole] * len(received)
        + [pl.BlockSpec(memory_space=pltpu.VMEM)] * len(after),
        out_specs=[whole] + [pl.BlockSpec(a.shape, lambda i: (0, 0)) for a in (last, MARK)],
        out_shape=[sent, last, MARK],
        cost_estimate=NO_COST,
        compiler_params=pltpu.CompilerParams(vmem_limit_bytes=VMEM),
    )(mine, from_x, *received, *after)


def total_kernel(core, up, down, kept, given, mark):
    total = up[...] + decoded(down[...])
    mark[...] = jnp.zeros_like(mark)
    rows = kept.shape[0]
    mine = jnp.where(core[0] == 0, 1.0, 0.0)
    kept[...] = jnp.where(mine > 0.5, total[:rows], total[rows:])
    given[...] = jnp.where(mine > 0.5, total[rows:], total[:rows])


def shifted(value, axis, steps):
    count = lax.axis_size(axis)
    return lax.ppermute(value, axis, [(i, (i + steps) % count) for i in range(count)])


def held(value, after, arrays=(), limit=VMEM):
    def body(*refs):
        pass

    anywhere = pl.BlockSpec(memory_space=pl.ANY)
    return pl.pallas_call(
        body,
        in_specs=[anywhere] * (1 + len(arrays))
        + [pl.BlockSpec(memory_space=pltpu.VMEM)] * len(after),
        out_specs=anywhere,
        out_shape=jax.ShapeDtypeStruct(value.shape, value.dtype),
        input_output_aliases={0: 0},
        cost_estimate=NO_COST,
        compiler_params=pltpu.CompilerParams(vmem_limit_bytes=limit),
    )(value, *arrays, *after)


def input_kernel(at, cotan, weights, other_weights, *refs):
    out, mark = refs[-2:]
    mark[...] = jnp.zeros_like(mark)
    column = pl.program_id(1)

    def planes(first, second):
        blocks = [first[column], second[column], first[2 + column], second[2 + column]]
        value = dot(cotan[...], jnp.concatenate(blocks, 0), NT)
        out[...] = value.astype(jnp.bfloat16)

    @pl.when(at[0] == 0)
    def _():
        planes(weights, other_weights)

    @pl.when(at[0] == 1)
    def _():
        planes(other_weights, weights)


def backward_input(core, x, first, cotan, weights, other_weights, after, into=()):
    tokens, width = cotan.shape
    rows = weights.shape[1]
    planes = pl.BlockSpec((4, rows, width), lambda i, j, at: (at[2] + i, 0, 0))
    scalars = jnp.stack([core, x, jnp.full_like(core, first)]).astype(jnp.int32)
    return pl.pallas_call(
        input_kernel,
        grid_spec=pltpu.PrefetchScalarGridSpec(
            num_scalar_prefetch=1,
            grid=(2, 2),
            in_specs=[pl.BlockSpec((tokens, width), lambda i, j, at: (0, 0)), planes, planes]
            + [pl.BlockSpec(memory_space=pl.ANY)] * len(into)
            + [pl.BlockSpec(memory_space=pltpu.VMEM)] * len(after),
            out_specs=[
                pl.BlockSpec(
                    (tokens, width // 8),
                    lambda i, j, at: (0, 4 * (at[1] * (1 - j) + (1 - at[1]) * j) + at[2] + i),
                ),
                pl.BlockSpec(MARK.shape, lambda i, j, at: (0, 0)),
            ],
        ),
        out_shape=[jax.ShapeDtypeStruct((tokens, width), jnp.bfloat16), MARK],
        input_output_aliases={4: 0} if into else {},
        cost_estimate=NO_COST,
        compiler_params=pltpu.CompilerParams(vmem_limit_bytes=NO_ROOM),
    )(scalars, cotan, weights, other_weights, *into, *after)


def update_kernel(core, weight, kept, taken, basis, right, left, from_right, from_left, out, out_q):
    next_right = right[...] - from_right[...]
    next_left = from_left[...] - left[...]
    out_q[...] = next_right
    moves = (
        basis[:, 0:1] * next_right[0:1]
        + basis[:, 1:2] * next_right[1:2]
        - basis[:, 2:3] * next_left[0:1]
        - basis[:, 3:4] * next_left[1:2]
    )
    stepped = weight[...].astype(jnp.float32) - GOSSIP * moves
    columns = kept.shape[1]
    swapped = jnp.broadcast_to(core[0], kept.shape) == 1
    first = jnp.where(swapped, taken[...], kept[...])
    second = jnp.where(swapped, kept[...], taken[...])
    out[:, :columns] = stepped[:, :columns] - LEARN * first
    out[:, columns:] = stepped[:, columns:] - LEARN * second


def on_device(activ, grad_out, weight, q_seed):
    acts = activ[0]
    cotan = grad_out[0]
    weight_bf = weight[0]
    rows, width = weight_bf.shape
    columns = width // 2
    core, x, z = lax.axis_index("core"), lax.axis_index("xl"), lax.axis_index("z")
    own = lax.axis_index(SHARD)
    replica = lax.axis_index(CYCLE)
    cycle_size = lax.axis_size(CYCLE)

    other_acts = partner(acts, "core", 1)
    other_cotan = partner(cotan, "core", 1)
    tokens = (acts, other_acts, cotan, other_cotan)

    q_right = lax.dynamic_index_in_dim(q_seed, replica, 0, keepdims=False)
    q_left = lax.dynamic_index_in_dim(
        q_seed, (replica + cycle_size - 1) % cycle_size, 0, keepdims=False
    )
    probes = jnp.concatenate([q_right, q_left], 1).astype(jnp.bfloat16).T
    probes = jnp.pad(probes, ((0, 12), (0, 0)))
    at = own[None].astype(jnp.int32)
    part = kernel_call(probe_kernel, (probes, acts, cotan, weight_bf), f32(4, width), at)

    place = [(z + offset) % 8 for step in range(4) for offset in (4 + step, 3 - step)]
    scalars = jnp.stack(place + [1 - x, core]).astype(jnp.int32)
    mine_scalars = jnp.stack(place + [x, core]).astype(jnp.int32)
    pieces = jax.ShapeDtypeStruct((4, 2 * rows, columns + LANES), jnp.int16)
    value = shard_sum(part, STEPS_ALONG[:1], {})

    pair = held(
        jnp.stack([weight_bf, partner(weight_bf, "xl", 1)], 0), (value,), (other_acts, other_cotan)
    )
    weights = lax.all_gather(pair, "z", axis=0, tiled=True)

    first, mark = chunks(
        functools.partial(chunk_kernel, 0), (pieces, MARK), scalars, *tokens, (value,)
    )
    value = shard_sum(value, STEPS_ALONG[1:2], {"xl1": (mark,)})
    first = partner(held(first, (value,)), "xl", 1)
    value = shard_sum(value, STEPS_ALONG[2:3], {})
    mine, mark = chunks(
        mine_kernel, (f32(8, 2 * rows, columns), MARK), mine_scalars, *tokens, (value,)
    )

    def hops(step, received, after, from_x):
        down, up, mark = hop(step, mine, from_x, received, after)
        return (shifted(down, "z", -1), shifted(up, "z", 1) if step < 3 else up), (mark,)

    value = shard_sum(value, STEPS_ALONG[3:4], {"z2": (mark,)})
    piece = jax.ShapeDtypeStruct((2, 2 * rows, columns + LANES), jnp.int16)
    second, third, mark = chunks(
        functools.partial(chunk_kernel, 4), (piece, piece, MARK), scalars, *tokens, (value,)
    )
    right, left = shard_sum(value, STEPS_ALONG[4:], {"z4": (mark,)}, "z4")
    arrived = neighbours(right, left)
    received, sent = hops(0, (), arrived, first)
    second = partner(held(second, sent), "xl", 1)
    back, basis = kernel_call(
        basis_kernel,
        (right, left, *arrived, acts, cotan, weight_bf),
        (f32(4, width), f32(8, rows)),
        at,
        sent,
    )
    value = shard_sum(back, STEPS_ALONG[:2], {})
    third = partner(held(third, (value,)), "xl", 1)
    value = shard_sum(value, STEPS_ALONG[2:3], {})
    received, sent = hops(1, received, (value,), first)
    value = shard_sum(value, STEPS_ALONG[3:4], {"z2": sent})
    received, sent = hops(2, received, (value,), second)
    weights = held(weights, sent, (), NO_ROOM)
    both = (cotan, weights, partner(weights, "core", 1))
    half, mark = backward_input(core, x, 0, *both, sent)
    right, left = shard_sum(value, STEPS_ALONG[4:], {"z4": (mark,)}, "z4")
    received, sent = hops(3, received, (right,), third)
    arrived = neighbours(right, left)
    grad_in, mark = backward_input(core, x, 2, *both, sent, (half,))
    kept, given, _ = kernel_call(
        total_kernel,
        (received[1], received[0]),
        (f32(rows, columns), f32(rows, columns), MARK),
        core[None].astype(jnp.int32),
        (mark, *arrived),
    )
    new_weight, next_q = kernel_call(
        update_kernel,
        (weight_bf, kept, partner(given, "core", 1), basis.T, right, left, *arrived),
        (f32(rows, width), f32(2, width)),
        core[None].astype(jnp.int32),
        (mark,),
    )
    return (grad_in[None], new_weight[None], next_q.T[None])


def solution(mesh):
    fine = Mesh(mesh.devices.reshape(2, 4, 2, 8, 2), CYCLE + SHARD)
    tokens = P(CYCLE, SHARD, None)
    return jax.shard_map(
        on_device,
        mesh=fine,
        in_specs=(tokens, tokens, tokens, P()),
        out_specs=(tokens, tokens, P(CYCLE, None, None)),
        check_vma=False,
    )
```

```python
import functools

import jax
import jax.numpy as jnp
from jax import lax
from jax.experimental import pallas as pl
from jax.experimental.pallas import tpu as pltpu
from jax.sharding import Mesh
from jax.sharding import PartitionSpec as P

LEARN = 0.002
GOSSIP = 0.5
EPS = 1e-06
LANES = 128
LEVELS = 64.0
STEPS = 32767.0
VMEM = 16 * 2**20
MOST_VMEM = 24 * 2**20
NO_ROOM = 52 * 2**20
MARK = jax.ShapeDtypeStruct((8, 128), jnp.float32)
NO_COST = pl.CostEstimate(flops=0, bytes_accessed=0, transcendentals=0)
STEPS_ALONG = (("core", 1), ("xl", 1), ("z", 1), ("z", 2), ("z", 4))

CYCLE = ("xh", "y")
SHARD = ("xl", "z", "core")
NT = (((1,), (1,)), ((), ()))
NN = (((1,), (0,)), ((), ()))
TN = (((0,), (0,)), ((), ()))


def dot(left, right, dims):
    return lax.dot_general(left, right, dims, preferred_element_type=jnp.float32)


def terms(value):
    high = value.astype(jnp.bfloat16)
    rest = value - high.astype(jnp.float32)
    middle = rest.astype(jnp.bfloat16)
    low = (rest - middle.astype(jnp.float32)).astype(jnp.bfloat16)
    parts = [part.astype(jnp.float32) for part in (high, middle, low)]
    return jnp.concatenate(parts, 0).astype(jnp.bfloat16)


def summed(value):
    return value[:8] + (value[8:16] + value[16:])


def thin(left, right, dims):
    return summed(dot(left, right, dims))


def own_columns(own, rows, width):
    row = lax.broadcasted_iota(jnp.int32, (rows, width), 0) + own * rows
    column = lax.broadcasted_iota(jnp.int32, (rows, width), 1)
    return jnp.where(row == column, 1.0, 0.0).astype(jnp.bfloat16)


def kernel_call(kernel, operands, out_shape, scalars=None, after=()):
    whole = pl.BlockSpec(memory_space=pltpu.VMEM)
    specs = [whole] * (len(operands) + len(after))
    first = []
    if scalars is not None:
        specs, first = [pl.BlockSpec(memory_space=pltpu.SMEM)] + specs, [scalars]
    lead, unused = len(first) + len(operands), len(after)

    def body(*refs):
        kernel(*refs[:lead], *refs[lead + unused :])

    return pl.pallas_call(
        body,
        in_specs=specs,
        out_specs=jax.tree.map(lambda _: whole, out_shape),
        out_shape=out_shape,
        cost_estimate=NO_COST,
        compiler_params=pltpu.CompilerParams(vmem_limit_bytes=VMEM),
    )(*first, *operands, *after)


def f32(*shape):
    return jax.ShapeDtypeStruct(shape, jnp.float32)


def probe_kernel(own, probes, acts, cotan, weight, out):
    rows, width = weight.shape
    from_grads = thin(terms(dot(probes[...], cotan[...], NT)[:8]), acts[...], NN)
    from_weight = terms(dot(probes[...], weight[...], NT)[:8])
    placed = thin(from_weight, own_columns(own[0], rows, width), NN)
    out[...] = (placed - LEARN * from_grads)[:4]


def unit_vectors(proj):
    first, second = proj[0:1], proj[1:2]
    unit_first = first * lax.rsqrt(jnp.sum(first * first, keepdims=True) + EPS)
    remain = second - jnp.sum(unit_first * second, keepdims=True) * unit_first
    unit_second = remain * lax.rsqrt(jnp.sum(remain * remain, keepdims=True) + EPS)
    return [unit_first, unit_second]


def basis_kernel(
    own, right, left, from_right, from_left, acts, cotan, weight, out, out_basis
):
    rows, width = weight.shape
    units = unit_vectors(right[...] - from_right[...])
    units += unit_vectors(from_left[...] - left[...])
    row = lax.broadcasted_iota(jnp.int32, (8, width), 0)
    basis = jnp.zeros((8, width), jnp.float32)
    for k, unit in enumerate(units):
        basis = jnp.where(row == k, jnp.broadcast_to(unit, (8, width)), basis)
    parts = terms(basis)
    own_parts = dot(parts, own_columns(own[0], rows, width), NT)
    out_basis[...] = summed(own_parts)
    from_weight = thin(own_parts.astype(jnp.bfloat16), weight[...], NN)
    from_grads = thin(terms(thin(parts, acts[...], NT)), cotan[...], NN)
    out[...] = (from_weight - LEARN * from_grads)[:4]


def add_kernel(left, right, out):
    out[...] = left[...] + right[...]


def add_split_kernel(left, right, out_right, out_left):
    total = left[...] + right[...]
    out_right[...] = total[:2]
    out_left[...] = total[2:]


def partner(value, axis, step):
    count = lax.axis_size(axis)
    return lax.ppermute(value, axis, [(i, i ^ step) for i in range(count)])


def shard_sum(value, steps, after, split=None):
    for axis, step in steps:
        key = axis + str(step)
        operands = (value, partner(value, axis, step))
        if key == split:
            halves = (f32(2, value.shape[1]), f32(2, value.shape[1]))
            value = kernel_call(add_split_kernel, operands, halves, after=after.get(key, ()))
        else:
            value = kernel_call(add_kernel, operands, f32(*value.shape), after=after.get(key, ()))
    return value


def passed_along(value, steps):
    count, row = lax.axis_size(CYCLE), lax.axis_size("y")
    pairs = []
    for source in range(count):
        target = (source + steps) % count
        crossed = int(source // row != target // row)
        pairs += [(2 * source + x, 2 * target + (x ^ crossed)) for x in range(2)]
    return lax.ppermute(value, CYCLE + ("xl",), pairs)


def neighbours(right, left):
    return passed_along(left, -1), passed_along(right, 1)


def coded(value):
    largest = jnp.maximum(jnp.max(jnp.abs(value), 1, keepdims=True), 1e-30)
    level = jnp.ceil(jnp.log2(largest) * LEVELS + 0.01)
    steps = jnp.floor(value * (STEPS * jnp.exp2(level * (-1.0 / LEVELS))) + 0.5)
    steps = jnp.clip(steps, -STEPS, STEPS).astype(jnp.int32)
    level = jnp.broadcast_to(level, (value.shape[0], LANES)).astype(jnp.int32)
    return jnp.concatenate([steps, level], 1).astype(jnp.int16)


def decoded(code):
    code = code.astype(jnp.int32).astype(jnp.float32)
    size = jnp.exp2(code[:, -1:] * (1.0 / LEVELS)) * (1.0 / STEPS)
    return code[:, :-LANES] * size


def product(place, first, count, acts, other_acts, cotan, other_cotan):
    rows = acts.shape[1] // 8

    def columns(ref):
        return jnp.concatenate(
            [ref[:, pl.ds(pl.multiple_of(place[first + k] * rows, rows), rows)] for k in range(count)], 1
        )

    return dot(columns(acts), cotan[...], TN) + dot(columns(other_acts), other_cotan[...], TN)


def chunk_kernel(first, place, acts, other_acts, cotan, other_cotan, *outs):
    rows = acts.shape[1] // 8
    outs, mark = outs[:-1], outs[-1]
    mark[...] = jnp.zeros_like(mark)
    for out in outs:
        count = out.shape[0]
        value = product(place, first, count, acts, other_acts, cotan, other_cotan)
        for k in range(count):
            out[k] = coded(value[k * rows : (k + 1) * rows])
        first += count


def mine_kernel(place, acts, other_acts, cotan, other_cotan, out, mark):
    rows = acts.shape[1] // 8
    mark[...] = jnp.zeros_like(mark)
    for k in range(2):
        value = product(place, 4 * k, 4, acts, other_acts, cotan, other_cotan)
        for j in range(4):
            out[4 * k + j] = value[rows * j : rows * (j + 1)]


def chunks(kernel, out_shape, scalars, acts, other_acts, cotan, other_cotan, after):
    tokens, width = acts.shape
    half = width // 2
    unused = len(after)

    def body(place, *refs):
        kernel(place, *refs[:4], *refs[4 + unused :])

    def spec(shape):
        return pl.BlockSpec(shape, lambda i, at: (0,) * len(shape))

    return pl.pallas_call(
        body,
        grid_spec=pltpu.PrefetchScalarGridSpec(
            num_scalar_prefetch=1,
            grid=(1,),
            in_specs=[
                pl.BlockSpec((tokens, half), lambda i, at: (0, at[8])),
                pl.BlockSpec((tokens, half), lambda i, at: (0, at[8])),
                pl.BlockSpec((tokens, half), lambda i, at: (0, at[9])),
                pl.BlockSpec((tokens, half), lambda i, at: (0, at[9])),
            ]
            + [pl.BlockSpec(memory_space=pltpu.VMEM)] * unused,
            out_specs=jax.tree.map(lambda a: spec(a.shape), out_shape),
        ),
        out_shape=out_shape,
        cost_estimate=NO_COST,
        compiler_params=pltpu.CompilerParams(vmem_limit_bytes=MOST_VMEM),
    )(scalars, acts, other_acts, cotan, other_cotan, *after)


def hop_kernel(step, unused, *refs):
    mine, from_x = refs[:2]
    down = mine[0] + decoded(from_x[0])
    up = mine[1] + decoded(from_x[1])
    if step > 0:
        down = down + decoded(refs[2][...])
        up = up + decoded(refs[3][...])
    refs[-3][...] = coded(down)
    refs[-2][...] = up if step == 3 else coded(up)
    refs[-1][...] = jnp.zeros_like(refs[-1])


def hop(step, mine, from_x, received, after):
    _, rows, columns = mine.shape
    wide = columns + LANES
    whole = pl.BlockSpec((rows, wide), lambda i: (0, 0))
    sent = jax.ShapeDtypeStruct((rows, wide), jnp.int16)
    last = jax.ShapeDtypeStruct((rows, columns), jnp.float32) if step == 3 else sent
    return pl.pallas_call(
        functools.partial(hop_kernel, step, len(after)),
        grid=(1,),
        in_specs=[
            pl.BlockSpec((2, rows, columns), lambda i: (step, 0, 0)),
            pl.BlockSpec((2, rows, wide), lambda i: (step if step < 2 else 0, 0, 0)),
        ]
        + [whole] * len(received)
        + [pl.BlockSpec(memory_space=pltpu.VMEM)] * len(after),
        out_specs=[whole] + [pl.BlockSpec(a.shape, lambda i: (0, 0)) for a in (last, MARK)],
        out_shape=[sent, last, MARK],
        cost_estimate=NO_COST,
        compiler_params=pltpu.CompilerParams(vmem_limit_bytes=VMEM),
    )(mine, from_x, *received, *after)


def total_kernel(core, up, down, kept, given, mark):
    total = up[...] + decoded(down[...])
    mark[...] = jnp.zeros_like(mark)
    rows = kept.shape[0]
    mine = jnp.where(core[0] == 0, 1.0, 0.0)
    kept[...] = jnp.where(mine > 0.5, total[:rows], total[rows:])
    given[...] = jnp.where(mine > 0.5, total[rows:], total[:rows])


def shifted(value, axis, steps):
    count = lax.axis_size(axis)
    return lax.ppermute(value, axis, [(i, (i + steps) % count) for i in range(count)])


def held(value, after, arrays=(), limit=VMEM):
    def body(*refs):
        pass

    anywhere = pl.BlockSpec(memory_space=pl.ANY)
    return pl.pallas_call(
        body,
        in_specs=[anywhere] * (1 + len(arrays))
        + [pl.BlockSpec(memory_space=pltpu.VMEM)] * len(after),
        out_specs=anywhere,
        out_shape=jax.ShapeDtypeStruct(value.shape, value.dtype),
        input_output_aliases={0: 0},
        cost_estimate=NO_COST,
        compiler_params=pltpu.CompilerParams(vmem_limit_bytes=limit),
    )(value, *arrays, *after)


def input_kernel(at, cotan, weights, other_weights, *refs):
    out, mark = refs[-2:]
    mark[...] = jnp.zeros_like(mark)
    column = pl.program_id(1)

    def planes(first, second):
        blocks = [first[column], second[column], first[2 + column], second[2 + column]]
        value = dot(cotan[...], jnp.concatenate(blocks, 0), NT)
        out[...] = value.astype(jnp.bfloat16)

    @pl.when(at[0] == 0)
    def _():
        planes(weights, other_weights)

    @pl.when(at[0] == 1)
    def _():
        planes(other_weights, weights)


def backward_input(core, x, first, cotan, weights, other_weights, after, into=()):
    tokens, width = cotan.shape
    rows = weights.shape[1]
    planes = pl.BlockSpec((4, rows, width), lambda i, j, at: (at[2] + i, 0, 0))
    scalars = jnp.stack([core, x, jnp.full_like(core, first)]).astype(jnp.int32)
    return pl.pallas_call(
        input_kernel,
        grid_spec=pltpu.PrefetchScalarGridSpec(
            num_scalar_prefetch=1,
            grid=(2, 2),
            in_specs=[pl.BlockSpec((tokens, width), lambda i, j, at: (0, 0)), planes, planes]
            + [pl.BlockSpec(memory_space=pl.ANY)] * len(into)
            + [pl.BlockSpec(memory_space=pltpu.VMEM)] * len(after),
            out_specs=[
                pl.BlockSpec(
                    (tokens, width // 8),
                    lambda i, j, at: (0, 4 * (at[1] * (1 - j) + (1 - at[1]) * j) + at[2] + i),
                ),
                pl.BlockSpec(MARK.shape, lambda i, j, at: (0, 0)),
            ],
        ),
        out_shape=[jax.ShapeDtypeStruct((tokens, width), jnp.bfloat16), MARK],
        input_output_aliases={4: 0} if into else {},
        cost_estimate=NO_COST,
        compiler_params=pltpu.CompilerParams(vmem_limit_bytes=NO_ROOM),
    )(scalars, cotan, weights, other_weights, *into, *after)


def update_kernel(core, weight, kept, taken, basis, right, left, from_right, from_left, out, out_q):
    next_right = right[...] - from_right[...]
    next_left = from_left[...] - left[...]
    out_q[...] = next_right
    moves = (
        basis[:, 0:1] * next_right[0:1]
        + basis[:, 1:2] * next_right[1:2]
        - basis[:, 2:3] * next_left[0:1]
        - basis[:, 3:4] * next_left[1:2]
    )
    stepped = weight[...].astype(jnp.float32) - GOSSIP * moves
    columns = kept.shape[1]
    swapped = jnp.broadcast_to(core[0], kept.shape) == 1
    first = jnp.where(swapped, taken[...], kept[...])
    second = jnp.where(swapped, kept[...], taken[...])
    out[:, :columns] = stepped[:, :columns] - LEARN * first
    out[:, columns:] = stepped[:, columns:] - LEARN * second


def on_device(activ, grad_out, weight, q_seed):
    acts = activ[0]
    cotan = grad_out[0]
    weight_bf = weight[0]
    rows, width = weight_bf.shape
    columns = width // 2
    core, x, z = lax.axis_index("core"), lax.axis_index("xl"), lax.axis_index("z")
    own = lax.axis_index(SHARD)
    replica = lax.axis_index(CYCLE)
    cycle_size = lax.axis_size(CYCLE)

    other_acts = partner(acts, "core", 1)
    other_cotan = partner(cotan, "core", 1)
    tokens = (acts, other_acts, cotan, other_cotan)

    q_right = lax.dynamic_index_in_dim(q_seed, replica, 0, keepdims=False)
    q_left = lax.dynamic_index_in_dim(
        q_seed, (replica + cycle_size - 1) % cycle_size, 0, keepdims=False
    )
    probes = jnp.concatenate([q_right, q_left], 1).astype(jnp.bfloat16).T
    probes = jnp.pad(probes, ((0, 12), (0, 0)))
    at = own[None].astype(jnp.int32)
    part = kernel_call(probe_kernel, (probes, acts, cotan, weight_bf), f32(4, width), at)

    place = [(z + offset) % 8 for step in range(4) for offset in (4 + step, 3 - step)]
    scalars = jnp.stack(place + [1 - x, core]).astype(jnp.int32)
    mine_scalars = jnp.stack(place + [x, core]).astype(jnp.int32)
    pieces = jax.ShapeDtypeStruct((4, 2 * rows, columns + LANES), jnp.int16)
    value = shard_sum(part, STEPS_ALONG[:1], {})

    pair = held(
        jnp.stack([weight_bf, partner(weight_bf, "xl", 1)], 0), (value,), (other_acts, other_cotan)
    )
    weights = lax.all_gather(pair, "z", axis=0, tiled=True)

    first, mark = chunks(
        functools.partial(chunk_kernel, 0), (pieces, MARK), scalars, *tokens, (value,)
    )
    value = shard_sum(value, STEPS_ALONG[1:2], {"xl1": (mark,)})
    first = partner(held(first, (value,)), "xl", 1)
    value = shard_sum(value, STEPS_ALONG[2:3], {})
    mine, mark = chunks(
        mine_kernel, (f32(8, 2 * rows, columns), MARK), mine_scalars, *tokens, (value,)
    )

    def hops(step, received, after, from_x):
        down, up, mark = hop(step, mine, from_x, received, after)
        return (shifted(down, "z", -1), shifted(up, "z", 1) if step < 3 else up), (mark,)

    value = shard_sum(value, STEPS_ALONG[3:4], {"z2": (mark,)})
    piece = jax.ShapeDtypeStruct((2, 2 * rows, columns + LANES), jnp.int16)
    second, third, mark = chunks(
        functools.partial(chunk_kernel, 4), (piece, piece, MARK), scalars, *tokens, (value,)
    )
    right, left = shard_sum(value, STEPS_ALONG[4:], {"z4": (mark,)}, "z4")
    arrived = neighbours(right, left)
    received, sent = hops(0, (), arrived, first)
    second = partner(held(second, sent), "xl", 1)
    back, basis = kernel_call(
        basis_kernel,
        (right, left, *arrived, acts, cotan, weight_bf),
        (f32(4, width), f32(8, rows)),
        at,
        sent,
    )
    value = shard_sum(back, STEPS_ALONG[:2], {})
    third = partner(held(third, (value,)), "xl", 1)
    value = shard_sum(value, STEPS_ALONG[2:3], {})
    received, sent = hops(1, received, (value,), first)
    value = shard_sum(value, STEPS_ALONG[3:4], {"z2": sent})
    received, sent = hops(2, received, (value,), second)
    weights = held(weights, sent, (), NO_ROOM)
    both = (cotan, weights, partner(weights, "core", 1))
    half, mark = backward_input(core, x, 0, *both, sent)
    right, left = shard_sum(value, STEPS_ALONG[4:], {"z4": (mark,)}, "z4")
    received, sent = hops(3, received, (right,), third)
    arrived = neighbours(right, left)
    grad_in, mark = backward_input(core, x, 2, *both, sent, (half,))
    kept, given, _ = kernel_call(
        total_kernel,
        (received[1], received[0]),
        (f32(rows, columns), f32(rows, columns), MARK),
        core[None].astype(jnp.int32),
        (mark, *arrived),
    )
    new_weight, next_q = kernel_call(
        update_kernel,
        (weight_bf, kept, partner(given, "core", 1), basis.T, right, left, *arrived),
        (f32(rows, width), f32(2, width)),
        core[None].astype(jnp.int32),
        (mark,),
    )
    return (grad_in[None], new_weight[None], next_q.T[None])


def solution(mesh):
    fine = Mesh(mesh.devices.reshape(2, 4, 2, 8, 2), CYCLE + SHARD)
    tokens = P(CYCLE, SHARD, None)
    return jax.shard_map(
        on_device,
        mesh=fine,
        in_specs=(tokens, tokens, tokens, P()),
        out_specs=(tokens, tokens, P(CYCLE, None, None)),
        check_vma=False,
    )
```
